32 devices in a mesh: dp: 8 (over y, x, core), fsdp: 4 (over z).
Axes of the slice: x: 2, y: 2, z: 4, core: 2. Of those that a mesh axis runs over, the one named last changes fastest.
Arguments:
- tokens: bfloat16 [32, 512, 1024], P(('dp', 'fsdp')), may hold values from -6 to 6
- lengths: int32 [32], P(('dp', 'fsdp')), may hold values from 128 to 512, as said below
- span_starts: int32 [32, 5], P(('dp', 'fsdp')), may hold values from 0 to 502
- mask_embed: bfloat16 [1024], P('fsdp'), may hold values from -6 to 6
- norm_gains: bfloat16 [5, 1024], P(None, 'fsdp'), may hold values from 0.099609375 to 1.8984375
- ffn1_in: bfloat16 [1024, 4096], P('fsdp'), may hold values from -0.1875 to 0.1875
- ffn1_out: bfloat16 [4096, 1024], P('fsdp'), may hold values from -0.09375 to 0.09375
- attn_in: bfloat16 [1024, 3072], P('fsdp'), may hold values from -0.1875 to 0.1875
- attn_out: bfloat16 [1024, 1024], P('fsdp'), may hold values from -0.75 to 0.75
- conv_in: bfloat16 [1024, 2048], P('fsdp'), may hold values from -0.1875 to 0.1875
- conv_out: bfloat16 [1024, 1024], P('fsdp'), may hold values from -0.1875 to 0.1875
- depth: bfloat16 [5, 1024], P(None, 'fsdp'), may hold values from -2.5 to 2.5
- bn_affine: bfloat16 [2, 1024], P(None, 'fsdp'), may hold values from 0.5 to 1.5
- ffn2_in: bfloat16 [1024, 4096], P('fsdp'), may hold values from -0.1875 to 0.1875
- ffn2_out: bfloat16 [4096, 1024], P('fsdp'), may hold values from -0.09375 to 0.09375
- cotangent: bfloat16 [32, 512, 1024], P(('dp', 'fsdp')), may hold values from -6 to 6
Outputs:
- output: bfloat16 [32, 512, 1024], P(('dp', 'fsdp'))
- input_grad: bfloat16 [32, 512, 1024], P(('dp', 'fsdp'))
- mask_embed_grad: float32 [1024], P('fsdp')
- norm_gains_grad: float32 [5, 1024], P(None, 'fsdp')
- ffn1_in_grad: float32 [1024, 4096], P('fsdp')
- ffn1_out_grad: float32 [4096, 1024], P('fsdp')
- attn_in_grad: float32 [1024, 3072], P('fsdp')
- attn_out_grad: float32 [1024, 1024], P('fsdp')
- conv_in_grad: float32 [1024, 2048], P('fsdp')
- conv_out_grad: float32 [1024, 1024], P('fsdp')
- depth_grad: float32 [5, 1024], P(None, 'fsdp')
- bn_affine_grad: float32 [2, 1024], P(None, 'fsdp')
- ffn2_in_grad: float32 [1024, 4096], P('fsdp')
- ffn2_out_grad: float32 [4096, 1024], P('fsdp')
The draws below stay inside these ranges and needn't reach their ends.
Inputs may be any that keep to these rules, and one draw needn't show every extreme that they name: `lengths`: some utterance fills all 512 slots in every draw.
All inputs are finite; a program needn't handle non-finite values.
Results may differ from the reference program's by a relative error of at most 0.02.
Values may be sent and summed in bfloat16 or wider, within the bound.
A program may use at most 256 MiB of HBM per device.

```python
import jax
import jax.numpy as jnp
from jax import lax

D = 1024
FF = 4096
HEADS = 8
HEAD = 128
KER = 5
FRAMES = 512
SPAN_LEN = 10
SPANS = 5
UTT = 32


def draw_lengths(key, part):
    key = jax.random.fold_in(key, 7)
    first_key, second_key = jax.random.split(key)
    drawn = jax.random.randint(first_key, (UTT,), FRAMES // 4, FRAMES + 1)
    longest = jax.random.randint(second_key, (), 0, UTT)
    return jnp.where(jnp.arange(UTT) == longest, FRAMES, drawn).astype(jnp.int32)


def touch_ends(entries, rng, low, high):
    index_at = [jax.random.randint(jax.random.fold_in(rng, axis), (), 0, length) for axis, length in enumerate(entries.shape)]
    widest = entries.shape.index(max(entries.shape))
    neighbour = index_at[:widest] + [(index_at[widest] + 1) % entries.shape[widest]] + index_at[widest + 1:]
    return entries.at[tuple(index_at)].set(low).at[tuple(neighbour)].set(high)


def levels(rng, shape, cuts, low, high):
    def one(dim, parts):
        steps = jax.random.uniform(jax.random.fold_in(jax.random.fold_in(rng, 6), dim), (parts,), jnp.float32, low / len(cuts), high / len(cuts))
        return jnp.repeat(jnp.exp(steps), shape[dim] // parts).reshape((-1,) + (1,) * (len(shape) - dim - 1))

    gain = one(*cuts[0])
    for cut in cuts[1:]:
        gain = gain * one(*cut)
    return gain


def gaussian(rng, extent, scale, most, shards=(), kind=jnp.bfloat16):
    factor_of = levels(rng, extent, shards, -0.22, 0.18) if shards else 1.0
    array = jax.random.normal(rng, extent, jnp.float32) * scale * factor_of
    return jnp.minimum(jnp.maximum(array, -most), most).astype(kind)


def setup_inputs(seed: int = 0) -> dict:
    key_of = jax.random.split(jax.random.key(seed), 17)
    return {
        "tokens": gaussian(key_of[0], (UTT, FRAMES, D), 1.0, 6.0, ((0, 32),)),
        "lengths": draw_lengths(jax.random.fold_in(key_of[16], 71), 0),
        "span_starts": touch_ends(jax.random.randint(key_of[2], (UTT, SPANS), 0, FRAMES - SPAN_LEN + 1), jax.random.fold_in(key_of[2], 1), 0, FRAMES - SPAN_LEN).astype(jnp.int32),
        "mask_embed": gaussian(key_of[3], (D,), 1.0, 6.0, ((0, 4),)),
        "norm_gains": jnp.clip(1.0 + 0.18 * jax.random.normal(key_of[4], (5, D), jnp.float32), 0.099609375, 1.8984375).astype(jnp.bfloat16),
        "ffn1_in": gaussian(key_of[5], (D, FF), D ** -0.5, 0.1875, ((0, 4),)),
        "ffn1_out": gaussian(key_of[6], (FF, D), FF ** -0.5, 0.09375, ((0, 4),)),
        "attn_in": gaussian(key_of[7], (D, 3 * D), D ** -0.5, 0.1875, ((0, 4),)),
        "attn_out": gaussian(key_of[8], (D, D), (D // 16) ** -0.5, 0.75, ((0, 4),)),
        "conv_in": gaussian(key_of[9], (D, 2 * D), D ** -0.5, 0.1875, ((0, 4),)),
        "conv_out": gaussian(key_of[10], (D, D), D ** -0.5, 0.1875, ((0, 4),)),
        "depth": gaussian(key_of[11], (KER, D), KER ** -0.5, 2.5, ((1, 4),)),
        "bn_affine": jnp.clip(0.5 + 1.0 * jax.random.uniform(key_of[12], (2, D), jnp.float32) ** levels(key_of[12], (2, D), ((1, 4),), -0.2, 0.2), 0.5, 1.5).astype(jnp.bfloat16),
        "ffn2_in": gaussian(key_of[13], (D, FF), D ** -0.5, 0.1875, ((0, 4),)),
        "ffn2_out": gaussian(key_of[14], (FF, D), FF ** -0.5, 0.09375, ((0, 4),)),
        "cotangent": gaussian(key_of[15], (UTT, FRAMES, D), 1.0, 6.0, ((0, 32),)),
    }


EPSILON = 1e-05
NEGATIVE = -1000000000.0

@jax.custom_vjp
def low(v):
    return lax.optimization_barrier(v.astype(jnp.bfloat16)).astype(jnp.float32)

@jax.custom_vjp
def low_back(v):
    return v

def low_keep(v):
    return (low(v), None)

def low_pass(kept, grad):
    return (grad,)

def back_keep(v):
    return (v, None)

def back_low(kept, grad):
    return (low(grad),)
low.defvjp(low_keep, low_pass)
low_back.defvjp(back_keep, back_low)

def dense(inputs, weight):
    return jnp.einsum('ufd,de->ufe', inputs, weight, precision=lax.Precision.HIGHEST)

def layer_norm(inputs, layer_gain):
    average = lax.optimization_barrier(jnp.mean(inputs, axis=-1, keepdims=True))
    centered = inputs - average
    return centered * lax.rsqrt(lax.optimization_barrier(jnp.mean(centered * centered, axis=-1, keepdims=True)) + EPSILON) * layer_gain

def rotate(inputs):
    half_size = HEAD // 2
    position = jnp.arange(FRAMES, dtype=jnp.float32)
    frequency = 10000.0 ** (-jnp.arange(half_size, dtype=jnp.float32) / half_size)
    angles = position[:, None] * frequency[None, :]
    cosine = jnp.cos(angles)[:, None, :]
    sine = jnp.sin(angles)[:, None, :]
    front = inputs[..., :half_size]
    back_half = inputs[..., half_size:]
    return jnp.concatenate([front * cosine - back_half * sine, front * sine + back_half * cosine], axis=-1)

def frame_masks(lengths, span_starts):
    position = jnp.arange(FRAMES, dtype=jnp.int32)
    valid = position[None, :] < lengths[:, None]
    inside = (position[None, None, :] >= span_starts[:, :, None]) & (position[None, None, :] < span_starts[:, :, None] + SPAN_LEN)
    return (valid, jnp.any(inside, axis=1) & valid)

def feed(inputs, layer_gain, weight_in, weight_out):
    hidden = low(layer_norm(inputs, layer_gain))
    inner = low_back(dense(hidden, weight_in))
    return low_back(dense(low(jax.nn.silu(inner)), weight_out))

def attend_one(items):
    queries, keys_rot, values_low, key_live = items
    raw_scores = low_back(jnp.einsum('qhd,khd->hqk', queries, keys_rot, precision=lax.Precision.HIGHEST))
    scores = jnp.where(key_live[None, None, :], raw_scores * HEAD ** (-0.5), NEGATIVE)
    top_score = lax.optimization_barrier(jnp.max(scores, axis=-1, keepdims=True))
    expo = jnp.exp(scores - top_score)
    probs = low(expo / lax.optimization_barrier(jnp.sum(expo, axis=-1, keepdims=True)))
    return low_back(jnp.einsum('hqk,khd->qhd', probs, values_low, precision=lax.Precision.HIGHEST))

def attend(inputs, layer_gain, weight_in, weight_out, valid):
    hidden = low(layer_norm(inputs, layer_gain))
    joined = low_back(dense(hidden, weight_in))
    shape_heads = inputs.shape[:2] + (HEADS, HEAD)
    queries = low(rotate(joined[..., :D].reshape(shape_heads)))
    keys_rot = low(rotate(joined[..., D:2 * D].reshape(shape_heads)))
    values_low = low(joined[..., 2 * D:].reshape(shape_heads))
    heads_out = lax.map(jax.checkpoint(attend_one), (queries, keys_rot, values_low, valid))
    merged = low(heads_out.reshape(inputs.shape))
    return low_back(dense(merged, weight_out))

def convolve(inputs, layer_gain, weight_in, weight_out, kernel, affine, valid):
    hidden = low(layer_norm(inputs, layer_gain))
    proj = low_back(dense(hidden, weight_in))
    live = valid.astype(jnp.float32)[..., None]
    glu = proj[..., :D] * jax.nn.sigmoid(proj[..., D:]) * live
    side = KER // 2
    padded = jnp.pad(glu, ((0, 0), (side, side), (0, 0)))
    mixed = kernel[0] * padded[:, 0:FRAMES]
    for offset in range(1, KER):
        mixed = mixed + kernel[offset] * padded[:, offset:offset + FRAMES]
    count = jnp.sum(live)
    bmean = lax.optimization_barrier(jnp.sum(mixed * live, axis=(0, 1))) / count
    bvar = lax.optimization_barrier(jnp.sum((mixed - bmean) * (mixed - bmean) * live, axis=(0, 1))) / count
    normed = (mixed - bmean) * lax.rsqrt(bvar + EPSILON)
    active = low(jax.nn.silu(affine[0] * normed + affine[1]))
    return low_back(dense(active, weight_out))

def reference(tokens, lengths, span_starts, mask_embed, norm_gains, ffn1_in, ffn1_out, attn_in, attn_out, conv_in, conv_out, depth, bn_affine, ffn2_in, ffn2_out, cotangent):
    valid, masked = frame_masks(lengths, span_starts)

    def forward(frames_in, embed, gains, first_in, first_out, att_in, att_out, cv_in, cv_out, kernel, affine, second_in, second_out):
        start = jnp.where(masked[..., None], embed, frames_in)
        first = start + 0.5 * feed(start, gains[0], first_in, first_out)
        second = first + attend(first, gains[1], att_in, att_out, valid)
        third = second + convolve(second, gains[2], cv_in, cv_out, kernel, affine, valid)
        fourth = third + 0.5 * feed(third, gains[3], second_in, second_out)
        return layer_norm(fourth, gains[4])
    inputs = (tokens, mask_embed, norm_gains, ffn1_in, ffn1_out, attn_in, attn_out, conv_in, conv_out, depth, bn_affine, ffn2_in, ffn2_out)
    inputs = tuple((item.astype(jnp.float32) for item in inputs))
    result, pullback = jax.vjp(forward, *inputs)
    grads = pullback(cotangent.astype(jnp.float32))
    return (result.astype(jnp.bfloat16), grads[0].astype(jnp.bfloat16), grads[1], grads[2], grads[3], grads[4], grads[5], grads[6], grads[7], grads[8], grads[9], grads[10], grads[11], grads[12])
```

```python
import functools

import jax
import jax.numpy as jnp
from jax import lax
from jax.experimental import pallas as pl
from jax.experimental.pallas import tpu as pltpu
from jax.sharding import PartitionSpec as P

HEAD = 128
KER = 5
SPAN_LEN = 10


EPSILON = 1e-05
NEGATIVE = -1000000000.0


def product(left_side, right_side):
    return jnp.dot(left_side, right_side, preferred_element_type=jnp.float32)


def product_tn(left_side, right_side):
    return lax.dot_general(
        left_side, right_side, (((0,), (0,)), ((), ())), preferred_element_type=jnp.float32
    )


def product_nt(left_side, right_side):
    return lax.dot_general(
        left_side, right_side, (((1,), (1,)), ((), ())), preferred_element_type=jnp.float32
    )


def layer_norm(inputs, layer_gain):
    average = jnp.mean(inputs, axis=-1, keepdims=True)
    centered = inputs - average
    inverse = lax.rsqrt(jnp.mean(centered * centered, axis=-1, keepdims=True) + EPSILON)
    normed = centered * inverse
    return (normed * layer_gain, normed, inverse)


def norm_back(upstream, layer_gain, normed, inverse):
    scaled = upstream * layer_gain
    first_mean = jnp.mean(scaled, axis=-1, keepdims=True)
    second_mean = jnp.mean(scaled * normed, axis=-1, keepdims=True)
    return (
        inverse * (scaled - first_mean - normed * second_mean),
        jnp.sum(upstream * normed, axis=0),
    )


def swish_slope(inputs):
    sigmoid_part = jax.nn.sigmoid(inputs)
    return sigmoid_part * (1.0 + inputs * (1.0 - sigmoid_part))


def rotation(frame_count):
    half_size = HEAD // 2
    position = jnp.arange(frame_count, dtype=jnp.float32)
    frequency = 10000.0 ** (-jnp.arange(half_size, dtype=jnp.float32) / half_size)
    angles = position[:, None] * frequency[None, :]
    return (jnp.cos(angles)[:, None, :], jnp.sin(angles)[:, None, :])


def rotate(inputs, cosine, sine):
    half_size = HEAD // 2
    front = inputs[..., :half_size]
    back_half = inputs[..., half_size:]
    return jnp.concatenate(
        [front * cosine - back_half * sine, front * sine + back_half * cosine], axis=-1
    )


def unrotate(inputs, cosine, sine):
    half_size = HEAD // 2
    front = inputs[..., :half_size]
    back_half = inputs[..., half_size:]
    return jnp.concatenate(
        [front * cosine + back_half * sine, back_half * cosine - front * sine], axis=-1
    )


MESH = pl.DeviceIdType.MESH
WAYS = 8


def coordinates():
    dp = lax.axis_index("dp")
    z = lax.axis_index("fsdp")
    core_bit = lax.rem(dp, 2)
    x_bit = lax.rem(dp // 2, 2)
    y_bit = lax.rem(dp // 4, 2)
    return dp, z, core_bit, x_bit, y_bit


def signal(sem, device):
    pl.semaphore_signal(sem, inc=1, device_id=device, device_id_type=MESH)


def greet(depth, dp, z, flat_peers):
    barrier = pltpu.get_barrier_semaphore()
    signal(barrier, (dp, lax.rem(z + 1, depth)))
    signal(barrier, (dp, lax.rem(z + depth - 1, depth)))
    for peer in flat_peers:
        signal(barrier, (peer, z))
    pl.semaphore_wait(barrier, 2 + len(flat_peers))


def gather_kernel(depth, count, chunks, lead, *refs):
    shards, small = refs[:count], refs[count]
    fulls, small_full = refs[count + 1 : 2 * count + 1], refs[2 * count + 1]
    send_sems, recv_sems, own_sems, small_sems = refs[2 * count + 2 :]
    dp, z, core_bit, x_bit, y_bit = coordinates()
    mine = lax.rem(dp, WAYS)
    step_c, step_x, step_y = 1 - 2 * core_bit, 2 - 4 * x_bit, 4 - 8 * y_bit
    peer_c, peer_x, peer_y = dp + step_c, dp + step_x, dp + step_y
    greet(depth, dp, z, (peer_c, peer_x, peer_y))

    def remote(source, target, send_sem, recv_sem, device):
        return pltpu.make_async_remote_copy(
            source, target, send_sem, recv_sem, device_id=device, device_id_type=MESH
        )

    def slot(chunk, owner, piece, half):
        index, first, width = chunks[chunk]
        rows = shards[index].shape[0]
        part = rows // WAYS
        if half is not None:
            width = width // 2
            first = first + half * width
        start = pl.multiple_of(owner * rows + piece * part, part)
        return fulls[index].at[pl.ds(start, part), pl.ds(first, width)]

    def place(chunk, index, message, owner, piece, device, half=None):
        where = slot(chunk, owner, piece, half)
        return remote(
            where,
            where,
            send_sems.at[chunk, index, message],
            recv_sems.at[chunk, index, message],
            device,
        )

    def each(action):
        for hop in range(depth - 1):

            @pl.when(z - 1 - hop >= 0)
            def _():
                action(2 * hop, z - 1 - hop, hop, 1)

            @pl.when(z + 1 + hop < depth)
            def _():
                action(2 * hop + 1, z + 1 + hop, hop, -1)

    here = (dp, z)
    core_dev, x_dev, y_dev = (peer_c, z), (peer_x, z), (peer_y, z)
    piece_x, piece_y, piece_xy = mine + step_x, mine + step_y, mine + step_x + step_y
    other = mine + step_c
    other_x, other_y, other_xy = other + step_x, other + step_y, other + step_x + step_y

    small_local = pltpu.make_async_copy(small, small_full.at[z], own_sems.at[count, 0])
    small_local.start()

    def small_out(index, source, owner, device):
        return remote(
            source, small_full.at[owner], small_sems.at[index, 0], small_sems.at[index, 1], device
        )

    @pl.when(z + 1 < depth)
    def _():
        small_out(0, small, z, (dp, z + 1)).start()

    @pl.when(z > 0)
    def _():
        small_out(1, small, z, (dp, z - 1)).start()

    def line_start(chunk):
        index, first, width = chunks[chunk]
        part = shards[index].shape[0] // WAYS
        source = shards[index].at[
            pl.ds(pl.multiple_of(mine * part, part), part), pl.ds(first, width)
        ]
        target = slot(chunk, z, mine, None)

        @pl.when(z + 1 < depth)
        def _():
            remote(
                source, target, send_sems.at[chunk, 0, 0], recv_sems.at[chunk, 0, 0], (dp, z + 1)
            ).start()

        @pl.when(z > 0)
        def _():
            remote(
                source, target, send_sems.at[chunk, 1, 0], recv_sems.at[chunk, 1, 0], (dp, z - 1)
            ).start()

    def line_arrived(chunk):
        def action(index, owner, hop, way):
            place(chunk, index, 0, owner, mine, here).wait_recv()
            if hop < depth - 2:
                following = z + way

                @pl.when((following >= 0) & (following < depth))
                def _():
                    place(chunk, index + 2, 0, owner, mine, (dp, following)).start()

            place(chunk, index, 1, owner, mine, x_dev).start()
            place(chunk, index, 2, owner, mine, y_dev).start()
            place(chunk, index, 5, owner, mine, core_dev).start()

        each(action)

    def plane_arrived(chunk):
        def action(index, owner, hop, way):
            place(chunk, index, 1, owner, piece_x, here).wait_recv()
            place(chunk, index, 3, owner, piece_x, y_dev, 0).start()
            place(chunk, index, 6, owner, piece_x, core_dev).start()
            place(chunk, index, 2, owner, piece_y, here).wait_recv()
            place(chunk, index, 4, owner, piece_y, x_dev, 1).start()
            place(chunk, index, 7, owner, piece_y, core_dev).start()

        each(action)

    def corner_arrived(chunk):
        def action(index, owner, hop, way):
            for half in range(2):
                place(chunk, index, 3 + half, owner, piece_xy, here, half).wait_recv()
                place(chunk, index, 8 + half, owner, piece_xy, core_dev, half).start()

        each(action)

    def core_arrived(chunk):
        def action(index, owner, hop, way):
            place(chunk, index, 5, owner, other, here).wait_recv()
            place(chunk, index, 6, owner, other_x, here).wait_recv()
            place(chunk, index, 7, owner, other_y, here).wait_recv()
            for half in range(2):
                place(chunk, index, 8 + half, owner, other_xy, here, half).wait_recv()

        each(action)

    def small_action(index, owner, hop, way):
        small_out(index, small, owner, here).wait_recv()
        if hop < depth - 2:
            following = z + way

            @pl.when((following >= 0) & (following < depth))
            def _():
                small_out(index + 2, small_full.at[owner], owner, (dp, following)).start()

    total = len(chunks)
    for chunk in range(min(lead, total)):
        line_start(chunk)
    own_copies = []
    for index in range(count):
        rows = shards[index].shape[0]
        target = fulls[index].at[pl.ds(pl.multiple_of(z * rows, rows), rows)]
        copy = remote(
            shards[index], target, own_sems.at[index, 0], own_sems.at[index, 1], core_dev
        )
        copy.start()
        own_copies.append(copy)
    for turn in range(total + 3):
        if turn + lead < total:
            line_start(turn + lead)
        if turn < total:
            line_arrived(turn)
        if turn == 0:
            each(small_action)
        if 0 <= turn - 1 < total:
            plane_arrived(turn - 1)
        if 0 <= turn - 2 < total:
            corner_arrived(turn - 2)
        if 0 <= turn - 3 < total:
            core_arrived(turn - 3)
    for copy in own_copies:
        copy.wait()
    small_local.wait()

    @pl.when(z + 1 < depth)
    def _():
        small_out(0, small, z, here).wait_send()

    @pl.when(z > 0)
    def _():
        small_out(1, small, z, here).wait_send()

    def small_drain(index, owner, hop, way):
        if hop < depth - 2:
            following = z + way

            @pl.when((following >= 0) & (following < depth))
            def _():
                small_out(index + 2, small, owner, here).wait_send()

    each(small_drain)
    for chunk in range(total):

        @pl.when(z + 1 < depth)
        def _():
            place(chunk, 0, 0, z, mine, here).wait_send()

        @pl.when(z > 0)
        def _():
            place(chunk, 1, 0, z, mine, here).wait_send()

        def drain(index, owner, hop, way):
            if hop < depth - 2:
                following = z + way

                @pl.when((following >= 0) & (following < depth))
                def _():
                    place(chunk, index + 2, 0, owner, mine, here).wait_send()

            for message in (1, 2, 5, 6, 7):
                place(chunk, index, message, owner, mine, here).wait_send()
            for message in (3, 4, 8, 9):
                place(chunk, index, message, owner, mine, here, 0).wait_send()

        each(drain)


def gather_all(depth, weights, small):
    count = len(weights)
    chunks = [(index, 0, weight.shape[1]) for index, weight in enumerate(weights)]
    shape = (len(chunks), 2 * (depth - 1), 10)
    outs = [
        jax.ShapeDtypeStruct((weight.shape[0] * depth, weight.shape[1]), weight.dtype)
        for weight in weights
    ]
    outs.append(jax.ShapeDtypeStruct((depth,) + small.shape, small.dtype))
    return pl.pallas_call(
        functools.partial(gather_kernel, depth, count, chunks, 2),
        out_shape=outs,
        in_specs=[pl.BlockSpec(memory_space=pl.ANY)] * (count + 1),
        out_specs=[pl.BlockSpec(memory_space=pl.ANY)] * (count + 1),
        scratch_shapes=[
            pltpu.SemaphoreType.DMA(shape),
            pltpu.SemaphoreType.DMA(shape),
            pltpu.SemaphoreType.DMA((count + 1, 2)),
            pltpu.SemaphoreType.DMA((2 * (depth - 1), 2)),
        ],
        compiler_params=pltpu.CompilerParams(collective_id=0, has_side_effects=True),
    )(*weights, small)


def reduce_grads(grad_in, grad_out, small_grad):
    shards = (
        lax.psum_scatter(
            grad_in.astype(jnp.bfloat16), "fsdp", scatter_dimension=0, tiled=True
        ).astype(jnp.float32),
        lax.psum_scatter(
            grad_out.astype(jnp.bfloat16), "fsdp", scatter_dimension=0, tiled=True
        ).astype(jnp.float32),
        lax.psum_scatter(
            small_grad.astype(jnp.bfloat16), "fsdp", scatter_dimension=1, tiled=True
        ).astype(jnp.float32),
    )
    return (
        lax.psum(shards[0].astype(jnp.bfloat16), "dp").astype(jnp.float32),
        lax.psum(shards[1].astype(jnp.bfloat16), "dp").astype(jnp.float32),
        lax.psum(shards[2].astype(jnp.bfloat16), "dp").astype(jnp.float32),
    )


def ffn_forward(inputs, layer_gain, weight_in, weight_out):
    out_norm, normed, inverse = layer_norm(inputs, layer_gain)
    hidden = out_norm.astype(jnp.bfloat16)
    inner = product(hidden, weight_in)
    active = jax.nn.silu(inner).astype(jnp.bfloat16)
    return (product(active, weight_out), (hidden, normed, inverse, inner, active))


def ffn_backward(upstream, stored, layer_gain, weight_in, weight_out):
    hidden, normed, inverse, inner, active = stored
    branch_grad = (0.5 * upstream).astype(jnp.bfloat16)
    grad_out = product_tn(active, branch_grad)
    active_grad = product_nt(branch_grad, weight_out)
    inner_grad = (active_grad * swish_slope(inner)).astype(jnp.bfloat16)
    grad_in = product_tn(hidden, inner_grad)
    norm_grad, gain_grad = norm_back(product_nt(inner_grad, weight_in), layer_gain, normed, inverse)
    return (upstream + norm_grad, grad_in, grad_out, gain_grad)


def attention_scores(queries, keys_rot, key_live):
    raw_scores = jnp.einsum(
        "uqhd,ukhd->uhqk", queries, keys_rot, preferred_element_type=jnp.float32
    )
    return jnp.where(key_live[:, None, None, :], raw_scores * HEAD ** (-0.5), NEGATIVE)


def attention_forward(inputs, layer_gain, weight_in, weight_out, key_live, tables, units):
    row_count, model_width = inputs.shape
    shape_heads = (units, row_count // units, model_width // HEAD, HEAD)
    out_norm, normed, inverse = layer_norm(inputs, layer_gain)
    hidden = out_norm.astype(jnp.bfloat16)
    joined = product(hidden, weight_in)
    queries = rotate(joined[:, :model_width].reshape(shape_heads), tables[0], tables[1]).astype(
        jnp.bfloat16
    )
    keys_rot = rotate(
        joined[:, model_width : 2 * model_width].reshape(shape_heads), tables[0], tables[1]
    ).astype(jnp.bfloat16)
    values_low = joined[:, 2 * model_width :].reshape(shape_heads).astype(jnp.bfloat16)
    scores = attention_scores(queries, keys_rot, key_live)
    top_score = jnp.max(scores, axis=-1, keepdims=True)
    log_total = top_score + jnp.log(jnp.sum(jnp.exp(scores - top_score), axis=-1, keepdims=True))
    probs_low = jnp.exp(scores - log_total).astype(jnp.bfloat16)
    heads_out = jnp.einsum(
        "uhqk,ukhd->uqhd", probs_low, values_low, preferred_element_type=jnp.float32
    )
    merged = heads_out.reshape(row_count, model_width).astype(jnp.bfloat16)
    return (
        product(merged, weight_out),
        (hidden, normed, inverse, queries, keys_rot, values_low, log_total, merged),
    )


def attention_backward(upstream, stored, layer_gain, weight_in, weight_out, key_live, tables):
    hidden, normed, inverse, queries, keys_rot, values_low, log_total, merged = stored
    row_count, model_width = upstream.shape
    branch_grad = upstream.astype(jnp.bfloat16)
    grad_out = product_tn(merged, branch_grad)
    merged_grad = product_nt(branch_grad, weight_out).astype(jnp.bfloat16).reshape(queries.shape)
    probs = jnp.exp(attention_scores(queries, keys_rot, key_live) - log_total)
    prob_grad = jnp.einsum(
        "uqhd,ukhd->uhqk", merged_grad, values_low, preferred_element_type=jnp.float32
    )
    value_grad = jnp.einsum(
        "uhqk,uqhd->ukhd",
        probs.astype(jnp.bfloat16),
        merged_grad,
        preferred_element_type=jnp.float32,
    )
    row_term = jnp.sum(probs * prob_grad, axis=-1, keepdims=True)
    score_grad = (probs * (prob_grad - row_term) * HEAD ** (-0.5)).astype(jnp.bfloat16)
    query_grad = unrotate(
        jnp.einsum("uhqk,ukhd->uqhd", score_grad, keys_rot, preferred_element_type=jnp.float32),
        tables[0],
        tables[1],
    )
    key_grad = unrotate(
        jnp.einsum("uhqk,uqhd->ukhd", score_grad, queries, preferred_element_type=jnp.float32),
        tables[0],
        tables[1],
    )
    joined_grad = jnp.concatenate(
        [
            query_grad.reshape(row_count, model_width),
            key_grad.reshape(row_count, model_width),
            value_grad.reshape(row_count, model_width),
        ],
        axis=1,
    ).astype(jnp.bfloat16)
    grad_in = product_tn(hidden, joined_grad)
    norm_grad, gain_grad = norm_back(
        product_nt(joined_grad, weight_in), layer_gain, normed, inverse
    )
    return (upstream + norm_grad, grad_in, grad_out, gain_grad)


def conv_forward(inputs, layer_gain, weight_in, weight_out, small_low, live, units):
    row_count, model_width = inputs.shape
    frame_count = row_count // units
    out_norm, normed, inverse = layer_norm(inputs, layer_gain)
    hidden = out_norm.astype(jnp.bfloat16)
    proj = product(hidden, weight_in)
    linear_part = proj[:, :model_width]
    gate_part = jax.nn.sigmoid(proj[:, model_width:])
    glu = (linear_part * gate_part * live).reshape(units, frame_count, model_width)
    side = KER // 2
    padded = jnp.pad(glu, ((0, 0), (side, side), (0, 0)))
    kernel = small_low[1 : KER + 1].astype(jnp.float32)
    mixed = kernel[0] * padded[:, 0:frame_count]
    for offset in range(1, KER):
        mixed = mixed + kernel[offset] * padded[:, offset : offset + frame_count]
    mixed = mixed.reshape(row_count, model_width)
    local_sum = jnp.sum(mixed * live, axis=0)
    local_count = jnp.sum(live)
    total_sum, count = lax.psum((local_sum, local_count), ("dp", "fsdp"))
    bmean = total_sum / count
    deviation = mixed - bmean
    bvar = lax.psum(jnp.sum(deviation * deviation * live, axis=0), ("dp", "fsdp")) / count
    bn_inverse = lax.rsqrt(bvar + EPSILON)
    bn_normed = (mixed - bmean) * bn_inverse
    pre_act = small_low[KER + 1].astype(jnp.float32) * bn_normed + small_low[KER + 2].astype(
        jnp.float32
    )
    active = jax.nn.silu(pre_act).astype(jnp.bfloat16)
    stored = (
        hidden,
        normed,
        inverse,
        linear_part,
        gate_part,
        padded,
        bn_normed,
        bn_inverse,
        count,
        pre_act,
        active,
    )
    return (product(active, weight_out), stored)


def conv_backward(upstream, stored, layer_gain, weight_in, weight_out, small_low, live, units):
    (
        hidden,
        normed,
        inverse,
        linear_part,
        gate_part,
        padded,
        bn_normed,
        bn_inverse,
        count,
        pre_act,
        active,
    ) = stored
    row_count, model_width = upstream.shape
    frame_count = row_count // units
    kernel = small_low[1 : KER + 1].astype(jnp.float32)
    bn_scale = small_low[KER + 1].astype(jnp.float32)
    branch_grad = upstream.astype(jnp.bfloat16)
    grad_out = product_tn(active, branch_grad)
    pre_grad = product_nt(branch_grad, weight_out) * swish_slope(pre_act)
    shift_total, scale_total = lax.psum(
        (jnp.sum(pre_grad, axis=0), jnp.sum(pre_grad * bn_normed, axis=0)), ("dp", "fsdp")
    )
    mixed_grad = bn_inverse * (
        bn_scale * pre_grad
        - live * (bn_scale * shift_total) / count
        - live * bn_normed * (bn_scale * scale_total) / count
    )
    side = KER // 2
    grid_grad = mixed_grad.reshape(units, frame_count, model_width)
    grad_padded = jnp.pad(grid_grad, ((0, 0), (side, side), (0, 0)))
    last_tap = KER - 1
    glu_grad = kernel[0] * grad_padded[:, last_tap : last_tap + frame_count]
    for offset in range(1, KER):
        glu_grad = (
            glu_grad
            + kernel[offset] * grad_padded[:, last_tap - offset : last_tap - offset + frame_count]
        )
    kernel_grad = jnp.stack(
        [
            jnp.sum(padded[:, offset : offset + frame_count] * grid_grad, axis=(0, 1))
            for offset in range(KER)
        ]
    )
    glu_grad = glu_grad.reshape(row_count, model_width) * live
    proj_grad = jnp.concatenate(
        [glu_grad * gate_part, glu_grad * linear_part * gate_part * (1.0 - gate_part)], axis=1
    ).astype(jnp.bfloat16)
    grad_in = product_tn(hidden, proj_grad)
    norm_grad, gain_grad = norm_back(product_nt(proj_grad, weight_in), layer_gain, normed, inverse)
    return (
        upstream + norm_grad,
        grad_in,
        grad_out,
        gain_grad,
        kernel_grad,
        jnp.stack([scale_total, shift_total]),
    )


def local(
    depth_devices,
    tokens,
    lengths,
    span_starts,
    mask_embed,
    norm_gains,
    ffn1_in,
    ffn1_out,
    attn_in,
    attn_out,
    conv_in,
    conv_out,
    depth,
    bn_affine,
    ffn2_in,
    ffn2_out,
    cotangent,
):
    units, frame_count, model_width = tokens.shape
    row_count = units * frame_count
    position = jnp.arange(frame_count, dtype=jnp.int32)
    valid = position[None, :] < lengths[:, None]
    inside = (position[None, None, :] >= span_starts[:, :, None]) & (
        position[None, None, :] < span_starts[:, :, None] + SPAN_LEN
    )
    masked = jnp.any(inside, axis=1) & valid
    live = valid.reshape(row_count, 1).astype(jnp.float32)
    masked_col = masked.reshape(row_count, 1)
    tables = rotation(frame_count)
    small = jnp.concatenate([norm_gains, mask_embed[None, :], depth, bn_affine], axis=0)
    small = jnp.pad(small, ((0, 16 - small.shape[0]), (0, 0)))
    gathered = gather_all(
        depth_devices,
        [ffn1_in, ffn1_out, attn_in, attn_out, conv_in, conv_out, ffn2_in, ffn2_out],
        small,
    )
    small_all = gathered[8].transpose(1, 0, 2).reshape(16, model_width)
    third_small = jnp.concatenate([small_all[2:3], small_all[6:13]], axis=0)
    first_weights = (gathered[0], gathered[1], small_all[jnp.array([0, 5])])
    second_weights = (gathered[2], gathered[3], small_all[1:2])
    third_weights = (gathered[4], gathered[5], third_small)
    fourth_weights = (gathered[6], gathered[7], small_all[3:5])
    first_back, second_back, third_back, fourth_back = (
        first_weights,
        second_weights,
        third_weights,
        fourth_weights,
    )
    gain_one = first_weights[2][0].astype(jnp.float32)
    embed = first_weights[2][1].astype(jnp.float32)
    start = jnp.where(masked_col, embed, tokens.reshape(row_count, model_width).astype(jnp.float32))
    branch, first_stored = ffn_forward(start, gain_one, first_weights[0], first_weights[1])
    first = start + 0.5 * branch
    gain_two = second_weights[2][0].astype(jnp.float32)
    branch, second_stored = attention_forward(
        first, gain_two, second_weights[0], second_weights[1], valid, tables, units
    )
    second = first + branch
    gain_three = third_weights[2][0].astype(jnp.float32)
    branch, third_stored = conv_forward(
        second, gain_three, third_weights[0], third_weights[1], third_weights[2], live, units
    )
    third = second + branch
    gain_four = fourth_weights[2][0].astype(jnp.float32)
    gain_five = fourth_weights[2][1].astype(jnp.float32)
    branch, fourth_stored = ffn_forward(third, gain_four, fourth_weights[0], fourth_weights[1])
    fourth = third + 0.5 * branch
    out_norm, final_normed, final_inverse = layer_norm(fourth, gain_five)
    output = out_norm.astype(jnp.bfloat16).reshape(units, frame_count, model_width)
    upstream = cotangent.reshape(row_count, model_width).astype(jnp.float32)
    grad_four, gain_five_grad = norm_back(upstream, gain_five, final_normed, final_inverse)
    grad_three, grad_in, grad_out, gain_four_grad = ffn_backward(
        grad_four, fourth_stored, gain_four, fourth_back[0], fourth_back[1]
    )
    fourth_red = reduce_grads(grad_in, grad_out, jnp.stack([gain_four_grad, gain_five_grad]))
    grad_two, grad_in, grad_out, gain_three_grad, kernel_grad, affine_full = conv_backward(
        grad_three,
        third_stored,
        gain_three,
        third_back[0],
        third_back[1],
        third_weights[2],
        live,
        units,
    )
    third_red = reduce_grads(
        grad_in, grad_out, jnp.concatenate([gain_three_grad[None, :], kernel_grad], axis=0)
    )
    grad_one, grad_in, grad_out, gain_two_grad = attention_backward(
        grad_two, second_stored, gain_two, second_back[0], second_back[1], valid, tables
    )
    second_red = reduce_grads(grad_in, grad_out, gain_two_grad[None, :])
    grad_zero, grad_in, grad_out, gain_one_grad = ffn_backward(
        grad_one, first_stored, gain_one, first_back[0], first_back[1]
    )
    masked_float = masked_col.astype(jnp.float32)
    embed_grad = jnp.sum(grad_zero * masked_float, axis=0)
    input_grad = (
        (grad_zero * (1.0 - masked_float))
        .astype(jnp.bfloat16)
        .reshape(units, frame_count, model_width)
    )
    first_red = reduce_grads(grad_in, grad_out, jnp.stack([gain_one_grad, embed_grad]))
    column_width = norm_gains.shape[1]
    affine_grad = lax.dynamic_slice_in_dim(
        affine_full, lax.axis_index("fsdp") * column_width, column_width, 1
    )
    gains_grad = jnp.concatenate(
        [first_red[2][0:1], second_red[2], third_red[2][0:1], fourth_red[2]], axis=0
    )
    return (
        output,
        input_grad,
        first_red[2][1],
        gains_grad,
        first_red[0],
        first_red[1],
        second_red[0],
        second_red[1],
        third_red[0],
        third_red[1],
        third_red[2][1:],
        affine_grad,
        fourth_red[0],
        fourth_red[1],
    )


def solution(mesh):
    in_specs = (
        P(("dp", "fsdp"), None, None),
        P(("dp", "fsdp")),
        P(("dp", "fsdp"), None),
        P("fsdp"),
        P(None, "fsdp"),
        P("fsdp", None),
        P("fsdp", None),
        P("fsdp", None),
        P("fsdp", None),
        P("fsdp", None),
        P("fsdp", None),
        P(None, "fsdp"),
        P(None, "fsdp"),
        P("fsdp", None),
        P("fsdp", None),
        P(("dp", "fsdp"), None, None),
    )
    out_specs = (
        P(("dp", "fsdp"), None, None),
        P(("dp", "fsdp"), None, None),
        P("fsdp"),
        P(None, "fsdp"),
        P("fsdp", None),
        P("fsdp", None),
        P("fsdp", None),
        P("fsdp", None),
        P("fsdp", None),
        P("fsdp", None),
        P(None, "fsdp"),
        P(None, "fsdp"),
        P("fsdp", None),
        P("fsdp", None),
    )
    return jax.shard_map(functools.partial(local, mesh.shape["fsdp"]), mesh=mesh, in_specs=in_specs, out_specs=out_specs, check_vma=False)
```

```python
import functools

import jax
import jax.numpy as jnp
from jax import lax
from jax.experimental import pallas as pl
from jax.experimental.pallas import tpu as pltpu
from jax.sharding import PartitionSpec as P

HEAD = 128
KER = 5
SPAN_LEN = 10


EPSILON = 1e-05
NEGATIVE = -1000000000.0


def product(left_side, right_side):
    return jnp.dot(left_side, right_side, preferred_element_type=jnp.float32)


def product_nt(left_side, right_side):
    return lax.dot_general(
        left_side, right_side, (((1,), (1,)), ((), ())), preferred_element_type=jnp.float32
    )


def layer_norm(inputs, layer_gain):
    average = jnp.mean(inputs, axis=-1, keepdims=True)
    centered = inputs - average
    inverse = lax.rsqrt(jnp.mean(centered * centered, axis=-1, keepdims=True) + EPSILON)
    normed = centered * inverse
    return (normed * layer_gain, normed, inverse)


def norm_back(upstream, layer_gain, normed, inverse):
    scaled = upstream * layer_gain
    first_mean = jnp.mean(scaled, axis=-1, keepdims=True)
    second_mean = jnp.mean(scaled * normed, axis=-1, keepdims=True)
    return (
        inverse * (scaled - first_mean - normed * second_mean),
        jnp.sum(upstream * normed, axis=0),
    )


def swish_slope(inputs):
    sigmoid_part = jax.nn.sigmoid(inputs)
    return sigmoid_part * (1.0 + inputs * (1.0 - sigmoid_part))


def rotation(frame_count):
    half_size = HEAD // 2
    position = jnp.arange(frame_count, dtype=jnp.float32)
    frequency = 10000.0 ** (-jnp.arange(half_size, dtype=jnp.float32) / half_size)
    angles = position[:, None] * frequency[None, :]
    return (jnp.cos(angles)[:, None, :], jnp.sin(angles)[:, None, :])


def rotate(inputs, cosine, sine):
    half_size = HEAD // 2
    front = inputs[..., :half_size]
    back_half = inputs[..., half_size:]
    return jnp.concatenate(
        [front * cosine - back_half * sine, front * sine + back_half * cosine], axis=-1
    )


def unrotate(inputs, cosine, sine):
    half_size = HEAD // 2
    front = inputs[..., :half_size]
    back_half = inputs[..., half_size:]
    return jnp.concatenate(
        [front * cosine + back_half * sine, back_half * cosine - front * sine], axis=-1
    )


MESH = pl.DeviceIdType.MESH
WAYS = 8


def coordinates():
    dp = lax.axis_index("dp")
    z = lax.axis_index("fsdp")
    core_bit = lax.rem(dp, 2)
    x_bit = lax.rem(dp // 2, 2)
    y_bit = lax.rem(dp // 4, 2)
    return dp, z, core_bit, x_bit, y_bit


def signal(sem, device):
    pl.semaphore_signal(sem, inc=1, device_id=device, device_id_type=MESH)


def greet(depth, dp, z, flat_peers):
    barrier = pltpu.get_barrier_semaphore()
    signal(barrier, (dp, lax.rem(z + 1, depth)))
    signal(barrier, (dp, lax.rem(z + depth - 1, depth)))
    for peer in flat_peers:
        signal(barrier, (peer, z))
    pl.semaphore_wait(barrier, 2 + len(flat_peers))


def gather_kernel(depth, count, chunks, lead, *refs):
    shards, small = refs[:count], refs[count]
    fulls, small_full = refs[count + 1 : 2 * count + 1], refs[2 * count + 1]
    send_sems, recv_sems, own_sems, small_sems = refs[2 * count + 2 :]
    dp, z, core_bit, x_bit, y_bit = coordinates()
    mine = lax.rem(dp, WAYS)
    step_c, step_x, step_y = 1 - 2 * core_bit, 2 - 4 * x_bit, 4 - 8 * y_bit
    peer_c, peer_x, peer_y = dp + step_c, dp + step_x, dp + step_y
    greet(depth, dp, z, (peer_c, peer_x, peer_y))

    def remote(source, target, send_sem, recv_sem, device):
        return pltpu.make_async_remote_copy(
            source, target, send_sem, recv_sem, device_id=device, device_id_type=MESH
        )

    def slot(chunk, owner, piece, half):
        index, first, width = chunks[chunk]
        rows = shards[index].shape[0]
        part = rows // WAYS
        if half is not None:
            width = width // 2
            first = first + half * width
        start = pl.multiple_of(owner * rows + piece * part, part)
        return fulls[index].at[pl.ds(start, part), pl.ds(first, width)]

    def place(chunk, index, message, owner, piece, device, half=None):
        where = slot(chunk, owner, piece, half)
        return remote(
            where,
            where,
            send_sems.at[chunk, index, message],
            recv_sems.at[chunk, index, message],
            device,
        )

    def each(action):
        for hop in range(depth - 1):

            @pl.when(z - 1 - hop >= 0)
            def _():
                action(2 * hop, z - 1 - hop, hop, 1)

            @pl.when(z + 1 + hop < depth)
            def _():
                action(2 * hop + 1, z + 1 + hop, hop, -1)

    here = (dp, z)
    core_dev, x_dev, y_dev = (peer_c, z), (peer_x, z), (peer_y, z)
    piece_x, piece_y, piece_xy = mine + step_x, mine + step_y, mine + step_x + step_y
    other = mine + step_c
    other_x, other_y, other_xy = other + step_x, other + step_y, other + step_x + step_y

    small_local = pltpu.make_async_copy(small, small_full.at[z], own_sems.at[count, 0])
    small_local.start()

    def small_out(index, source, owner, device):
        return remote(
            source, small_full.at[owner], small_sems.at[index, 0], small_sems.at[index, 1], device
        )

    @pl.when(z + 1 < depth)
    def _():
        small_out(0, small, z, (dp, z + 1)).start()

    @pl.when(z > 0)
    def _():
        small_out(1, small, z, (dp, z - 1)).start()

    def line_start(chunk):
        index, first, width = chunks[chunk]
        part = shards[index].shape[0] // WAYS
        source = shards[index].at[
            pl.ds(pl.multiple_of(mine * part, part), part), pl.ds(first, width)
        ]
        target = slot(chunk, z, mine, None)

        @pl.when(z + 1 < depth)
        def _():
            remote(
                source, target, send_sems.at[chunk, 0, 0], recv_sems.at[chunk, 0, 0], (dp, z + 1)
            ).start()

        @pl.when(z > 0)
        def _():
            remote(
                source, target, send_sems.at[chunk, 1, 0], recv_sems.at[chunk, 1, 0], (dp, z - 1)
            ).start()

    def line_arrived(chunk):
        def action(index, owner, hop, way):
            place(chunk, index, 0, owner, mine, here).wait_recv()
            if hop < depth - 2:
                following = z + way

                @pl.when((following >= 0) & (following < depth))
                def _():
                    place(chunk, index + 2, 0, owner, mine, (dp, following)).start()

            place(chunk, index, 1, owner, mine, x_dev).start()
            place(chunk, index, 2, owner, mine, y_dev).start()
            place(chunk, index, 5, owner, mine, core_dev).start()

        each(action)

    def plane_arrived(chunk):
        def action(index, owner, hop, way):
            place(chunk, index, 1, owner, piece_x, here).wait_recv()
            place(chunk, index, 3, owner, piece_x, y_dev, 0).start()
            place(chunk, index, 6, owner, piece_x, core_dev).start()
            place(chunk, index, 2, owner, piece_y, here).wait_recv()
            place(chunk, index, 4, owner, piece_y, x_dev, 1).start()
            place(chunk, index, 7, owner, piece_y, core_dev).start()

        each(action)

    def corner_arrived(chunk):
        def action(index, owner, hop, way):
            for half in range(2):
                place(chunk, index, 3 + half, owner, piece_xy, here, half).wait_recv()
                place(chunk, index, 8 + half, owner, piece_xy, core_dev, half).start()

        each(action)

    def core_arrived(chunk):
        def action(index, owner, hop, way):
            place(chunk, index, 5, owner, other, here).wait_recv()
            place(chunk, index, 6, owner, other_x, here).wait_recv()
            place(chunk, index, 7, owner, other_y, here).wait_recv()
            for half in range(2):
                place(chunk, index, 8 + half, owner, other_xy, here, half).wait_recv()

        each(action)

    def small_action(index, owner, hop, way):
        small_out(index, small, owner, here).wait_recv()
        if hop < depth - 2:
            following = z + way

            @pl.when((following >= 0) & (following < depth))
            def _():
                small_out(index + 2, small_full.at[owner], owner, (dp, following)).start()

    total = len(chunks)
    for chunk in range(min(lead, total)):
        line_start(chunk)
    own_copies = []
    for index in range(count):
        rows = shards[index].shape[0]
        target = fulls[index].at[pl.ds(pl.multiple_of(z * rows, rows), rows)]
        copy = remote(
            shards[index], target, own_sems.at[index, 0], own_sems.at[index, 1], core_dev
        )
        copy.start()
        own_copies.append(copy)
    for turn in range(total + 3):
        if turn + lead < total:
            line_start(turn + lead)
        if turn < total:
            line_arrived(turn)
        if turn == 0:
            each(small_action)
        if 0 <= turn - 1 < total:
            plane_arrived(turn - 1)
        if 0 <= turn - 2 < total:
            corner_arrived(turn - 2)
        if 0 <= turn - 3 < total:
            core_arrived(turn - 3)
    for copy in own_copies:
        copy.wait()
    small_local.wait()

    @pl.when(z + 1 < depth)
    def _():
        small_out(0, small, z, here).wait_send()

    @pl.when(z > 0)
    def _():
        small_out(1, small, z, here).wait_send()

    def small_drain(index, owner, hop, way):
        if hop < depth - 2:
            following = z + way

            @pl.when((following >= 0) & (following < depth))
            def _():
                small_out(index + 2, small, owner, here).wait_send()

    each(small_drain)
    for chunk in range(total):

        @pl.when(z + 1 < depth)
        def _():
            place(chunk, 0, 0, z, mine, here).wait_send()

        @pl.when(z > 0)
        def _():
            place(chunk, 1, 0, z, mine, here).wait_send()

        def drain(index, owner, hop, way):
            if hop < depth - 2:
                following = z + way

                @pl.when((following >= 0) & (following < depth))
                def _():
                    place(chunk, index + 2, 0, owner, mine, here).wait_send()

            for message in (1, 2, 5, 6, 7):
                place(chunk, index, message, owner, mine, here).wait_send()
            for message in (3, 4, 8, 9):
                place(chunk, index, message, owner, mine, here, 0).wait_send()

        each(drain)


def gather_all(depth, weights, small):
    count = len(weights)
    chunks = [(index, 0, weight.shape[1]) for index, weight in enumerate(weights)]
    shape = (len(chunks), 2 * (depth - 1), 10)
    outs = [
        jax.ShapeDtypeStruct((weight.shape[0] * depth, weight.shape[1]), weight.dtype)
        for weight in weights
    ]
    outs.append(jax.ShapeDtypeStruct((depth,) + small.shape, small.dtype))
    return pl.pallas_call(
        functools.partial(gather_kernel, depth, count, chunks, 2),
        out_shape=outs,
        in_specs=[pl.BlockSpec(memory_space=pl.ANY)] * (count + 1),
        out_specs=[pl.BlockSpec(memory_space=pl.ANY)] * (count + 1),
        scratch_shapes=[
            pltpu.SemaphoreType.DMA(shape),
            pltpu.SemaphoreType.DMA(shape),
            pltpu.SemaphoreType.DMA((count + 1, 2)),
            pltpu.SemaphoreType.DMA((2 * (depth - 1), 2)),
        ],
        compiler_params=pltpu.CompilerParams(collective_id=0, has_side_effects=True),
    )(*weights, small)


def add_pair(left, right):
    return left + right


def join_moments(left, right):
    count = left[0:1] + right[0:1]
    mean = (left[0:1] * left[1:2] + right[0:1] * right[1:2]) / count
    gap = right[1:2] - left[1:2]
    spread = left[2:3] + right[2:3] + gap * gap * (left[0:1] * right[0:1] / count)
    return jnp.concatenate([count, mean, spread, left[3:]], axis=0)


def exchange_kernel(depth, groups, combine, value, result, work, inbox, line, send_sems, recv_sems):
    dp, z, core_bit, x_bit, y_bit = coordinates()
    peers = [dp + 1 - 2 * core_bit, dp + 2 - 4 * x_bit, dp + 4 - 8 * y_bit]
    group = dp // WAYS
    barrier = pltpu.get_barrier_semaphore()
    far = [lax.rem(group + step, groups) * WAYS + lax.rem(dp, WAYS) for step in range(1, groups)]
    for peer in peers + far:
        signal(barrier, (peer, z))
    for step in range(1, depth):
        signal(barrier, (dp, lax.rem(z + step, depth)))
    pl.semaphore_wait(barrier, len(peers) + len(far) + depth - 1)
    work[0] = value[...]
    for turn, peer in enumerate(peers):
        copy = pltpu.make_async_remote_copy(
            work.at[turn],
            inbox.at[turn],
            send_sems.at[turn],
            recv_sems.at[turn],
            device_id=(peer, z),
            device_id_type=MESH,
        )
        copy.start()
        copy.wait()
        work[turn + 1] = combine(work[turn], inbox[turn])

    def spread(source, slots, first, targets, own):
        copies = []
        for step, target in enumerate(targets):
            copy = pltpu.make_async_remote_copy(
                source,
                slots.at[own],
                send_sems.at[first + step],
                recv_sems.at[first + step],
                device_id=target,
                device_id_type=MESH,
            )
            copy.start()
            copies.append(copy)
        local = pltpu.make_async_copy(source, slots.at[own], send_sems.at[first + len(targets)])
        local.start()
        for copy in copies:
            copy.wait()
        local.wait()

    last = len(peers)
    if groups > 1:
        spread(work.at[last], inbox.at[pl.ds(last, groups)], last, [(peer, z) for peer in far], group)
        total = inbox[last]
        for step in range(1, groups):
            total = combine(total, inbox[last + step])
        work[last] = total
    first = last + groups
    spread(
        work.at[last],
        line,
        first,
        [(dp, lax.rem(z + step, depth)) for step in range(1, depth)],
        z,
    )
    total = line[0]
    for step in range(1, depth):
        total = combine(total, line[step])
    result[...] = total


def exchange(depth, groups, combine, value, collective):
    shape = value.shape
    sems = 3 + groups + depth
    return pl.pallas_call(
        functools.partial(exchange_kernel, depth, groups, combine),
        out_shape=jax.ShapeDtypeStruct(shape, value.dtype),
        in_specs=[pl.BlockSpec(memory_space=pltpu.VMEM)],
        out_specs=pl.BlockSpec(memory_space=pltpu.VMEM),
        scratch_shapes=[
            pltpu.VMEM((4,) + shape, value.dtype),
            pltpu.VMEM((3 + groups,) + shape, value.dtype),
            pltpu.VMEM((depth,) + shape, value.dtype),
            pltpu.SemaphoreType.DMA((sems,)),
            pltpu.SemaphoreType.DMA((sems,)),
        ],
        compiler_params=pltpu.CompilerParams(collective_id=collective, has_side_effects=True),
    )(value)


LANES = 128
HELD = 4


def reduce_kernel(depth, groups, count, chunks, *refs):
    lefts, rights, small = refs[0 : 2 * count : 2], refs[1 : 2 * count : 2], refs[2 * count]
    at = 2 * count + 1
    outs, small_out = refs[at : at + count], refs[at + count]
    at += count + 1
    left_peers, right_peers = refs[at : at + count], refs[at + count : at + 2 * count]
    at += 2 * count
    (
        left_buf,
        right_buf,
        held,
        first_in,
        second_in,
        line_in,
        far_in,
        final,
        small_work,
        small_in,
        small_line,
        pair_send,
        pair_recv,
        load_sems,
        send_sems,
        recv_sems,
        store_sems,
        small_send,
        small_recv,
    ) = refs[at:]
    dp, z, core_bit, x_bit, y_bit = coordinates()
    group = dp // WAYS
    peer_c, peer_x, peer_y = (
        dp + 1 - 2 * core_bit,
        dp + 2 - 4 * x_bit,
        dp + 4 - 8 * y_bit,
    )
    far = [lax.rem(group + step, groups) * WAYS + lax.rem(dp, WAYS) for step in range(1, groups)]
    barrier = pltpu.get_barrier_semaphore()
    for peer in [peer_c, peer_x, peer_y] + far:
        signal(barrier, (peer, z))
    for step in range(1, depth):
        signal(barrier, (dp, lax.rem(z + step, depth)))
    pl.semaphore_wait(barrier, 3 + len(far) + depth - 1)
    tokens = lefts[0].shape[0]
    block = left_buf.shape[2] // depth
    here = (dp, z)

    def remote(source, target, send_sem, recv_sem, device):
        return pltpu.make_async_remote_copy(
            source, target, send_sem, recv_sem, device_id=device, device_id_type=MESH
        )

    pair_copies = []
    for index in range(count):
        half = rights[index].shape[1] // 2
        columns = pl.ds(pl.multiple_of((1 - core_bit) * half, half), half)
        pair_copies.append(
            (
                remote(
                    lefts[index],
                    left_peers[index],
                    pair_send.at[index, 0],
                    pair_recv.at[index, 0],
                    (peer_c, z),
                ),
                remote(
                    rights[index].at[:, columns],
                    right_peers[index],
                    pair_send.at[index, 1],
                    pair_recv.at[index, 1],
                    (peer_c, z),
                ),
            )
        )
        for copy in pair_copies[index]:
            copy.start()

    def loads(chunk):
        index, row, part, left_slot, right_slot, new_left, new_right = chunks[chunk]
        rows = lefts[index].shape[1] // depth
        half = rights[index].shape[1] // 2
        piece = half // 4
        copies = []
        if new_left:
            for side, source in enumerate((lefts[index], left_peers[index])):
                for owner in range(depth):
                    copies.append(
                        pltpu.make_async_copy(
                            source.at[:, pl.ds(owner * rows + row, block)],
                            left_buf.at[
                                left_slot, pl.ds(side * tokens, tokens), pl.ds(owner * block, block)
                            ],
                            load_sems.at[left_slot, side * depth + owner],
                        )
                    )
        if new_right:
            for quarter in range(4):
                start = quarter * piece + part * LANES
                own_start = pl.multiple_of(core_bit * half + start, LANES)
                target = pl.ds(quarter * LANES, LANES)
                copies.append(
                    pltpu.make_async_copy(
                        rights[index].at[:, pl.ds(own_start, LANES)],
                        right_buf.at[right_slot, pl.ds(0, tokens), target],
                        load_sems.at[2 + right_slot, quarter],
                    )
                )
                copies.append(
                    pltpu.make_async_copy(
                        right_peers[index].at[:, pl.ds(start, LANES)],
                        right_buf.at[right_slot, pl.ds(tokens, tokens), target],
                        load_sems.at[2 + right_slot, 4 + quarter],
                    )
                )
        return copies

    arrived = set()

    def load_start(chunk):
        index = chunks[chunk][0]
        if index not in arrived:
            arrived.add(index)
            for copy in pair_copies[index]:
                copy.wait_recv()
        for copy in loads(chunk):
            copy.start()

    def axes(chunk):
        if chunk % 2 == 0:
            return peer_x, peer_y, x_bit, y_bit
        return peer_y, peer_x, y_bit, x_bit

    def quarter_of(chunk, first_bit, second_bit):
        if chunk % 2 == 0:
            return 2 * first_bit + second_bit
        return 2 * second_bit + first_bit

    def first_copy(chunk, which, device):
        _, _, first_bit, _ = axes(chunk)
        return remote(
            held.at[chunk % HELD, quarter_of(chunk, 1 - first_bit, which)],
            first_in.at[chunk, which],
            send_sems.at[chunk, which],
            recv_sems.at[chunk, which],
            device,
        )

    def second_copy(chunk, device):
        _, _, _, second_bit = axes(chunk)
        return remote(
            first_in.at[chunk, 1 - second_bit],
            second_in.at[chunk],
            send_sems.at[chunk, 2],
            recv_sems.at[chunk, 2],
            device,
        )

    def line_copy(chunk, step, device):
        return remote(
            second_in.at[chunk, lax.rem(z + step, depth)],
            line_in.at[chunk, step - 1],
            send_sems.at[chunk, 2 + step],
            recv_sems.at[chunk, 2 + step],
            device,
        )

    def multiply(chunk):
        index, row, part, left_slot, right_slot, new_left, new_right = chunks[chunk]
        for copy in loads(chunk):
            copy.wait()
        if chunk + 1 < len(chunks):
            load_start(chunk + 1)
        if chunk >= HELD:
            for which in range(2):
                first_copy(chunk - HELD, which, here).wait_send()

        def body(owner):
            columns = pl.ds(pl.multiple_of(owner * block, block), block)
            product = lax.dot_general(
                left_buf[left_slot, :, columns],
                right_buf[right_slot],
                (((0,), (0,)), ((), ())),
                preferred_element_type=jnp.float32,
            ).astype(jnp.bfloat16)
            for quarter in range(4):
                held[chunk % HELD, quarter, owner] = product[
                    :, quarter * LANES : (quarter + 1) * LANES
                ]

        pl.loop(0, depth)(body)
        first_peer, _, _, _ = axes(chunk)
        for which in range(2):
            first_copy(chunk, which, (first_peer, z)).start()

    def add_first(chunk):
        _, second_peer, first_bit, second_bit = axes(chunk)
        for which in range(2):
            first_copy(chunk, which, here).wait_recv()

        def add(which):
            first_in[chunk, which] = (
                first_in[chunk, which].astype(jnp.float32)
                + held[chunk % HELD, quarter_of(chunk, first_bit, which)].astype(jnp.float32)
            ).astype(jnp.bfloat16)

        add(1 - second_bit)
        second_copy(chunk, (second_peer, z)).start()
        add(second_bit)

    def add_second(chunk):
        _, _, _, second_bit = axes(chunk)
        second_copy(chunk, here).wait_recv()
        second_in[chunk] = (
            second_in[chunk].astype(jnp.float32) + first_in[chunk, second_bit].astype(jnp.float32)
        ).astype(jnp.bfloat16)
        for step in range(1, depth):
            line_copy(chunk, step, (dp, lax.rem(z + step, depth))).start()

    base = 2 + depth

    def where(chunk, core, x_at, y_at, half=None):
        index, row, part = chunks[chunk][:3]
        width = outs[index].shape[1]
        start = core * (width // 2) + (2 * x_at + y_at) * (width // 8) + part * LANES
        size = block
        if half is not None:
            size = block // 2
            row = row + half * size
        return outs[index].at[pl.ds(row, size), pl.ds(pl.multiple_of(start, LANES), LANES)]

    def from_final(chunk, message, device):
        return remote(
            final.at[chunk],
            where(chunk, core_bit, x_bit, y_bit),
            send_sems.at[chunk, base + message],
            recv_sems.at[chunk, base + message],
            device,
        )

    def passed(chunk, message, core, x_at, y_at, device, half=None):
        place = where(chunk, core, x_at, y_at, half)
        return remote(
            place,
            place,
            send_sems.at[chunk, base + message],
            recv_sems.at[chunk, base + message],
            device,
        )

    def store(chunk):
        return pltpu.make_async_copy(
            final.at[chunk], where(chunk, core_bit, x_bit, y_bit), store_sems.at[chunk]
        )

    def far_copy(chunk, step, device):
        return remote(
            far_in.at[chunk, groups],
            far_in.at[chunk, group],
            send_sems.at[chunk, base + 9 + step],
            recv_sems.at[chunk, base + 9 + step],
            device,
        )

    def finish(chunk):
        for step in range(1, depth):
            line_copy(chunk, step, here).wait_recv()
        total = second_in[chunk, z].astype(jnp.float32)
        for step in range(1, depth):
            total = total + line_in[chunk, step - 1].astype(jnp.float32)
        if groups > 1:
            own = total.astype(jnp.bfloat16)
            far_in[chunk, groups] = own
            far_in[chunk, group] = own
            for step, peer in enumerate(far):
                far_copy(chunk, step, (peer, z)).start()
            for step in range(len(far)):
                far_copy(chunk, step, here).wait()
            total = far_in[chunk, 0].astype(jnp.float32)
            for step in range(1, groups):
                total = total + far_in[chunk, step].astype(jnp.float32)
        final[chunk] = total.astype(jnp.bfloat16)
        for message, peer in enumerate((peer_x, peer_y, peer_c)):
            from_final(chunk, message, (peer, z)).start()
        store(chunk).start()

    def plane_arrived(chunk):
        passed(chunk, 0, core_bit, 1 - x_bit, y_bit, here).wait_recv()
        passed(chunk, 3, core_bit, 1 - x_bit, y_bit, (peer_y, z), 0).start()
        passed(chunk, 5, core_bit, 1 - x_bit, y_bit, (peer_c, z)).start()
        passed(chunk, 1, core_bit, x_bit, 1 - y_bit, here).wait_recv()
        passed(chunk, 4, core_bit, x_bit, 1 - y_bit, (peer_x, z), 1).start()
        passed(chunk, 6, core_bit, x_bit, 1 - y_bit, (peer_c, z)).start()

    def corner_arrived(chunk):
        for half in range(2):
            passed(chunk, 3 + half, core_bit, 1 - x_bit, 1 - y_bit, here, half).wait_recv()
            passed(chunk, 7 + half, core_bit, 1 - x_bit, 1 - y_bit, (peer_c, z), half).start()

    def core_arrived(chunk):
        other = 1 - core_bit
        passed(chunk, 2, other, x_bit, y_bit, here).wait_recv()
        passed(chunk, 5, other, 1 - x_bit, y_bit, here).wait_recv()
        passed(chunk, 6, other, x_bit, 1 - y_bit, here).wait_recv()
        for half in range(2):
            passed(chunk, 7 + half, other, 1 - x_bit, 1 - y_bit, here, half).wait_recv()

    def small_copy(turn, device):
        return remote(
            small_work.at[turn],
            small_in.at[turn],
            small_send.at[turn],
            small_recv.at[turn],
            device,
        )

    def small_far_copy(step, device):
        return remote(
            small_work.at[3],
            small_in.at[3 + group],
            small_send.at[3 + step],
            small_recv.at[3 + step],
            device,
        )

    slice_width = small_out.shape[1]

    def small_line_copy(step, device):
        columns = pl.ds(
            pl.multiple_of(lax.rem(z + step, depth) * slice_width, slice_width), slice_width
        )
        return remote(
            small_work.at[4, :, columns],
            small_line.at[step - 1],
            small_send.at[2 + groups + step],
            small_recv.at[2 + groups + step],
            device,
        )

    small_peers = (peer_c, peer_x, peer_y)

    def small_turn(turn):
        if turn == 0:
            small_work[0] = small[...]
        if 1 <= turn <= 3:
            small_copy(turn - 1, here).wait_recv()
            small_work[turn] = small_work[turn - 1] + small_in[turn - 1]
        if turn < 3:
            small_copy(turn, (small_peers[turn], z)).start()
        if turn == 3:
            if groups > 1:
                small_in[3 + group] = small_work[3]
                for step, peer in enumerate(far):
                    small_far_copy(step, (peer, z)).start()
                for step in range(len(far)):
                    small_far_copy(step, here).wait()
                total = small_in[3]
                for step in range(1, groups):
                    total = total + small_in[3 + step]
                small_work[4] = total
            else:
                small_work[4] = small_work[3]
            for step in range(1, depth):
                small_line_copy(step, (dp, lax.rem(z + step, depth))).start()
        if turn == 4:
            columns = pl.ds(pl.multiple_of(z * slice_width, slice_width), slice_width)
            total = small_work[4, :, columns]
            for step in range(1, depth):
                small_line_copy(step, here).wait_recv()
                total = total + small_line[step - 1]
            small_out[...] = total

    total_chunks = len(chunks)
    load_start(0)
    for turn in range(total_chunks + 9):
        if turn < 5:
            small_turn(turn)
        if turn < total_chunks:
            multiply(turn)
        for lag, action in (
            (2, add_first),
            (4, add_second),
            (5, finish),
            (6, plane_arrived),
            (7, corner_arrived),
            (8, core_arrived),
        ):
            if 0 <= turn - lag < total_chunks:
                action(turn - lag)
    for index in range(count):
        for copy in pair_copies[index]:
            copy.wait_send()
    for turn in range(3):
        small_copy(turn, here).wait_send()
    for step in range(1, depth):
        small_line_copy(step, here).wait_send()
    for chunk in range(total_chunks):
        if chunk >= total_chunks - HELD:
            for which in range(2):
                first_copy(chunk, which, here).wait_send()
        second_copy(chunk, here).wait_send()
        for step in range(1, depth):
            line_copy(chunk, step, here).wait_send()
        for message in range(3):
            from_final(chunk, message, here).wait_send()
        for message in (5, 6):
            passed(chunk, message, core_bit, x_bit, y_bit, here).wait_send()
        for message in (3, 4, 7, 8):
            passed(chunk, message, core_bit, x_bit, y_bit, here, 0).wait_send()
        store(chunk).wait()


def reduce_chunks(depth, pairs, block):
    chunks = []
    left_slot, right_slot = 1, 1
    last_left, last_right = None, None
    for index, (left, right) in enumerate(pairs):
        rows = left.shape[1] // depth
        for row in range(0, rows, block):
            for part in range(right.shape[1] // (WAYS * LANES)):
                new_left = last_left != (index, row)
                new_right = last_right != (index, part)
                if new_left:
                    left_slot = 1 - left_slot
                if new_right:
                    right_slot = 1 - right_slot
                last_left, last_right = (index, row), (index, part)
                chunks.append((index, row, part, left_slot, right_slot, new_left, new_right))
    return chunks


def reduce_all(depth, groups, pairs, small, collective):
    count = len(pairs)
    tokens = pairs[0][0].shape[0]
    block = small.shape[1] // depth
    chunks = reduce_chunks(depth, pairs, block)
    total = len(chunks)
    outs, left_peers, right_peers = [], [], []
    for left, right in pairs:
        outs.append(
            jax.ShapeDtypeStruct((left.shape[1] // depth, right.shape[1]), jnp.bfloat16)
        )
        left_peers.append(jax.ShapeDtypeStruct(left.shape, jnp.bfloat16))
        right_peers.append(jax.ShapeDtypeStruct((tokens, right.shape[1] // 2), jnp.bfloat16))
    outs.append(jax.ShapeDtypeStruct((small.shape[0], block), jnp.float32))
    low = jnp.bfloat16
    messages = 2 + depth + 9 + groups
    any_spec = pl.BlockSpec(memory_space=pl.ANY)
    vmem_spec = pl.BlockSpec(memory_space=pltpu.VMEM)
    operands = [array for pair in pairs for array in pair]
    results = pl.pallas_call(
        functools.partial(reduce_kernel, depth, groups, count, chunks),
        out_shape=outs + left_peers + right_peers,
        in_specs=[any_spec] * (2 * count) + [vmem_spec],
        out_specs=[any_spec] * count + [vmem_spec] + [any_spec] * (2 * count),
        scratch_shapes=[
            pltpu.VMEM((2, 2 * tokens, depth * block), low),
            pltpu.VMEM((2, 2 * tokens, 4 * LANES), low),
            pltpu.VMEM((HELD, 4, depth, block, LANES), low),
            pltpu.VMEM((total, 2, depth, block, LANES), low),
            pltpu.VMEM((total, depth, block, LANES), low),
            pltpu.VMEM((total, depth - 1, block, LANES), low),
            pltpu.VMEM((total, groups + 1, block, LANES) if groups > 1 else (1, 1, 16, LANES), low),
            pltpu.VMEM((total, block, LANES), low),
            pltpu.VMEM((5,) + small.shape, jnp.float32),
            pltpu.VMEM((3 + groups,) + small.shape, jnp.float32),
            pltpu.VMEM((depth - 1, small.shape[0], block), jnp.float32),
            pltpu.SemaphoreType.DMA((count, 2)),
            pltpu.SemaphoreType.DMA((count, 2)),
            pltpu.SemaphoreType.DMA((4, max(2 * depth, 8))),
            pltpu.SemaphoreType.DMA((total, messages)),
            pltpu.SemaphoreType.DMA((total, messages)),
            pltpu.SemaphoreType.DMA((total,)),
            pltpu.SemaphoreType.DMA((3 + groups + depth,)),
            pltpu.SemaphoreType.DMA((3 + groups + depth,)),
        ],
        compiler_params=pltpu.CompilerParams(
            collective_id=collective, has_side_effects=True, vmem_limit_bytes=58 * 1024 * 1024
        ),
    )(*operands, small)
    return results[:count], results[count]


def ffn_forward(inputs, layer_gain, weight_in, weight_out):
    out_norm, normed, inverse = layer_norm(inputs, layer_gain)
    hidden = out_norm.astype(jnp.bfloat16)
    inner = product(hidden, weight_in)
    active = jax.nn.silu(inner).astype(jnp.bfloat16)
    return (product(active, weight_out), (hidden, normed, inverse, inner, active))


def ffn_backward(upstream, stored, layer_gain, weight_in, weight_out):
    hidden, normed, inverse, inner, active = stored
    branch_grad = (0.5 * upstream).astype(jnp.bfloat16)
    active_grad = product_nt(branch_grad, weight_out)
    inner_grad = (active_grad * swish_slope(inner)).astype(jnp.bfloat16)
    norm_grad, gain_grad = norm_back(product_nt(inner_grad, weight_in), layer_gain, normed, inverse)
    return (upstream + norm_grad, [(hidden, inner_grad), (active, branch_grad)], gain_grad)


def attention_scores(queries, keys_rot, key_live):
    raw_scores = jnp.einsum(
        "uqhd,ukhd->uhqk", queries, keys_rot, preferred_element_type=jnp.float32
    )
    return jnp.where(key_live[:, None, None, :], raw_scores * HEAD ** (-0.5), NEGATIVE)


def attention_forward(inputs, layer_gain, weight_in, weight_out, key_live, tables, units):
    row_count, model_width = inputs.shape
    shape_heads = (units, row_count // units, model_width // HEAD, HEAD)
    out_norm, normed, inverse = layer_norm(inputs, layer_gain)
    hidden = out_norm.astype(jnp.bfloat16)
    joined = product(hidden, weight_in)
    queries = rotate(joined[:, :model_width].reshape(shape_heads), tables[0], tables[1]).astype(
        jnp.bfloat16
    )
    keys_rot = rotate(
        joined[:, model_width : 2 * model_width].reshape(shape_heads), tables[0], tables[1]
    ).astype(jnp.bfloat16)
    values_low = joined[:, 2 * model_width :].reshape(shape_heads).astype(jnp.bfloat16)
    scores = attention_scores(queries, keys_rot, key_live)
    top_score = jnp.max(scores, axis=-1, keepdims=True)
    log_total = top_score + jnp.log(jnp.sum(jnp.exp(scores - top_score), axis=-1, keepdims=True))
    probs_low = jnp.exp(scores - log_total).astype(jnp.bfloat16)
    heads_out = jnp.einsum(
        "uhqk,ukhd->uqhd", probs_low, values_low, preferred_element_type=jnp.float32
    )
    merged = heads_out.reshape(row_count, model_width).astype(jnp.bfloat16)
    return (
        product(merged, weight_out),
        (hidden, normed, inverse, queries, keys_rot, values_low, log_total, merged),
    )


def attention_backward(upstream, stored, layer_gain, weight_in, weight_out, key_live, tables):
    hidden, normed, inverse, queries, keys_rot, values_low, log_total, merged = stored
    row_count, model_width = upstream.shape
    branch_grad = upstream.astype(jnp.bfloat16)
    merged_grad = product_nt(branch_grad, weight_out).astype(jnp.bfloat16).reshape(queries.shape)
    probs = jnp.exp(attention_scores(queries, keys_rot, key_live) - log_total)
    prob_grad = jnp.einsum(
        "uqhd,ukhd->uhqk", merged_grad, values_low, preferred_element_type=jnp.float32
    )
    value_grad = jnp.einsum(
        "uhqk,uqhd->ukhd",
        probs.astype(jnp.bfloat16),
        merged_grad,
        preferred_element_type=jnp.float32,
    )
    row_term = jnp.sum(probs * prob_grad, axis=-1, keepdims=True)
    score_grad = (probs * (prob_grad - row_term) * HEAD ** (-0.5)).astype(jnp.bfloat16)
    query_grad = unrotate(
        jnp.einsum("uhqk,ukhd->uqhd", score_grad, keys_rot, preferred_element_type=jnp.float32),
        tables[0],
        tables[1],
    )
    key_grad = unrotate(
        jnp.einsum("uhqk,uqhd->ukhd", score_grad, queries, preferred_element_type=jnp.float32),
        tables[0],
        tables[1],
    )
    joined_grad = jnp.concatenate(
        [
            query_grad.reshape(row_count, model_width),
            key_grad.reshape(row_count, model_width),
            value_grad.reshape(row_count, model_width),
        ],
        axis=1,
    ).astype(jnp.bfloat16)
    norm_grad, gain_grad = norm_back(
        product_nt(joined_grad, weight_in), layer_gain, normed, inverse
    )
    return (upstream + norm_grad, [(hidden, joined_grad), (merged, branch_grad)], gain_grad)


def conv_forward(inputs, layer_gain, weight_in, weight_out, small_low, live, units, share):
    row_count, model_width = inputs.shape
    frame_count = row_count // units
    out_norm, normed, inverse = layer_norm(inputs, layer_gain)
    hidden = out_norm.astype(jnp.bfloat16)
    proj = product(hidden, weight_in)
    linear_part = proj[:, :model_width]
    gate_part = jax.nn.sigmoid(proj[:, model_width:])
    glu = (linear_part * gate_part * live).reshape(units, frame_count, model_width)
    side = KER // 2
    padded = jnp.pad(glu, ((0, 0), (side, side), (0, 0)))
    kernel = small_low[1 : KER + 1].astype(jnp.float32)
    mixed = kernel[0] * padded[:, 0:frame_count]
    for offset in range(1, KER):
        mixed = mixed + kernel[offset] * padded[:, offset : offset + frame_count]
    mixed = mixed.reshape(row_count, model_width)
    local_count = jnp.sum(live)
    local_mean = jnp.sum(mixed * live, axis=0) / local_count
    local_spread = jnp.sum(jnp.square(mixed - local_mean) * live, axis=0)
    moments = jnp.stack([jnp.full((model_width,), local_count), local_mean, local_spread])
    moments = share(join_moments, jnp.pad(moments, ((0, 5), (0, 0))), 1)
    count, bmean = moments[0, 0], moments[1]
    bvar = moments[2] / count
    bn_inverse = lax.rsqrt(bvar + EPSILON)
    bn_normed = (mixed - bmean) * bn_inverse
    pre_act = small_low[KER + 1].astype(jnp.float32) * bn_normed + small_low[KER + 2].astype(
        jnp.float32
    )
    active = jax.nn.silu(pre_act).astype(jnp.bfloat16)
    stored = (
        hidden,
        normed,
        inverse,
        linear_part,
        gate_part,
        padded,
        bn_normed,
        bn_inverse,
        count,
        pre_act,
        active,
    )
    return (product(active, weight_out), stored)


def conv_backward(upstream, stored, layer_gain, weight_in, weight_out, small_low, live, units, share):
    (
        hidden,
        normed,
        inverse,
        linear_part,
        gate_part,
        padded,
        bn_normed,
        bn_inverse,
        count,
        pre_act,
        active,
    ) = stored
    row_count, model_width = upstream.shape
    frame_count = row_count // units
    kernel = small_low[1 : KER + 1].astype(jnp.float32)
    bn_scale = small_low[KER + 1].astype(jnp.float32)
    branch_grad = upstream.astype(jnp.bfloat16)
    pre_grad = product_nt(branch_grad, weight_out) * swish_slope(pre_act)
    sums = jnp.stack([jnp.sum(pre_grad, axis=0), jnp.sum(pre_grad * bn_normed, axis=0)])
    sums = share(add_pair, jnp.pad(sums, ((0, 6), (0, 0))), 2)
    shift_total, scale_total = sums[0], sums[1]
    mixed_grad = bn_inverse * (
        bn_scale * pre_grad
        - live * (bn_scale * shift_total) / count
        - live * bn_normed * (bn_scale * scale_total) / count
    )
    side = KER // 2
    grid_grad = mixed_grad.reshape(units, frame_count, model_width)
    grad_padded = jnp.pad(grid_grad, ((0, 0), (side, side), (0, 0)))
    last_tap = KER - 1
    glu_grad = kernel[0] * grad_padded[:, last_tap : last_tap + frame_count]
    for offset in range(1, KER):
        glu_grad = (
            glu_grad
            + kernel[offset] * grad_padded[:, last_tap - offset : last_tap - offset + frame_count]
        )
    kernel_grad = jnp.stack(
        [
            jnp.sum(padded[:, offset : offset + frame_count] * grid_grad, axis=(0, 1))
            for offset in range(KER)
        ]
    )
    glu_grad = glu_grad.reshape(row_count, model_width) * live
    proj_grad = jnp.concatenate(
        [glu_grad * gate_part, glu_grad * linear_part * gate_part * (1.0 - gate_part)], axis=1
    ).astype(jnp.bfloat16)
    norm_grad, gain_grad = norm_back(product_nt(proj_grad, weight_in), layer_gain, normed, inverse)
    return (
        upstream + norm_grad,
        [(hidden, proj_grad), (active, branch_grad)],
        gain_grad,
        kernel_grad,
        jnp.stack([scale_total, shift_total]),
    )


def local(
    depth_devices,
    groups,
    tokens,
    lengths,
    span_starts,
    mask_embed,
    norm_gains,
    ffn1_in,
    ffn1_out,
    attn_in,
    attn_out,
    conv_in,
    conv_out,
    depth,
    bn_affine,
    ffn2_in,
    ffn2_out,
    cotangent,
):
    units, frame_count, model_width = tokens.shape
    row_count = units * frame_count
    position = jnp.arange(frame_count, dtype=jnp.int32)
    valid = position[None, :] < lengths[:, None]
    inside = (position[None, None, :] >= span_starts[:, :, None]) & (
        position[None, None, :] < span_starts[:, :, None] + SPAN_LEN
    )
    masked = jnp.any(inside, axis=1) & valid
    live = valid.reshape(row_count, 1).astype(jnp.float32)
    masked_col = masked.reshape(row_count, 1)
    tables = rotation(frame_count)
    small = jnp.concatenate([norm_gains, mask_embed[None, :], depth, bn_affine], axis=0)
    small = jnp.pad(small, ((0, 16 - small.shape[0]), (0, 0)))
    gathered = gather_all(
        depth_devices,
        [ffn1_in, ffn1_out, attn_in, attn_out, conv_in, conv_out, ffn2_in, ffn2_out],
        small,
    )
    small_all = gathered[8].transpose(1, 0, 2).reshape(16, model_width)
    third_small = jnp.concatenate([small_all[2:3], small_all[6:13]], axis=0)
    first_weights = (gathered[0], gathered[1], small_all[jnp.array([0, 5])])
    second_weights = (gathered[2], gathered[3], small_all[1:2])
    third_weights = (gathered[4], gathered[5], third_small)
    fourth_weights = (gathered[6], gathered[7], small_all[3:5])
    gain_one = first_weights[2][0].astype(jnp.float32)
    embed = first_weights[2][1].astype(jnp.float32)
    start = jnp.where(masked_col, embed, tokens.reshape(row_count, model_width).astype(jnp.float32))
    branch, first_stored = ffn_forward(start, gain_one, first_weights[0], first_weights[1])
    first = start + 0.5 * branch
    gain_two = second_weights[2][0].astype(jnp.float32)
    branch, second_stored = attention_forward(
        first, gain_two, second_weights[0], second_weights[1], valid, tables, units
    )
    second = first + branch
    gain_three = third_weights[2][0].astype(jnp.float32)
    share = functools.partial(exchange, depth_devices, groups)
    branch, third_stored = conv_forward(
        second, gain_three, third_weights[0], third_weights[1], third_weights[2], live, units, share
    )
    third = second + branch
    gain_four = fourth_weights[2][0].astype(jnp.float32)
    gain_five = fourth_weights[2][1].astype(jnp.float32)
    branch, fourth_stored = ffn_forward(third, gain_four, fourth_weights[0], fourth_weights[1])
    fourth = third + 0.5 * branch
    out_norm, final_normed, final_inverse = layer_norm(fourth, gain_five)
    output = out_norm.astype(jnp.bfloat16).reshape(units, frame_count, model_width)
    upstream = cotangent.reshape(row_count, model_width).astype(jnp.float32)
    grad_four, gain_five_grad = norm_back(upstream, gain_five, final_normed, final_inverse)
    grad_three, fourth_pairs, gain_four_grad = ffn_backward(
        grad_four, fourth_stored, gain_four, fourth_weights[0], fourth_weights[1]
    )
    grad_two, third_pairs, gain_three_grad, kernel_grad, affine_full = conv_backward(
        grad_three,
        third_stored,
        gain_three,
        third_weights[0],
        third_weights[1],
        third_weights[2],
        live,
        units,
        share,
    )
    grad_one, second_pairs, gain_two_grad = attention_backward(
        grad_two, second_stored, gain_two, second_weights[0], second_weights[1], valid, tables
    )
    grad_zero, first_pairs, gain_one_grad = ffn_backward(
        grad_one, first_stored, gain_one, first_weights[0], first_weights[1]
    )
    masked_float = masked_col.astype(jnp.float32)
    embed_grad = jnp.sum(grad_zero * masked_float, axis=0)
    input_grad = (
        (grad_zero * (1.0 - masked_float))
        .astype(jnp.bfloat16)
        .reshape(units, frame_count, model_width)
    )
    small_grads = jnp.concatenate(
        [
            jnp.stack(
                [
                    gain_one_grad,
                    gain_two_grad,
                    gain_three_grad,
                    gain_four_grad,
                    gain_five_grad,
                    embed_grad,
                ]
            ),
            kernel_grad,
            jnp.zeros((5, model_width), jnp.float32),
        ],
        axis=0,
    )
    reduced, small_sum = reduce_all(
        depth_devices,
        groups,
        fourth_pairs + third_pairs + second_pairs + first_pairs,
        small_grads,
        3,
    )
    ffn2_in_grad, ffn2_out_grad, conv_in_grad, conv_out_grad = (
        array.astype(jnp.float32) for array in reduced[:4]
    )
    attn_in_grad, attn_out_grad, ffn1_in_grad, ffn1_out_grad = (
        array.astype(jnp.float32) for array in reduced[4:]
    )
    column_width = norm_gains.shape[1]
    affine_grad = lax.dynamic_slice_in_dim(
        affine_full, lax.axis_index("fsdp") * column_width, column_width, 1
    )
    return (
        output,
        input_grad,
        small_sum[5],
        small_sum[0:5],
        ffn1_in_grad,
        ffn1_out_grad,
        attn_in_grad,
        attn_out_grad,
        conv_in_grad,
        conv_out_grad,
        small_sum[6 : 6 + KER],
        affine_grad,
        ffn2_in_grad,
        ffn2_out_grad,
    )


def solution(mesh):
    in_specs = (
        P(("dp", "fsdp"), None, None),
        P(("dp", "fsdp")),
        P(("dp", "fsdp"), None),
        P("fsdp"),
        P(None, "fsdp"),
        P("fsdp", None),
        P("fsdp", None),
        P("fsdp", None),
        P("fsdp", None),
        P("fsdp", None),
        P("fsdp", None),
        P(None, "fsdp"),
        P(None, "fsdp"),
        P("fsdp", None),
        P("fsdp", None),
        P(("dp", "fsdp"), None, None),
    )
    out_specs = (
        P(("dp", "fsdp"), None, None),
        P(("dp", "fsdp"), None, None),
        P("fsdp"),
        P(None, "fsdp"),
        P("fsdp", None),
        P("fsdp", None),
        P("fsdp", None),
        P("fsdp", None),
        P("fsdp", None),
        P("fsdp", None),
        P(None, "fsdp"),
        P(None, "fsdp"),
        P("fsdp", None),
        P("fsdp", None),
    )
    body = functools.partial(local, mesh.shape["fsdp"], mesh.shape["dp"] // WAYS)
    return jax.shard_map(body, mesh=mesh, in_specs=in_specs, out_specs=out_specs, check_vma=False)
```

```python
import functools

import jax
import jax.numpy as jnp
from jax import lax
from jax.experimental import pallas as pl
from jax.experimental.pallas import tpu as pltpu
from jax.sharding import PartitionSpec as P

HEAD = 128
KER = 5
SPAN_LEN = 10


EPSILON = 1e-05
NEGATIVE = -1000000000.0


def product(left_side, right_side):
    return jnp.dot(left_side, right_side, preferred_element_type=jnp.float32)


def product_nt(left_side, right_side):
    return lax.dot_general(
        left_side, right_side, (((1,), (1,)), ((), ())), preferred_element_type=jnp.float32
    )


def layer_norm(inputs, layer_gain):
    average = jnp.mean(inputs, axis=-1, keepdims=True)
    centered = inputs - average
    inverse = lax.rsqrt(jnp.mean(centered * centered, axis=-1, keepdims=True) + EPSILON)
    normed = centered * inverse
    return (normed * layer_gain, normed, inverse)


def norm_back(upstream, layer_gain, normed, inverse):
    scaled = upstream * layer_gain
    first_mean = jnp.mean(scaled, axis=-1, keepdims=True)
    second_mean = jnp.mean(scaled * normed, axis=-1, keepdims=True)
    return (
        inverse * (scaled - first_mean - normed * second_mean),
        jnp.sum(upstream * normed, axis=0),
    )


def swish_slope(inputs):
    sigmoid_part = jax.nn.sigmoid(inputs)
    return sigmoid_part * (1.0 + inputs * (1.0 - sigmoid_part))


def rotation(frame_count):
    half_size = HEAD // 2
    position = jnp.arange(frame_count, dtype=jnp.float32)
    frequency = 10000.0 ** (-jnp.arange(half_size, dtype=jnp.float32) / half_size)
    angles = position[:, None] * frequency[None, :]
    return (jnp.cos(angles)[:, None, :], jnp.sin(angles)[:, None, :])


def rotate(inputs, cosine, sine):
    half_size = HEAD // 2
    front = inputs[..., :half_size]
    back_half = inputs[..., half_size:]
    return jnp.concatenate(
        [front * cosine - back_half * sine, front * sine + back_half * cosine], axis=-1
    )


MESH = pl.DeviceIdType.MESH
WAYS = 8


def coordinates():
    dp = lax.axis_index("dp")
    z = lax.axis_index("fsdp")
    core_bit = lax.rem(dp, 2)
    x_bit = lax.rem(dp // 2, 2)
    y_bit = lax.rem(dp // 4, 2)
    return dp, z, core_bit, x_bit, y_bit


def signal(sem, device):
    pl.semaphore_signal(sem, inc=1, device_id=device, device_id_type=MESH)


def greet(depth, dp, z, flat_peers):
    barrier = pltpu.get_barrier_semaphore()
    signal(barrier, (dp, lax.rem(z + 1, depth)))
    signal(barrier, (dp, lax.rem(z + depth - 1, depth)))
    for peer in flat_peers:
        signal(barrier, (peer, z))
    pl.semaphore_wait(barrier, 2 + len(flat_peers))


def gather_kernel(depth, count, chunks, lead, *refs):
    shards, small = refs[:count], refs[count]
    fulls, small_full = refs[count + 1 : 2 * count + 1], refs[2 * count + 1]
    send_sems, recv_sems, own_sems, small_sems = refs[2 * count + 2 :]
    dp, z, core_bit, x_bit, y_bit = coordinates()
    mine = lax.rem(dp, WAYS)
    step_c, step_x, step_y = 1 - 2 * core_bit, 2 - 4 * x_bit, 4 - 8 * y_bit
    peer_c, peer_x, peer_y = dp + step_c, dp + step_x, dp + step_y
    greet(depth, dp, z, (peer_c, peer_x, peer_y))

    def remote(source, target, send_sem, recv_sem, device):
        return pltpu.make_async_remote_copy(
            source, target, send_sem, recv_sem, device_id=device, device_id_type=MESH
        )

    def slot(chunk, owner, piece, half):
        index, first, width = chunks[chunk]
        rows = shards[index].shape[0]
        part = rows // WAYS
        if half is not None:
            width = width // 2
            first = first + half * width
        start = pl.multiple_of(owner * rows + piece * part, part)
        return fulls[index].at[pl.ds(start, part), pl.ds(first, width)]

    def place(chunk, index, message, owner, piece, device, half=None):
        where = slot(chunk, owner, piece, half)
        return remote(
            where,
            where,
            send_sems.at[chunk, index, message],
            recv_sems.at[chunk, index, message],
            device,
        )

    def each(action):
        for hop in range(depth - 1):

            @pl.when(z - 1 - hop >= 0)
            def _():
                action(2 * hop, z - 1 - hop, hop, 1)

            @pl.when(z + 1 + hop < depth)
            def _():
                action(2 * hop + 1, z + 1 + hop, hop, -1)

    here = (dp, z)
    core_dev, x_dev, y_dev = (peer_c, z), (peer_x, z), (peer_y, z)
    piece_x, piece_y, piece_xy = mine + step_x, mine + step_y, mine + step_x + step_y
    other = mine + step_c
    other_x, other_y, other_xy = other + step_x, other + step_y, other + step_x + step_y

    small_local = pltpu.make_async_copy(small, small_full.at[z], own_sems.at[count, 0])
    small_local.start()

    def small_out(index, source, owner, device):
        return remote(
            source, small_full.at[owner], small_sems.at[index, 0], small_sems.at[index, 1], device
        )

    @pl.when(z + 1 < depth)
    def _():
        small_out(0, small, z, (dp, z + 1)).start()

    @pl.when(z > 0)
    def _():
        small_out(1, small, z, (dp, z - 1)).start()

    def line_start(chunk):
        index, first, width = chunks[chunk]
        part = shards[index].shape[0] // WAYS
        source = shards[index].at[
            pl.ds(pl.multiple_of(mine * part, part), part), pl.ds(first, width)
        ]
        target = slot(chunk, z, mine, None)

        @pl.when(z + 1 < depth)
        def _():
            remote(
                source, target, send_sems.at[chunk, 0, 0], recv_sems.at[chunk, 0, 0], (dp, z + 1)
            ).start()

        @pl.when(z > 0)
        def _():
            remote(
                source, target, send_sems.at[chunk, 1, 0], recv_sems.at[chunk, 1, 0], (dp, z - 1)
            ).start()

    def line_arrived(chunk):
        def action(index, owner, hop, way):
            place(chunk, index, 0, owner, mine, here).wait_recv()
            if hop < depth - 2:
                following = z + way

                @pl.when((following >= 0) & (following < depth))
                def _():
                    place(chunk, index + 2, 0, owner, mine, (dp, following)).start()

            place(chunk, index, 1, owner, mine, x_dev).start()
            place(chunk, index, 2, owner, mine, y_dev).start()
            place(chunk, index, 5, owner, mine, core_dev).start()

        each(action)

    def plane_arrived(chunk):
        def action(index, owner, hop, way):
            place(chunk, index, 1, owner, piece_x, here).wait_recv()
            place(chunk, index, 3, owner, piece_x, y_dev, 0).start()
            place(chunk, index, 6, owner, piece_x, core_dev).start()
            place(chunk, index, 2, owner, piece_y, here).wait_recv()
            place(chunk, index, 4, owner, piece_y, x_dev, 1).start()
            place(chunk, index, 7, owner, piece_y, core_dev).start()

        each(action)

    def corner_arrived(chunk):
        def action(index, owner, hop, way):
            for half in range(2):
                place(chunk, index, 3 + half, owner, piece_xy, here, half).wait_recv()
                place(chunk, index, 8 + half, owner, piece_xy, core_dev, half).start()

        each(action)

    def core_arrived(chunk):
        def action(index, owner, hop, way):
            place(chunk, index, 5, owner, other, here).wait_recv()
            place(chunk, index, 6, owner, other_x, here).wait_recv()
            place(chunk, index, 7, owner, other_y, here).wait_recv()
            for half in range(2):
                place(chunk, index, 8 + half, owner, other_xy, here, half).wait_recv()

        each(action)

    def small_action(index, owner, hop, way):
        small_out(index, small, owner, here).wait_recv()
        if hop < depth - 2:
            following = z + way

            @pl.when((following >= 0) & (following < depth))
            def _():
                small_out(index + 2, small_full.at[owner], owner, (dp, following)).start()

    total = len(chunks)
    for chunk in range(min(lead, total)):
        line_start(chunk)
    own_copies = []
    for index in range(count):
        rows = shards[index].shape[0]
        target = fulls[index].at[pl.ds(pl.multiple_of(z * rows, rows), rows)]
        copy = remote(
            shards[index], target, own_sems.at[index, 0], own_sems.at[index, 1], core_dev
        )
        copy.start()
        own_copies.append(copy)
    for turn in range(total + 3):
        if turn + lead < total:
            line_start(turn + lead)
        if turn < total:
            line_arrived(turn)
        if turn == 0:
            each(small_action)
        if 0 <= turn - 1 < total:
            plane_arrived(turn - 1)
        if 0 <= turn - 2 < total:
            corner_arrived(turn - 2)
        if 0 <= turn - 3 < total:
            core_arrived(turn - 3)
    for copy in own_copies:
        copy.wait()
    small_local.wait()

    @pl.when(z + 1 < depth)
    def _():
        small_out(0, small, z, here).wait_send()

    @pl.when(z > 0)
    def _():
        small_out(1, small, z, here).wait_send()

    def small_drain(index, owner, hop, way):
        if hop < depth - 2:
            following = z + way

            @pl.when((following >= 0) & (following < depth))
            def _():
                small_out(index + 2, small, owner, here).wait_send()

    each(small_drain)
    for chunk in range(total):

        @pl.when(z + 1 < depth)
        def _():
            place(chunk, 0, 0, z, mine, here).wait_send()

        @pl.when(z > 0)
        def _():
            place(chunk, 1, 0, z, mine, here).wait_send()

        def drain(index, owner, hop, way):
            if hop < depth - 2:
                following = z + way

                @pl.when((following >= 0) & (following < depth))
                def _():
                    place(chunk, index + 2, 0, owner, mine, here).wait_send()

            for message in (1, 2, 5, 6, 7):
                place(chunk, index, message, owner, mine, here).wait_send()
            for message in (3, 4, 8, 9):
                place(chunk, index, message, owner, mine, here, 0).wait_send()

        each(drain)


def gather_all(depth, weights, small):
    count = len(weights)
    chunks = [(index, 0, weight.shape[1]) for index, weight in enumerate(weights)]
    shape = (len(chunks), 2 * (depth - 1), 10)
    outs = [
        jax.ShapeDtypeStruct((weight.shape[0] * depth, weight.shape[1]), weight.dtype)
        for weight in weights
    ]
    outs.append(jax.ShapeDtypeStruct((depth,) + small.shape, small.dtype))
    return pl.pallas_call(
        functools.partial(gather_kernel, depth, count, chunks, 2),
        out_shape=outs,
        in_specs=[pl.BlockSpec(memory_space=pl.ANY)] * (count + 1),
        out_specs=[pl.BlockSpec(memory_space=pl.ANY)] * (count + 1),
        scratch_shapes=[
            pltpu.SemaphoreType.DMA(shape),
            pltpu.SemaphoreType.DMA(shape),
            pltpu.SemaphoreType.DMA((count + 1, 2)),
            pltpu.SemaphoreType.DMA((2 * (depth - 1), 2)),
        ],
        compiler_params=pltpu.CompilerParams(collective_id=0, has_side_effects=True),
    )(*weights, small)


def add_pair(left, right):
    return left + right


def join_moments(left, right):
    count = left[0:1] + right[0:1]
    mean = (left[0:1] * left[1:2] + right[0:1] * right[1:2]) / count
    gap = right[1:2] - left[1:2]
    spread = left[2:3] + right[2:3] + gap * gap * (left[0:1] * right[0:1] / count)
    return jnp.concatenate([count, mean, spread, left[3:]], axis=0)


def exchange_kernel(depth, groups, combine, value, result, work, inbox, line, send_sems, recv_sems):
    dp, z, core_bit, x_bit, y_bit = coordinates()
    peers = [dp + 1 - 2 * core_bit, dp + 2 - 4 * x_bit, dp + 4 - 8 * y_bit]
    group = dp // WAYS
    barrier = pltpu.get_barrier_semaphore()
    far = [lax.rem(group + step, groups) * WAYS + lax.rem(dp, WAYS) for step in range(1, groups)]
    for peer in peers + far:
        signal(barrier, (peer, z))
    for step in range(1, depth):
        signal(barrier, (dp, lax.rem(z + step, depth)))
    pl.semaphore_wait(barrier, len(peers) + len(far) + depth - 1)
    work[0] = value[...]
    for turn, peer in enumerate(peers):
        copy = pltpu.make_async_remote_copy(
            work.at[turn],
            inbox.at[turn],
            send_sems.at[turn],
            recv_sems.at[turn],
            device_id=(peer, z),
            device_id_type=MESH,
        )
        copy.start()
        copy.wait()
        work[turn + 1] = combine(work[turn], inbox[turn])

    def spread(source, slots, first, targets, own):
        copies = []
        for step, target in enumerate(targets):
            copy = pltpu.make_async_remote_copy(
                source,
                slots.at[own],
                send_sems.at[first + step],
                recv_sems.at[first + step],
                device_id=target,
                device_id_type=MESH,
            )
            copy.start()
            copies.append(copy)
        local = pltpu.make_async_copy(source, slots.at[own], send_sems.at[first + len(targets)])
        local.start()
        for copy in copies:
            copy.wait()
        local.wait()

    last = len(peers)
    if groups > 1:
        spread(work.at[last], inbox.at[pl.ds(last, groups)], last, [(peer, z) for peer in far], group)
        total = inbox[last]
        for step in range(1, groups):
            total = combine(total, inbox[last + step])
        work[last] = total
    first = last + groups
    spread(
        work.at[last],
        line,
        first,
        [(dp, lax.rem(z + step, depth)) for step in range(1, depth)],
        z,
    )
    total = line[0]
    for step in range(1, depth):
        total = combine(total, line[step])
    result[...] = total


def exchange(depth, groups, combine, value, collective):
    shape = value.shape
    sems = 3 + groups + depth
    return pl.pallas_call(
        functools.partial(exchange_kernel, depth, groups, combine),
        out_shape=jax.ShapeDtypeStruct(shape, value.dtype),
        in_specs=[pl.BlockSpec(memory_space=pltpu.VMEM)],
        out_specs=pl.BlockSpec(memory_space=pltpu.VMEM),
        scratch_shapes=[
            pltpu.VMEM((4,) + shape, value.dtype),
            pltpu.VMEM((3 + groups,) + shape, value.dtype),
            pltpu.VMEM((depth,) + shape, value.dtype),
            pltpu.SemaphoreType.DMA((sems,)),
            pltpu.SemaphoreType.DMA((sems,)),
        ],
        compiler_params=pltpu.CompilerParams(collective_id=collective, has_side_effects=True),
    )(value)


LANES = 128
HELD = 3
TILE = 512
ROWS = 256


def column_tile(index):
    return pl.ds(index * TILE, TILE)


def row_blocks(rows, body):
    def step(block):
        body(pl.ds(pl.multiple_of(block * ROWS, ROWS), ROWS))

    pl.loop(0, rows // ROWS)(step)


def nt(left_side, right_side):
    return lax.dot_general(
        left_side, right_side, (((1,), (1,)), ((), ())), preferred_element_type=jnp.float32
    )


def backward_units(inputs, made, results, scratch, small_first, pair_start):
    (
        grad_in,
        branch_in,
        queries_in,
        keys_in,
        values_in,
        attn_in_w,
        attn_out_w,
        ffn_in_w,
        ffn_out_w,
        inner_in,
        first_in,
        start_in,
        log_total,
        live,
        masked,
        cosine,
        sine,
        gains,
        small,
    ) = inputs
    joined_out, fresh_out, inner_out = made
    (input_grad,) = results
    (
        heads,
        joined,
        row_tiles,
        column_tiles,
        inner_tiles,
        grad,
        resid,
        total,
        gain_rows,
        sems,
        row_sems,
        column_sems,
        inner_sems,
        put_sems,
    ) = scratch
    frames, width = grad.shape
    ff_tiles = inner_in.shape[1] // TILE
    joined_tiles = joined_out.shape[1] // TILE
    row_plan = [(attn_out_w, index) for index in range(width // TILE)]
    row_plan += [(ffn_out_w, index) for index in range(ff_tiles)]
    column_plan = [(attn_in_w, index) for index in range(joined_tiles)]
    column_plan += [(ffn_in_w, index) for index in range(ff_tiles)]

    def row_copy(at):
        source, index = row_plan[at]
        return pltpu.make_async_copy(
            source.at[pl.ds(index * TILE, TILE)], row_tiles.at[at % 2], row_sems.at[at % 2]
        )

    def column_copy(at):
        source, index = column_plan[at]
        return pltpu.make_async_copy(
            source.at[:, column_tile(index)], column_tiles.at[at % 2], column_sems.at[at % 2]
        )

    def inner_copy(at):
        return pltpu.make_async_copy(
            inner_in.at[:, column_tile(at)], inner_tiles.at[at % 2], inner_sems.at[at % 2]
        )

    first_loads = [
        pltpu.make_async_copy(source, target, sems.at[index])
        for index, (source, target) in enumerate(
            (
                (branch_in, joined.at[:, pl.ds(0, width)]),
                (queries_in, heads.at[0]),
                (keys_in, heads.at[1]),
                (values_in, heads.at[2]),
                (grad_in, grad),
                (first_in, resid),
            )
        )
    ]

    def start_loads():
        for copy in first_loads[:1]:
            copy.start()
        for at in range(2):
            row_copy(at).start()
        for copy in first_loads[1:]:
            copy.start()
        for at in range(2):
            column_copy(at).start()
            inner_copy(at).start()

    def merged_grad():
        first_loads[0].wait()
        for at in range(width // TILE):
            row_copy(at).wait()

            def body(rows, at=at):
                heads[3, rows, column_tile(at)] = nt(
                    joined[rows, pl.ds(0, width)], row_tiles[at % 2]
                ).astype(jnp.bfloat16)

            row_blocks(frames, body)
            row_copy(at + 2).start()
        for copy in first_loads[1:4]:
            copy.wait()

    def turned(gradient):
        return gradient * cosine[...] + pltpu.roll(gradient, HEAD // 2, 1) * sine[...]

    def head_step(head):
        columns = pl.ds(pl.multiple_of(head * HEAD, HEAD), HEAD)
        query, key, value = heads[0, :, columns], heads[1, :, columns], heads[2, :, columns]
        upstream = heads[3, :, columns]
        scale = HEAD ** (-0.5)
        scores = jnp.where(live[...] > 0.0, nt(key, query) * scale, NEGATIVE)
        probs = jnp.exp(scores - log_total[head])
        value_grad = product(probs.astype(jnp.bfloat16), upstream)
        prob_grad = nt(value, upstream)
        row_term = jnp.sum(probs * prob_grad, axis=0, keepdims=True)
        score_grad = (probs * (prob_grad - row_term) * scale).astype(jnp.bfloat16)
        key_grad = turned(product(score_grad, query))
        query_grad = turned(
            lax.dot_general(
                score_grad, key, (((0,), (0,)), ((), ())), preferred_element_type=jnp.float32
            )
        )
        for part, value_of in enumerate((query_grad, key_grad, value_grad)):
            target = pl.ds(pl.multiple_of(part * width + head * HEAD, HEAD), HEAD)
            joined[:, target] = value_of.astype(jnp.bfloat16)

    def some_heads(low_head, high_head):
        def unit():
            pl.loop(low_head, high_head)(head_step)

        return unit

    joined_store = pltpu.make_async_copy(joined, joined_out, sems.at[6])
    fresh_store = pltpu.make_async_copy(heads.at[0], fresh_out, sems.at[7])
    start_load = pltpu.make_async_copy(start_in, resid, sems.at[5])
    grad_store = pltpu.make_async_copy(heads.at[1], input_grad, sems.at[8])

    def add_tile(at, source_of, first):
        column_copy(at).wait()

        def body(rows):
            product_part = nt(source_of(rows), column_tiles[at % 2])
            total[rows] = product_part if first else total[rows] + product_part

        row_blocks(frames, body)
        if at + 2 < len(column_plan):
            column_copy(at + 2).start()

    def project(low_tile, high_tile):
        def unit():
            if low_tile == 0:
                joined_store.start()
            for at in range(low_tile, high_tile):
                add_tile(at, lambda rows, at=at: joined[rows, column_tile(at)], at == 0)

        return unit

    def norm_step(row, rows, gain):
        value = resid[rows]
        centered = value - jnp.mean(value, axis=-1, keepdims=True)
        inverse = lax.rsqrt(jnp.mean(centered * centered, axis=-1, keepdims=True) + EPSILON)
        normed = centered * inverse
        upstream = total[rows]
        scaled = upstream * gain
        first_mean = jnp.mean(scaled, axis=-1, keepdims=True)
        second_mean = jnp.mean(scaled * normed, axis=-1, keepdims=True)
        gain_rows[row] = gain_rows[row] + jnp.sum(upstream * normed, axis=0, keepdims=True)
        grad[rows] = grad[rows] + inverse * (scaled - first_mean - normed * second_mean)

    def attention_done():
        joined_store.wait()
        pair_start(0)
        for copy in first_loads[4:]:
            copy.wait()
        gain_rows[...] = jnp.zeros_like(gain_rows)
        gain = gains[1:2]

        def body(rows):
            norm_step(1, rows, gain)
            heads[0, rows] = (0.5 * grad[rows]).astype(jnp.bfloat16)

        row_blocks(frames, body)
        start_load.start()
        fresh_store.start()

    def inner_put(at):
        return pltpu.make_async_copy(
            joined.at[:, column_tile(at % 2)], inner_out.at[:, column_tile(at)], put_sems.at[at % 2]
        )

    def feed_tiles(low_tile, high_tile):
        def unit():
            for at in range(low_tile, high_tile):
                if at == 0:
                    fresh_store.wait()
                    pair_start(1)
                row_at = width // TILE + at
                row_copy(row_at).wait()
                inner_copy(at).wait()
                if at >= 2:
                    inner_put(at - 2).wait()

                def body(rows, at=at, row_at=row_at):
                    active_grad = nt(heads[0, rows], row_tiles[row_at % 2])
                    inner = inner_tiles[at % 2, rows]
                    gate = jax.nn.sigmoid(inner)
                    joined[rows, column_tile(at % 2)] = (
                        active_grad * (gate * (1.0 + inner * (1.0 - gate)))
                    ).astype(jnp.bfloat16)

                row_blocks(frames, body)
                inner_put(at).start()
                if row_at + 2 < len(row_plan):
                    row_copy(row_at + 2).start()
                if at + 2 < ff_tiles:
                    inner_copy(at + 2).start()
                add_tile(
                    joined_tiles + at, lambda rows, at=at: joined[rows, column_tile(at % 2)], at == 0
                )
            if high_tile == ff_tiles:
                for at in range(ff_tiles - 2, ff_tiles):
                    inner_put(at).wait()
                pair_start(2)

        return unit

    def feed_done():
        start_load.wait()
        gain = gains[0:1]

        def body(rows):
            norm_step(0, rows, gain)
            hidden = masked[rows]
            final = grad[rows]
            gain_rows[2] = gain_rows[2] + jnp.sum(final * hidden, axis=0, keepdims=True)
            heads[1, rows] = (final * (1.0 - hidden)).astype(jnp.bfloat16)

        row_blocks(frames, body)
        grad_store.start()
        small_first[...] = small[...]
        small_first[0:1] = gain_rows[0]
        small_first[1:2] = gain_rows[1]
        small_first[5:6] = gain_rows[2]
        grad_store.wait()

    head_count = width // HEAD
    units = [merged_grad]
    for at in range(0, head_count, 2):
        units.append(some_heads(at, at + 2))
    for at in range(0, joined_tiles, 3):
        units.append(project(at, at + 3))
    units.append(attention_done)
    for at in range(0, ff_tiles, 2):
        units.append(feed_tiles(at, at + 2))
    units.append(feed_done)
    return start_loads, units


INPUTS = 19


def reduce_kernel(depth, groups, count, chunks, given, late, *refs):
    extra, refs = refs[:INPUTS], refs[INPUTS:]
    given_refs, refs = refs[: len(given)], refs[len(given) :]
    outs, small_out = refs[:count], refs[count]
    input_grad, made = refs[count + 1], refs[count + 2 : count + 2 + len(late)]
    at = count + 2 + len(late)
    left_peers, right_peers = refs[at : at + count], refs[at + count : at + 2 * count]
    at += 2 * count
    slots = dict(zip(given, given_refs))
    for name, ref in zip(late, made):
        slots[(name, 1)] = ref
    lefts = [slots[(index, 0)] for index in range(count)]
    rights = [slots[(index, 1)] for index in range(count)]
    unit_scratch, refs = refs[at : at + 14], refs[at + 14 :]
    at = 0
    (
        left_buf,
        right_buf,
        held,
        first_in,
        second_in,
        line_in,
        far_in,
        final,
        small_work,
        small_in,
        small_line,
        pair_send,
        pair_recv,
        load_sems,
        send_sems,
        recv_sems,
        store_sems,
        small_send,
        small_recv,
    ) = refs[at:]
    dp, z, core_bit, x_bit, y_bit = coordinates()
    group = dp // WAYS
    peer_c, peer_x, peer_y = (
        dp + 1 - 2 * core_bit,
        dp + 2 - 4 * x_bit,
        dp + 4 - 8 * y_bit,
    )
    far = [lax.rem(group + step, groups) * WAYS + lax.rem(dp, WAYS) for step in range(1, groups)]
    barrier = pltpu.get_barrier_semaphore()
    for peer in [peer_c, peer_x, peer_y] + far:
        signal(barrier, (peer, z))
    for step in range(1, depth):
        signal(barrier, (dp, lax.rem(z + step, depth)))
    pl.semaphore_wait(barrier, 3 + len(far) + depth - 1)
    tokens = lefts[0].shape[0]
    block = left_buf.shape[2] // depth
    here = (dp, z)

    def remote(source, target, send_sem, recv_sem, device):
        return pltpu.make_async_remote_copy(
            source, target, send_sem, recv_sem, device_id=device, device_id_type=MESH
        )

    pair_copies = []
    for index in range(count):
        half = rights[index].shape[1] // 2
        columns = pl.ds(pl.multiple_of((1 - core_bit) * half, half), half)
        pair_copies.append(
            (
                remote(
                    lefts[index],
                    left_peers[index],
                    pair_send.at[index, 0],
                    pair_recv.at[index, 0],
                    (peer_c, z),
                ),
                remote(
                    rights[index].at[:, columns],
                    right_peers[index],
                    pair_send.at[index, 1],
                    pair_recv.at[index, 1],
                    (peer_c, z),
                ),
            )
        )

    def pair_start(index):
        for copy in pair_copies[index]:
            copy.start()

    for index in range(count):
        if index not in late:
            pair_start(index)
    start_loads, units = backward_units(
        extra,
        made,
        (input_grad,),
        unit_scratch,
        small_work.at[0],
        lambda number: pair_start(late[number]),
    )
    start_loads()

    def loads(chunk):
        index, row, part, left_slot, right_slot, new_left, new_right = chunks[chunk]
        rows = lefts[index].shape[1] // depth
        half = rights[index].shape[1] // 2
        piece = half // 4
        copies = []
        if new_left:
            for side, source in enumerate((lefts[index], left_peers[index])):
                for owner in range(depth):
                    copies.append(
                        pltpu.make_async_copy(
                            source.at[:, pl.ds(owner * rows + row, block)],
                            left_buf.at[
                                left_slot, pl.ds(side * tokens, tokens), pl.ds(owner * block, block)
                            ],
                            load_sems.at[left_slot, side * depth + owner],
                        )
                    )
        if new_right:
            for quarter in range(4):
                start = quarter * piece + part * LANES
                own_start = pl.multiple_of(core_bit * half + start, LANES)
                target = pl.ds(quarter * LANES, LANES)
                copies.append(
                    pltpu.make_async_copy(
                        rights[index].at[:, pl.ds(own_start, LANES)],
                        right_buf.at[right_slot, pl.ds(0, tokens), target],
                        load_sems.at[2 + right_slot, quarter],
                    )
                )
                copies.append(
                    pltpu.make_async_copy(
                        right_peers[index].at[:, pl.ds(start, LANES)],
                        right_buf.at[right_slot, pl.ds(tokens, tokens), target],
                        load_sems.at[2 + right_slot, 4 + quarter],
                    )
                )
        return copies

    arrived = set()

    def load_start(chunk):
        index = chunks[chunk][0]
        if index not in arrived:
            arrived.add(index)
            for copy in pair_copies[index]:
                copy.wait_recv()
        for copy in loads(chunk):
            copy.start()

    def axes(chunk):
        if chunk % 2 == 0:
            return peer_x, peer_y, x_bit, y_bit
        return peer_y, peer_x, y_bit, x_bit

    def quarter_of(chunk, first_bit, second_bit):
        if chunk % 2 == 0:
            return 2 * first_bit + second_bit
        return 2 * second_bit + first_bit

    def first_copy(chunk, which, device):
        _, _, first_bit, _ = axes(chunk)
        return remote(
            held.at[chunk % HELD, quarter_of(chunk, 1 - first_bit, which)],
            first_in.at[chunk, which],
            send_sems.at[chunk, which],
            recv_sems.at[chunk, which],
            device,
        )

    def second_copy(chunk, device):
        _, _, _, second_bit = axes(chunk)
        return remote(
            first_in.at[chunk, 1 - second_bit],
            second_in.at[chunk],
            send_sems.at[chunk, 2],
            recv_sems.at[chunk, 2],
            device,
        )

    def line_copy(chunk, step, device):
        return remote(
            second_in.at[chunk, lax.rem(z + step, depth)],
            line_in.at[chunk, step - 1],
            send_sems.at[chunk, 2 + step],
            recv_sems.at[chunk, 2 + step],
            device,
        )

    def multiply(chunk):
        index, row, part, left_slot, right_slot, new_left, new_right = chunks[chunk]
        for copy in loads(chunk):
            copy.wait()
        if chunk + 1 < len(chunks):
            load_start(chunk + 1)
        if chunk >= HELD:
            for which in range(2):
                first_copy(chunk - HELD, which, here).wait_send()

        def body(owner):
            columns = pl.ds(pl.multiple_of(owner * block, block), block)
            product = lax.dot_general(
                left_buf[left_slot, :, columns],
                right_buf[right_slot],
                (((0,), (0,)), ((), ())),
                preferred_element_type=jnp.float32,
            ).astype(jnp.bfloat16)
            for quarter in range(4):
                held[chunk % HELD, quarter, owner] = product[
                    :, quarter * LANES : (quarter + 1) * LANES
                ]

        pl.loop(0, depth)(body)
        first_peer, _, _, _ = axes(chunk)
        for which in range(2):
            first_copy(chunk, which, (first_peer, z)).start()

    def add_first(chunk):
        _, second_peer, first_bit, second_bit = axes(chunk)
        for which in range(2):
            first_copy(chunk, which, here).wait_recv()

        def add(which):
            first_in[chunk, which] = (
                first_in[chunk, which].astype(jnp.float32)
                + held[chunk % HELD, quarter_of(chunk, first_bit, which)].astype(jnp.float32)
            ).astype(jnp.bfloat16)

        add(1 - second_bit)
        second_copy(chunk, (second_peer, z)).start()
        add(second_bit)

    def add_second(chunk):
        _, _, _, second_bit = axes(chunk)
        second_copy(chunk, here).wait_recv()
        second_in[chunk] = (
            second_in[chunk].astype(jnp.float32) + first_in[chunk, second_bit].astype(jnp.float32)
        ).astype(jnp.bfloat16)
        for step in range(1, depth):
            line_copy(chunk, step, (dp, lax.rem(z + step, depth))).start()

    base = 2 + depth

    def where(chunk, core, x_at, y_at, half=None):
        index, row, part = chunks[chunk][:3]
        width = outs[index].shape[1]
        start = core * (width // 2) + (2 * x_at + y_at) * (width // 8) + part * LANES
        size = block
        if half is not None:
            size = block // 2
            row = row + half * size
        return outs[index].at[pl.ds(row, size), pl.ds(pl.multiple_of(start, LANES), LANES)]

    def from_final(chunk, message, device):
        return remote(
            final.at[chunk],
            where(chunk, core_bit, x_bit, y_bit),
            send_sems.at[chunk, base + message],
            recv_sems.at[chunk, base + message],
            device,
        )

    def passed(chunk, message, core, x_at, y_at, device, half=None):
        place = where(chunk, core, x_at, y_at, half)
        return remote(
            place,
            place,
            send_sems.at[chunk, base + message],
            recv_sems.at[chunk, base + message],
            device,
        )

    def store(chunk):
        return pltpu.make_async_copy(
            final.at[chunk], where(chunk, core_bit, x_bit, y_bit), store_sems.at[chunk]
        )

    def far_copy(chunk, step, device):
        return remote(
            far_in.at[chunk, groups],
            far_in.at[chunk, group],
            send_sems.at[chunk, base + 9 + step],
            recv_sems.at[chunk, base + 9 + step],
            device,
        )

    def finish(chunk):
        for step in range(1, depth):
            line_copy(chunk, step, here).wait_recv()
        total = second_in[chunk, z].astype(jnp.float32)
        for step in range(1, depth):
            total = total + line_in[chunk, step - 1].astype(jnp.float32)
        if groups > 1:
            own = total.astype(jnp.bfloat16)
            far_in[chunk, groups] = own
            far_in[chunk, group] = own
            for step, peer in enumerate(far):
                far_copy(chunk, step, (peer, z)).start()
            for step in range(len(far)):
                far_copy(chunk, step, here).wait()
            total = far_in[chunk, 0].astype(jnp.float32)
            for step in range(1, groups):
                total = total + far_in[chunk, step].astype(jnp.float32)
        final[chunk] = total.astype(jnp.bfloat16)
        for message, peer in enumerate((peer_x, peer_y, peer_c)):
            from_final(chunk, message, (peer, z)).start()
        store(chunk).start()

    def plane_arrived(chunk):
        passed(chunk, 0, core_bit, 1 - x_bit, y_bit, here).wait_recv()
        passed(chunk, 3, core_bit, 1 - x_bit, y_bit, (peer_y, z), 0).start()
        passed(chunk, 5, core_bit, 1 - x_bit, y_bit, (peer_c, z)).start()
        passed(chunk, 1, core_bit, x_bit, 1 - y_bit, here).wait_recv()
        passed(chunk, 4, core_bit, x_bit, 1 - y_bit, (peer_x, z), 1).start()
        passed(chunk, 6, core_bit, x_bit, 1 - y_bit, (peer_c, z)).start()

    def corner_arrived(chunk):
        for half in range(2):
            passed(chunk, 3 + half, core_bit, 1 - x_bit, 1 - y_bit, here, half).wait_recv()
            passed(chunk, 7 + half, core_bit, 1 - x_bit, 1 - y_bit, (peer_c, z), half).start()

    def core_arrived(chunk):
        other = 1 - core_bit
        passed(chunk, 2, other, x_bit, y_bit, here).wait_recv()
        passed(chunk, 5, other, 1 - x_bit, y_bit, here).wait_recv()
        passed(chunk, 6, other, x_bit, 1 - y_bit, here).wait_recv()
        for half in range(2):
            passed(chunk, 7 + half, other, 1 - x_bit, 1 - y_bit, here, half).wait_recv()

    def small_copy(turn, device):
        return remote(
            small_work.at[turn],
            small_in.at[turn],
            small_send.at[turn],
            small_recv.at[turn],
            device,
        )

    def small_far_copy(step, device):
        return remote(
            small_work.at[3],
            small_in.at[3 + group],
            small_send.at[3 + step],
            small_recv.at[3 + step],
            device,
        )

    slice_width = small_out.shape[1]

    def small_line_copy(step, device):
        columns = pl.ds(
            pl.multiple_of(lax.rem(z + step, depth) * slice_width, slice_width), slice_width
        )
        return remote(
            small_work.at[4, :, columns],
            small_line.at[step - 1],
            small_send.at[2 + groups + step],
            small_recv.at[2 + groups + step],
            device,
        )

    small_peers = (peer_c, peer_x, peer_y)

    def small_turn(turn):
        if 1 <= turn <= 3:
            small_copy(turn - 1, here).wait_recv()
            small_work[turn] = small_work[turn - 1] + small_in[turn - 1]
        if turn < 3:
            small_copy(turn, (small_peers[turn], z)).start()
        if turn == 3:
            if groups > 1:
                small_in[3 + group] = small_work[3]
                for step, peer in enumerate(far):
                    small_far_copy(step, (peer, z)).start()
                for step in range(len(far)):
                    small_far_copy(step, here).wait()
                total = small_in[3]
                for step in range(1, groups):
                    total = total + small_in[3 + step]
                small_work[4] = total
            else:
                small_work[4] = small_work[3]
            for step in range(1, depth):
                small_line_copy(step, (dp, lax.rem(z + step, depth))).start()
        if turn == 4:
            columns = pl.ds(pl.multiple_of(z * slice_width, slice_width), slice_width)
            total = small_work[4, :, columns]
            for step in range(1, depth):
                small_line_copy(step, here).wait_recv()
                total = total + small_line[step - 1]
            small_out[...] = total

    total_chunks = len(chunks)
    load_start(0)
    for turn in range(total_chunks + 9):
        if turn < total_chunks:
            multiply(turn)
        if turn < len(units):
            units[turn]()
        if 0 <= turn - len(units) < 5:
            small_turn(turn - len(units))
        for lag, action in (
            (2, add_first),
            (4, add_second),
            (5, finish),
            (6, plane_arrived),
            (7, corner_arrived),
            (8, core_arrived),
        ):
            if 0 <= turn - lag < total_chunks:
                action(turn - lag)
    for index in range(count):
        for copy in pair_copies[index]:
            copy.wait_send()
    for turn in range(3):
        small_copy(turn, here).wait_send()
    for step in range(1, depth):
        small_line_copy(step, here).wait_send()
    for chunk in range(total_chunks):
        if chunk >= total_chunks - HELD:
            for which in range(2):
                first_copy(chunk, which, here).wait_send()
        second_copy(chunk, here).wait_send()
        for step in range(1, depth):
            line_copy(chunk, step, here).wait_send()
        for message in range(3):
            from_final(chunk, message, here).wait_send()
        for message in (5, 6):
            passed(chunk, message, core_bit, x_bit, y_bit, here).wait_send()
        for message in (3, 4, 7, 8):
            passed(chunk, message, core_bit, x_bit, y_bit, here, 0).wait_send()
        store(chunk).wait()


def reduce_chunks(depth, pairs, block):
    chunks = []
    left_slot, right_slot = 1, 1
    last_left, last_right = None, None
    for index, (left, right) in enumerate(pairs):
        rows = left.shape[1] // depth
        for row in range(0, rows, block):
            for part in range(right.shape[1] // (WAYS * LANES)):
                new_left = last_left != (index, row)
                new_right = last_right != (index, part)
                if new_left:
                    left_slot = 1 - left_slot
                if new_right:
                    right_slot = 1 - right_slot
                last_left, last_right = (index, row), (index, part)
                chunks.append((index, row, part, left_slot, right_slot, new_left, new_right))
    return chunks


def reduce_all(depth, groups, pairs, extra, small, collective):
    count = len(pairs)
    tokens = pairs[0][0].shape[0]
    width = small.shape[1]
    block = width // depth
    shapes = [
        (left, right if not isinstance(right, int) else jax.ShapeDtypeStruct((tokens, right), left.dtype))
        for left, right in pairs
    ]
    chunks = reduce_chunks(depth, shapes, block)
    total = len(chunks)
    low = jnp.bfloat16
    given, operands, late = [], [], []
    for index, (left, right) in enumerate(pairs):
        given.append((index, 0))
        operands.append(left)
        if isinstance(right, int):
            late.append(index)
        else:
            given.append((index, 1))
            operands.append(right)
    outs, made, left_peers, right_peers = [], [], [], []
    for index, (left, right) in enumerate(shapes):
        outs.append(jax.ShapeDtypeStruct((left.shape[1] // depth, right.shape[1]), low))
        left_peers.append(jax.ShapeDtypeStruct(left.shape, low))
        right_peers.append(jax.ShapeDtypeStruct((tokens, right.shape[1] // 2), low))
        if index in late:
            made.append(jax.ShapeDtypeStruct(right.shape, low))
    outs.append(jax.ShapeDtypeStruct((small.shape[0], block), jnp.float32))
    outs.append(jax.ShapeDtypeStruct((tokens, width), low))
    messages = 2 + depth + 9 + groups
    any_spec = pl.BlockSpec(memory_space=pl.ANY)
    vmem_spec = pl.BlockSpec(memory_space=pltpu.VMEM)
    results = pl.pallas_call(
        functools.partial(reduce_kernel, depth, groups, count, chunks, given, late),
        out_shape=outs + made + left_peers + right_peers,
        in_specs=[any_spec] * 12 + [vmem_spec] * 7 + [any_spec] * len(operands),
        out_specs=[any_spec] * count
        + [vmem_spec]
        + [any_spec] * (1 + len(made) + 2 * count),
        scratch_shapes=[
            pltpu.VMEM((4, tokens, width), low),
            pltpu.VMEM((tokens, 3 * width), low),
            pltpu.VMEM((2, TILE, width), low),
            pltpu.VMEM((2, width, TILE), low),
            pltpu.VMEM((2, tokens, TILE), jnp.float32),
            pltpu.VMEM((tokens, width), jnp.float32),
            pltpu.VMEM((tokens, width), jnp.float32),
            pltpu.VMEM((tokens, width), jnp.float32),
            pltpu.VMEM((3, 1, width), jnp.float32),
            pltpu.SemaphoreType.DMA((9,)),
            pltpu.SemaphoreType.DMA((2,)),
            pltpu.SemaphoreType.DMA((2,)),
            pltpu.SemaphoreType.DMA((2,)),
            pltpu.SemaphoreType.DMA((2,)),
            pltpu.VMEM((2, 2 * tokens, depth * block), low),
            pltpu.VMEM((2, 2 * tokens, 4 * LANES), low),
            pltpu.VMEM((HELD, 4, depth, block, LANES), low),
            pltpu.VMEM((total, 2, depth, block, LANES), low),
            pltpu.VMEM((total, depth, block, LANES), low),
            pltpu.VMEM((total, depth - 1, block, LANES), low),
            pltpu.VMEM((total, groups + 1, block, LANES) if groups > 1 else (1, 1, 16, LANES), low),
            pltpu.VMEM((total, block, LANES), low),
            pltpu.VMEM((5,) + small.shape, jnp.float32),
            pltpu.VMEM((3 + groups,) + small.shape, jnp.float32),
            pltpu.VMEM((depth - 1, small.shape[0], block), jnp.float32),
            pltpu.SemaphoreType.DMA((count, 2)),
            pltpu.SemaphoreType.DMA((count, 2)),
            pltpu.SemaphoreType.DMA((4, max(2 * depth, 8))),
            pltpu.SemaphoreType.DMA((total, messages)),
            pltpu.SemaphoreType.DMA((total, messages)),
            pltpu.SemaphoreType.DMA((total,)),
            pltpu.SemaphoreType.DMA((3 + groups + depth,)),
            pltpu.SemaphoreType.DMA((3 + groups + depth,)),
        ],
        compiler_params=pltpu.CompilerParams(
            collective_id=collective, has_side_effects=True, vmem_limit_bytes=62 * 1024 * 1024
        ),
    )(*extra, small, *operands)
    return results[:count], results[count], results[count + 1]


def ffn_forward(inputs, layer_gain, weight_in, weight_out):
    out_norm, normed, inverse = layer_norm(inputs, layer_gain)
    hidden = out_norm.astype(jnp.bfloat16)
    inner = product(hidden, weight_in)
    active = jax.nn.silu(inner).astype(jnp.bfloat16)
    return (product(active, weight_out), (hidden, normed, inverse, inner, active))


def ffn_backward(upstream, stored, layer_gain, weight_in, weight_out):
    hidden, normed, inverse, inner, active = stored
    branch_grad = (0.5 * upstream).astype(jnp.bfloat16)
    active_grad = product_nt(branch_grad, weight_out)
    inner_grad = (active_grad * swish_slope(inner)).astype(jnp.bfloat16)
    norm_grad, gain_grad = norm_back(product_nt(inner_grad, weight_in), layer_gain, normed, inverse)
    return (upstream + norm_grad, [(hidden, inner_grad), (active, branch_grad)], gain_grad)


def attention_scores(queries, keys_rot, key_live):
    raw_scores = jnp.einsum(
        "uqhd,ukhd->uhqk", queries, keys_rot, preferred_element_type=jnp.float32
    )
    return jnp.where(key_live[:, None, None, :], raw_scores * HEAD ** (-0.5), NEGATIVE)


def attention_forward(inputs, layer_gain, weight_in, weight_out, key_live, tables, units):
    row_count, model_width = inputs.shape
    shape_heads = (units, row_count // units, model_width // HEAD, HEAD)
    out_norm, normed, inverse = layer_norm(inputs, layer_gain)
    hidden = out_norm.astype(jnp.bfloat16)
    joined = product(hidden, weight_in)
    queries = rotate(joined[:, :model_width].reshape(shape_heads), tables[0], tables[1]).astype(
        jnp.bfloat16
    )
    keys_rot = rotate(
        joined[:, model_width : 2 * model_width].reshape(shape_heads), tables[0], tables[1]
    ).astype(jnp.bfloat16)
    values_low = joined[:, 2 * model_width :].reshape(shape_heads).astype(jnp.bfloat16)
    scores = attention_scores(queries, keys_rot, key_live)
    top_score = jnp.max(scores, axis=-1, keepdims=True)
    log_total = top_score + jnp.log(jnp.sum(jnp.exp(scores - top_score), axis=-1, keepdims=True))
    probs_low = jnp.exp(scores - log_total).astype(jnp.bfloat16)
    heads_out = jnp.einsum(
        "uhqk,ukhd->uqhd", probs_low, values_low, preferred_element_type=jnp.float32
    )
    merged = heads_out.reshape(row_count, model_width).astype(jnp.bfloat16)
    return (
        product(merged, weight_out),
        (hidden, normed, inverse, queries, keys_rot, values_low, log_total, merged),
    )


def conv_forward(inputs, layer_gain, weight_in, weight_out, small_low, live, units, share):
    row_count, model_width = inputs.shape
    frame_count = row_count // units
    out_norm, normed, inverse = layer_norm(inputs, layer_gain)
    hidden = out_norm.astype(jnp.bfloat16)
    proj = product(hidden, weight_in)
    linear_part = proj[:, :model_width]
    gate_part = jax.nn.sigmoid(proj[:, model_width:])
    glu = (linear_part * gate_part * live).reshape(units, frame_count, model_width)
    side = KER // 2
    padded = jnp.pad(glu, ((0, 0), (side, side), (0, 0)))
    kernel = small_low[1 : KER + 1].astype(jnp.float32)
    mixed = kernel[0] * padded[:, 0:frame_count]
    for offset in range(1, KER):
        mixed = mixed + kernel[offset] * padded[:, offset : offset + frame_count]
    mixed = mixed.reshape(row_count, model_width)
    local_count = jnp.sum(live)
    local_mean = jnp.sum(mixed * live, axis=0) / local_count
    local_spread = jnp.sum(jnp.square(mixed - local_mean) * live, axis=0)
    moments = jnp.stack([jnp.full((model_width,), local_count), local_mean, local_spread])
    moments = share(join_moments, jnp.pad(moments, ((0, 5), (0, 0))), 1)
    count, bmean = moments[0, 0], moments[1]
    bvar = moments[2] / count
    bn_inverse = lax.rsqrt(bvar + EPSILON)
    bn_normed = (mixed - bmean) * bn_inverse
    pre_act = small_low[KER + 1].astype(jnp.float32) * bn_normed + small_low[KER + 2].astype(
        jnp.float32
    )
    active = jax.nn.silu(pre_act).astype(jnp.bfloat16)
    stored = (
        hidden,
        normed,
        inverse,
        linear_part,
        gate_part,
        padded,
        bn_normed,
        bn_inverse,
        count,
        pre_act,
        active,
    )
    return (product(active, weight_out), stored)


def conv_backward(upstream, stored, layer_gain, weight_in, weight_out, small_low, live, units, share):
    (
        hidden,
        normed,
        inverse,
        linear_part,
        gate_part,
        padded,
        bn_normed,
        bn_inverse,
        count,
        pre_act,
        active,
    ) = stored
    row_count, model_width = upstream.shape
    frame_count = row_count // units
    kernel = small_low[1 : KER + 1].astype(jnp.float32)
    bn_scale = small_low[KER + 1].astype(jnp.float32)
    branch_grad = upstream.astype(jnp.bfloat16)
    pre_grad = product_nt(branch_grad, weight_out) * swish_slope(pre_act)
    sums = jnp.stack([jnp.sum(pre_grad, axis=0), jnp.sum(pre_grad * bn_normed, axis=0)])
    sums = share(add_pair, jnp.pad(sums, ((0, 6), (0, 0))), 2)
    shift_total, scale_total = sums[0], sums[1]
    mixed_grad = bn_inverse * (
        bn_scale * pre_grad
        - live * (bn_scale * shift_total) / count
        - live * bn_normed * (bn_scale * scale_total) / count
    )
    side = KER // 2
    grid_grad = mixed_grad.reshape(units, frame_count, model_width)
    grad_padded = jnp.pad(grid_grad, ((0, 0), (side, side), (0, 0)))
    last_tap = KER - 1
    glu_grad = kernel[0] * grad_padded[:, last_tap : last_tap + frame_count]
    for offset in range(1, KER):
        glu_grad = (
            glu_grad
            + kernel[offset] * grad_padded[:, last_tap - offset : last_tap - offset + frame_count]
        )
    kernel_grad = jnp.stack(
        [
            jnp.sum(padded[:, offset : offset + frame_count] * grid_grad, axis=(0, 1))
            for offset in range(KER)
        ]
    )
    glu_grad = glu_grad.reshape(row_count, model_width) * live
    proj_grad = jnp.concatenate(
        [glu_grad * gate_part, glu_grad * linear_part * gate_part * (1.0 - gate_part)], axis=1
    ).astype(jnp.bfloat16)
    norm_grad, gain_grad = norm_back(product_nt(proj_grad, weight_in), layer_gain, normed, inverse)
    return (
        upstream + norm_grad,
        [(hidden, proj_grad), (active, branch_grad)],
        gain_grad,
        kernel_grad,
        jnp.stack([scale_total, shift_total]),
    )


def local(
    depth_devices,
    groups,
    tokens,
    lengths,
    span_starts,
    mask_embed,
    norm_gains,
    ffn1_in,
    ffn1_out,
    attn_in,
    attn_out,
    conv_in,
    conv_out,
    depth,
    bn_affine,
    ffn2_in,
    ffn2_out,
    cotangent,
):
    units, frame_count, model_width = tokens.shape
    row_count = units * frame_count
    position = jnp.arange(frame_count, dtype=jnp.int32)
    valid = position[None, :] < lengths[:, None]
    inside = (position[None, None, :] >= span_starts[:, :, None]) & (
        position[None, None, :] < span_starts[:, :, None] + SPAN_LEN
    )
    masked = jnp.any(inside, axis=1) & valid
    live = valid.reshape(row_count, 1).astype(jnp.float32)
    masked_col = masked.reshape(row_count, 1)
    tables = rotation(frame_count)
    small = jnp.concatenate([norm_gains, mask_embed[None, :], depth, bn_affine], axis=0)
    small = jnp.pad(small, ((0, 16 - small.shape[0]), (0, 0)))
    gathered = gather_all(
        depth_devices,
        [ffn1_in, ffn1_out, attn_in, attn_out, conv_in, conv_out, ffn2_in, ffn2_out],
        small,
    )
    small_all = gathered[8].transpose(1, 0, 2).reshape(16, model_width)
    third_small = jnp.concatenate([small_all[2:3], small_all[6:13]], axis=0)
    first_weights = (gathered[0], gathered[1], small_all[jnp.array([0, 5])])
    second_weights = (gathered[2], gathered[3], small_all[1:2])
    third_weights = (gathered[4], gathered[5], third_small)
    fourth_weights = (gathered[6], gathered[7], small_all[3:5])
    gain_one = first_weights[2][0].astype(jnp.float32)
    embed = first_weights[2][1].astype(jnp.float32)
    start = jnp.where(masked_col, embed, tokens.reshape(row_count, model_width).astype(jnp.float32))
    branch, first_stored = ffn_forward(start, gain_one, first_weights[0], first_weights[1])
    first = start + 0.5 * branch
    gain_two = second_weights[2][0].astype(jnp.float32)
    branch, second_stored = attention_forward(
        first, gain_two, second_weights[0], second_weights[1], valid, tables, units
    )
    second = first + branch
    gain_three = third_weights[2][0].astype(jnp.float32)
    share = functools.partial(exchange, depth_devices, groups)
    branch, third_stored = conv_forward(
        second, gain_three, third_weights[0], third_weights[1], third_weights[2], live, units, share
    )
    third = second + branch
    gain_four = fourth_weights[2][0].astype(jnp.float32)
    gain_five = fourth_weights[2][1].astype(jnp.float32)
    branch, fourth_stored = ffn_forward(third, gain_four, fourth_weights[0], fourth_weights[1])
    fourth = third + 0.5 * branch
    out_norm, final_normed, final_inverse = layer_norm(fourth, gain_five)
    output = out_norm.astype(jnp.bfloat16).reshape(units, frame_count, model_width)
    upstream = cotangent.reshape(row_count, model_width).astype(jnp.float32)
    grad_four, gain_five_grad = norm_back(upstream, gain_five, final_normed, final_inverse)
    grad_three, fourth_pairs, gain_four_grad = ffn_backward(
        grad_four, fourth_stored, gain_four, fourth_weights[0], fourth_weights[1]
    )
    grad_two, third_pairs, gain_three_grad, kernel_grad, affine_full = conv_backward(
        grad_three,
        third_stored,
        gain_three,
        third_weights[0],
        third_weights[1],
        third_weights[2],
        live,
        units,
        share,
    )
    hidden_one, _, _, inner_one, active_one = first_stored
    hidden_two, _, _, queries, keys_rot, values_low, log_total, merged = second_stored
    zero_row = jnp.zeros((1, model_width), jnp.float32)
    small_grads = jnp.concatenate(
        [
            zero_row,
            zero_row,
            gain_three_grad[None, :],
            gain_four_grad[None, :],
            gain_five_grad[None, :],
            zero_row,
            kernel_grad,
            jnp.zeros((5, model_width), jnp.float32),
        ],
        axis=0,
    )
    branch_grad = grad_two.astype(jnp.bfloat16)
    flat = (row_count, model_width)
    cosine, sine = tables[0][:, 0], tables[1][:, 0]
    extra = [
        grad_two,
        branch_grad,
        queries.reshape(flat),
        keys_rot.reshape(flat),
        values_low.reshape(flat),
        second_weights[0],
        second_weights[1],
        first_weights[0],
        first_weights[1],
        inner_one,
        first,
        start,
        log_total.reshape(model_width // HEAD, 1, row_count),
        live,
        masked_col.astype(jnp.float32),
        jnp.concatenate([cosine, cosine], axis=1),
        jnp.concatenate([sine, -sine], axis=1),
        small_all[0:8].astype(jnp.float32),
    ]
    pairs = fourth_pairs + third_pairs
    pairs += [(merged, branch_grad), (hidden_two, attn_in.shape[1])]
    pairs += [(active_one, model_width), (hidden_one, ffn1_in.shape[1])]
    reduced, small_sum, input_grad = reduce_all(
        depth_devices, groups, pairs, extra, small_grads, 3
    )
    input_grad = input_grad.reshape(units, frame_count, model_width)
    ffn2_in_grad, ffn2_out_grad, conv_in_grad, conv_out_grad = (
        array.astype(jnp.float32) for array in reduced[:4]
    )
    attn_out_grad, attn_in_grad, ffn1_out_grad, ffn1_in_grad = (
        array.astype(jnp.float32) for array in reduced[4:]
    )
    column_width = norm_gains.shape[1]
    affine_grad = lax.dynamic_slice_in_dim(
        affine_full, lax.axis_index("fsdp") * column_width, column_width, 1
    )
    return (
        output,
        input_grad,
        small_sum[5],
        small_sum[0:5],
        ffn1_in_grad,
        ffn1_out_grad,
        attn_in_grad,
        attn_out_grad,
        conv_in_grad,
        conv_out_grad,
        small_sum[6 : 6 + KER],
        affine_grad,
        ffn2_in_grad,
        ffn2_out_grad,
    )


def solution(mesh):
    in_specs = (
        P(("dp", "fsdp"), None, None),
        P(("dp", "fsdp")),
        P(("dp", "fsdp"), None),
        P("fsdp"),
        P(None, "fsdp"),
        P("fsdp", None),
        P("fsdp", None),
        P("fsdp", None),
        P("fsdp", None),
        P("fsdp", None),
        P("fsdp", None),
        P(None, "fsdp"),
        P(None, "fsdp"),
        P("fsdp", None),
        P("fsdp", None),
        P(("dp", "fsdp"), None, None),
    )
    out_specs = (
        P(("dp", "fsdp"), None, None),
        P(("dp", "fsdp"), None, None),
        P("fsdp"),
        P(None, "fsdp"),
        P("fsdp", None),
        P("fsdp", None),
        P("fsdp", None),
        P("fsdp", None),
        P("fsdp", None),
        P("fsdp", None),
        P(None, "fsdp"),
        P(None, "fsdp"),
        P("fsdp", None),
        P("fsdp", None),
    )
    body = functools.partial(local, mesh.shape["fsdp"], mesh.shape["dp"] // WAYS)
    return jax.shard_map(body, mesh=mesh, in_specs=in_specs, out_specs=out_specs, check_vma=False)
```

```python
import functools

import jax
import jax.numpy as jnp
from jax import lax
from jax.experimental import pallas as pl
from jax.experimental.pallas import tpu as pltpu
from jax.sharding import PartitionSpec as P

HEAD = 128
KER = 5
SPAN_LEN = 10


EPSILON = 1e-05
NEGATIVE = -1000000000.0


def product(left_side, right_side):
    return jnp.dot(left_side, right_side, preferred_element_type=jnp.float32)


def product_nt(left_side, right_side):
    return lax.dot_general(
        left_side, right_side, (((1,), (1,)), ((), ())), preferred_element_type=jnp.float32
    )


def layer_norm(inputs, layer_gain):
    average = jnp.mean(inputs, axis=-1, keepdims=True)
    centered = inputs - average
    inverse = lax.rsqrt(jnp.mean(centered * centered, axis=-1, keepdims=True) + EPSILON)
    normed = centered * inverse
    return (normed * layer_gain, normed, inverse)


def norm_back(upstream, layer_gain, normed, inverse):
    scaled = upstream * layer_gain
    first_mean = jnp.mean(scaled, axis=-1, keepdims=True)
    second_mean = jnp.mean(scaled * normed, axis=-1, keepdims=True)
    return (
        inverse * (scaled - first_mean - normed * second_mean),
        jnp.sum(upstream * normed, axis=0),
    )


def swish_slope(inputs):
    sigmoid_part = jax.nn.sigmoid(inputs)
    return sigmoid_part * (1.0 + inputs * (1.0 - sigmoid_part))


def rotation(frame_count):
    half_size = HEAD // 2
    position = jnp.arange(frame_count, dtype=jnp.float32)
    frequency = 10000.0 ** (-jnp.arange(half_size, dtype=jnp.float32) / half_size)
    angles = position[:, None] * frequency[None, :]
    return (jnp.cos(angles)[:, None, :], jnp.sin(angles)[:, None, :])


MESH = pl.DeviceIdType.MESH
WAYS = 8


def coordinates():
    dp = lax.axis_index("dp")
    z = lax.axis_index("fsdp")
    core_bit = lax.rem(dp, 2)
    x_bit = lax.rem(dp // 2, 2)
    y_bit = lax.rem(dp // 4, 2)
    return dp, z, core_bit, x_bit, y_bit


def signal(sem, device):
    pl.semaphore_signal(sem, inc=1, device_id=device, device_id_type=MESH)


def greet(depth, dp, z, flat_peers):
    barrier = pltpu.get_barrier_semaphore()
    signal(barrier, (dp, lax.rem(z + 1, depth)))
    signal(barrier, (dp, lax.rem(z + depth - 1, depth)))
    for peer in flat_peers:
        signal(barrier, (peer, z))
    pl.semaphore_wait(barrier, 2 + len(flat_peers))


TILE = 512
ROWS = 256
ALONG_LINE = ()
GATHER_LAGS = (2, 4, 6)
GATHER_LEAD = 3
PER_TURN = 3


def column_tile(index):
    return pl.ds(index * TILE, TILE)


def row_blocks(rows, body):
    def step(block):
        body(pl.ds(pl.multiple_of(block * ROWS, ROWS), ROWS))

    pl.loop(0, rows // ROWS)(step)


def nt(left_side, right_side):
    return lax.dot_general(
        left_side, right_side, (((1,), (1,)), ((), ())), preferred_element_type=jnp.float32
    )


def forward_units(inputs, weights, results, scratch, small_full):
    tokens, masked, live, cosine, sine = inputs
    ffn_in_w, ffn_out_w, attn_in_w, attn_out_w = weights
    (
        start_out,
        hidden_one_out,
        inner_out,
        active_out,
        first_out,
        hidden_two_out,
        queries_out,
        keys_out,
        values_out,
        log_out,
        merged_out,
        second_out,
    ) = results
    (
        resid,
        total,
        hidden,
        active,
        heads,
        merged,
        row_tiles,
        column_tiles,
        inner_tiles,
        gains,
        sems,
        row_sems,
        column_sems,
        inner_sems,
    ) = scratch
    frames, width = resid.shape
    ff_tiles = active.shape[1] // TILE
    head_tiles = width // TILE

    def row_copy(source):
        return lambda at: pltpu.make_async_copy(
            source.at[pl.ds(at * TILE, TILE)], row_tiles.at[at % 2], row_sems.at[at % 2]
        )

    def column_copy(source):
        return lambda at: pltpu.make_async_copy(
            source.at[:, column_tile(at)], column_tiles.at[at % 2], column_sems.at[at % 2]
        )

    def stream(copy_of, low_tile, high_tile, count, body):
        if low_tile == 0:
            for at in range(min(2, count)):
                copy_of(at).start()
        for at in range(low_tile, high_tile):
            copy_of(at).wait()
            body(at)
            if at + 2 < count:
                copy_of(at + 2).start()

    def put(source, target, index):
        return pltpu.make_async_copy(source, target, sems.at[index])

    start_put = put(resid, start_out, 0)
    hidden_one_put = put(hidden, hidden_one_out, 1)
    active_put = put(active, active_out, 2)
    first_put = put(resid, first_out, 3)
    hidden_two_put = put(hidden, hidden_two_out, 4)
    head_puts = [
        put(heads.at[part], target, 5 + part)
        for part, target in enumerate((queries_out, keys_out, values_out))
    ]
    merged_put = put(merged, merged_out, 8)
    second_put = put(total, second_out, 9)

    def normed(value, gain):
        centered = value - jnp.mean(value, axis=-1, keepdims=True)
        inverse = lax.rsqrt(jnp.mean(centered * centered, axis=-1, keepdims=True) + EPSILON)
        return (centered * inverse * gain).astype(jnp.bfloat16)

    def prepare():
        depth, _, piece = small_full.shape
        for owner in range(depth):
            gains[:, owner * piece : (owner + 1) * piece] = small_full[owner].astype(jnp.float32)
        gain, embed = gains[0:1], gains[5:6]

        def body(rows):
            value = jnp.where(masked[rows] > 0.0, embed, tokens[rows].astype(jnp.float32))
            resid[rows] = value
            hidden[rows] = normed(value, gain)

        row_blocks(frames, body)
        start_put.start()
        hidden_one_put.start()

    def inner_put(at):
        return pltpu.make_async_copy(
            inner_tiles.at[at % 2], inner_out.at[:, column_tile(at)], inner_sems.at[at % 2]
        )

    def widen(low_tile, high_tile):
        def unit():
            def body(at):
                if at >= 2:
                    inner_put(at - 2).wait()

                def step(rows):
                    inner = product(hidden[rows], column_tiles[at % 2])
                    inner_tiles[at % 2, rows] = inner
                    active[rows, column_tile(at)] = (inner * jax.nn.sigmoid(inner)).astype(
                        jnp.bfloat16
                    )

                row_blocks(frames, step)
                inner_put(at).start()

            stream(column_copy(ffn_in_w), low_tile, high_tile, ff_tiles, body)
            if high_tile == ff_tiles:
                active_put.start()
                for at in range(ff_tiles - 2, ff_tiles):
                    inner_put(at).wait()

        return unit

    def narrow(low_tile, high_tile):
        def unit():
            def body(at):
                def step(rows):
                    part = product(active[rows, column_tile(at)], row_tiles[at % 2])
                    total[rows] = part if at == 0 else total[rows] + part

                row_blocks(frames, step)

            stream(row_copy(ffn_out_w), low_tile, high_tile, ff_tiles, body)

        return unit

    def first_done():
        start_put.wait()
        hidden_one_put.wait()
        active_put.wait()
        gain = gains[1:2]

        def body(rows):
            value = resid[rows] + 0.5 * total[rows]
            resid[rows] = value
            hidden[rows] = normed(value, gain)

        row_blocks(frames, body)
        first_put.start()
        hidden_two_put.start()

    def split_heads(low_tile, high_tile):
        def unit():
            def body(at):
                part = at // head_tiles

                def step(rows):
                    value = product(hidden[rows], column_tiles[at % 2])
                    for head in range(TILE // HEAD):
                        piece = value[:, head * HEAD : (head + 1) * HEAD]
                        if part < 2:
                            piece = piece * cosine[rows] + pltpu.roll(piece, HEAD // 2, 1) * sine[rows]
                        first = (at % head_tiles) * TILE + head * HEAD
                        heads[part, rows, pl.ds(first, HEAD)] = piece.astype(jnp.bfloat16)

                row_blocks(frames, step)

            stream(column_copy(attn_in_w), low_tile, high_tile, 3 * head_tiles, body)
            if high_tile == 3 * head_tiles:
                for copy in head_puts:
                    copy.start()

        return unit

    def head_step(head):
        columns = pl.ds(pl.multiple_of(head * HEAD, HEAD), HEAD)
        query, key, value = heads[0, :, columns], heads[1, :, columns], heads[2, :, columns]
        scores = jnp.where(live[...] > 0.0, nt(key, query) * HEAD ** (-0.5), NEGATIVE)
        top_score = jnp.max(scores, axis=0, keepdims=True)
        raised = jnp.exp(scores - top_score)
        amount = jnp.sum(raised, axis=0, keepdims=True)
        log_out[head] = top_score + jnp.log(amount)
        probs = (raised * (1.0 / amount)).astype(jnp.bfloat16)
        merged[:, columns] = lax.dot_general(
            probs, value, (((0,), (0,)), ((), ())), preferred_element_type=jnp.float32
        ).astype(jnp.bfloat16)

    def some_heads(low_head, high_head):
        def unit():
            pl.loop(low_head, high_head)(head_step)

        return unit

    def attention_done():
        merged_put.start()

        def body(at):
            def step(rows):
                part = product(merged[rows, column_tile(at)], row_tiles[at % 2])
                total[rows] = (resid[rows] if at == 0 else total[rows]) + part

            row_blocks(frames, step)

        stream(row_copy(attn_out_w), 0, head_tiles, head_tiles, body)
        second_put.start()

    def finish():
        for copy in [first_put, hidden_two_put, merged_put, second_put] + head_puts:
            copy.wait()

    units = [(None, prepare)]
    for at in range(0, ff_tiles, 2):
        units.append((0, widen(at, at + 2)))
    for at in range(0, ff_tiles, 4):
        units.append((1, narrow(at, at + 4)))
    units.append((1, first_done))
    for at in range(0, 3 * head_tiles, 3):
        units.append((2, split_heads(at, at + 3)))
    for at in range(0, width // HEAD, 2):
        units.append((2, some_heads(at, at + 2)))
    units.append((3, attention_done))
    return units, finish


FORWARD_INPUTS = 5
FORWARD_RESULTS = 12
FORWARD_SCRATCH = 14


def gather_kernel(depth, count, chunks, lead, *refs):
    extra, refs = refs[:FORWARD_INPUTS], refs[FORWARD_INPUTS:]
    shards, small = refs[:count], refs[count]
    fulls, small_full = refs[count + 1 : 2 * count + 1], refs[2 * count + 1]
    refs = refs[2 * count + 2 :]
    results, refs = refs[:FORWARD_RESULTS], refs[FORWARD_RESULTS:]
    unit_scratch, refs = refs[:FORWARD_SCRATCH], refs[FORWARD_SCRATCH:]
    send_sems, recv_sems, own_sems, small_sems = refs
    dp, z, core_bit, x_bit, y_bit = coordinates()
    mine = lax.rem(dp, WAYS)
    step_c, step_x, step_y = 1 - 2 * core_bit, 2 - 4 * x_bit, 4 - 8 * y_bit
    peer_c, peer_x, peer_y = dp + step_c, dp + step_x, dp + step_y
    greet(depth, dp, z, (peer_c, peer_x, peer_y))

    def remote(source, target, send_sem, recv_sem, device):
        return pltpu.make_async_remote_copy(
            source, target, send_sem, recv_sem, device_id=device, device_id_type=MESH
        )

    def slot(chunk, owner, piece, half):
        index, first, width = chunks[chunk]
        rows = shards[index].shape[0]
        part = rows // WAYS
        if index in ALONG_LINE:
            part = rows // 2
        if half is not None:
            width = width // 2
            first = first + half * width
        start = pl.multiple_of(owner * rows + piece * part, part)
        return fulls[index].at[pl.ds(start, part), pl.ds(first, width)]

    def place(chunk, index, message, owner, piece, device, half=None):
        where = slot(chunk, owner, piece, half)
        return remote(
            where,
            where,
            send_sems.at[chunk, index, message],
            recv_sems.at[chunk, index, message],
            device,
        )

    def each(action):
        for hop in range(depth - 1):

            @pl.when(z - 1 - hop >= 0)
            def _():
                action(2 * hop, z - 1 - hop, hop, 1)

            @pl.when(z + 1 + hop < depth)
            def _():
                action(2 * hop + 1, z + 1 + hop, hop, -1)

    here = (dp, z)
    core_dev, x_dev, y_dev = (peer_c, z), (peer_x, z), (peer_y, z)
    piece_x, piece_y, piece_xy = mine + step_x, mine + step_y, mine + step_x + step_y
    other = mine + step_c
    other_x, other_y, other_xy = other + step_x, other + step_y, other + step_x + step_y

    small_local = pltpu.make_async_copy(small, small_full.at[z], own_sems.at[count, 0])
    small_local.start()

    def small_out(index, source, owner, device):
        return remote(
            source, small_full.at[owner], small_sems.at[index, 0], small_sems.at[index, 1], device
        )

    @pl.when(z + 1 < depth)
    def _():
        small_out(0, small, z, (dp, z + 1)).start()

    @pl.when(z > 0)
    def _():
        small_out(1, small, z, (dp, z - 1)).start()

    def line_start(chunk):
        index, first, width = chunks[chunk]
        whole_line = index in ALONG_LINE
        part = shards[index].shape[0] // (2 if whole_line else WAYS)
        piece = core_bit if whole_line else mine
        source = shards[index].at[
            pl.ds(pl.multiple_of(piece * part, part), part), pl.ds(first, width)
        ]
        target = slot(chunk, z, piece, None)

        @pl.when(z + 1 < depth)
        def _():
            remote(
                source, target, send_sems.at[chunk, 0, 0], recv_sems.at[chunk, 0, 0], (dp, z + 1)
            ).start()

        @pl.when(z > 0)
        def _():
            remote(
                source, target, send_sems.at[chunk, 1, 0], recv_sems.at[chunk, 1, 0], (dp, z - 1)
            ).start()

    def along_line(chunk):
        return chunks[chunk][0] in ALONG_LINE

    def line_arrived(chunk):
        piece = core_bit if along_line(chunk) else mine

        def action(index, owner, hop, way):
            place(chunk, index, 0, owner, piece, here).wait_recv()
            if hop < depth - 2:
                following = z + way

                @pl.when((following >= 0) & (following < depth))
                def _():
                    place(chunk, index + 2, 0, owner, piece, (dp, following)).start()

            if along_line(chunk):
                place(chunk, index, 5, owner, piece, core_dev).start()
                return
            place(chunk, index, 1, owner, mine, x_dev).start()
            place(chunk, index, 2, owner, mine, y_dev).start()
            place(chunk, index, 5, owner, mine, core_dev).start()

        each(action)

    def plane_arrived(chunk):
        def action(index, owner, hop, way):
            place(chunk, index, 1, owner, piece_x, here).wait_recv()
            place(chunk, index, 3, owner, piece_x, y_dev, 0).start()
            place(chunk, index, 6, owner, piece_x, core_dev).start()
            place(chunk, index, 2, owner, piece_y, here).wait_recv()
            place(chunk, index, 4, owner, piece_y, x_dev, 1).start()
            place(chunk, index, 7, owner, piece_y, core_dev).start()

        each(action)

    def corner_arrived(chunk):
        def action(index, owner, hop, way):
            for half in range(2):
                place(chunk, index, 3 + half, owner, piece_xy, here, half).wait_recv()
                place(chunk, index, 8 + half, owner, piece_xy, core_dev, half).start()

        each(action)

    def core_arrived(chunk):
        def action(index, owner, hop, way):
            if along_line(chunk):
                place(chunk, index, 5, owner, 1 - core_bit, here).wait_recv()
                return
            place(chunk, index, 5, owner, other, here).wait_recv()
            place(chunk, index, 6, owner, other_x, here).wait_recv()
            place(chunk, index, 7, owner, other_y, here).wait_recv()
            for half in range(2):
                place(chunk, index, 8 + half, owner, other_xy, here, half).wait_recv()

        each(action)

    def small_action(index, owner, hop, way):
        small_out(index, small, owner, here).wait_recv()
        if hop < depth - 2:
            following = z + way

            @pl.when((following >= 0) & (following < depth))
            def _():
                small_out(index + 2, small_full.at[owner], owner, (dp, following)).start()

    total = len(chunks)
    for chunk in range(min(lead, total)):
        line_start(chunk)
    own_copies = []
    for index in range(count):
        rows = shards[index].shape[0]
        target = fulls[index].at[pl.ds(pl.multiple_of(z * rows, rows), rows)]
        copy = remote(
            shards[index], target, own_sems.at[index, 0], own_sems.at[index, 1], core_dev
        )
        copy.start()
        own_copies.append(copy)
    last_chunk = {index: chunk for chunk, (index, _, _) in enumerate(chunks)}
    seen = set()
    units, finish = forward_units(extra, fulls[:4], results, unit_scratch, small_full)
    plane_lag, corner_lag, core_lag = GATHER_LAGS
    for turn in range(total + core_lag):
        if turn + lead < total:
            line_start(turn + lead)
        if turn < total:
            line_arrived(turn)
        if turn == 0:
            each(small_action)
            small_local.wait()
        if 0 <= turn - plane_lag < total and not along_line(turn - plane_lag):
            plane_arrived(turn - plane_lag)
        if 0 <= turn - corner_lag < total and not along_line(turn - corner_lag):
            corner_arrived(turn - corner_lag)
        if 0 <= turn - core_lag < total:
            core_arrived(turn - core_lag)
        for _ in range(PER_TURN):
            if units and (units[0][0] is None or last_chunk[units[0][0]] <= turn - core_lag):
                needed, unit = units.pop(0)
                if needed is not None and needed not in seen:
                    seen.add(needed)
                    own_copies[needed].wait_recv()
                unit()
    assert not units
    finish()
    for index, copy in enumerate(own_copies):
        if index not in seen:
            copy.wait_recv()
        copy.wait_send()

    @pl.when(z + 1 < depth)
    def _():
        small_out(0, small, z, here).wait_send()

    @pl.when(z > 0)
    def _():
        small_out(1, small, z, here).wait_send()

    def small_drain(index, owner, hop, way):
        if hop < depth - 2:
            following = z + way

            @pl.when((following >= 0) & (following < depth))
            def _():
                small_out(index + 2, small, owner, here).wait_send()

    each(small_drain)
    for chunk in range(total):
        piece = core_bit if along_line(chunk) else mine

        @pl.when(z + 1 < depth)
        def _():
            place(chunk, 0, 0, z, piece, here).wait_send()

        @pl.when(z > 0)
        def _():
            place(chunk, 1, 0, z, piece, here).wait_send()

        def drain(index, owner, hop, way):
            if hop < depth - 2:
                following = z + way

                @pl.when((following >= 0) & (following < depth))
                def _():
                    place(chunk, index + 2, 0, owner, piece, here).wait_send()

            if along_line(chunk):
                place(chunk, index, 5, owner, piece, here).wait_send()
                return
            for message in (1, 2, 5, 6, 7):
                place(chunk, index, message, owner, mine, here).wait_send()
            for message in (3, 4, 8, 9):
                place(chunk, index, message, owner, mine, here, 0).wait_send()

        each(drain)


def gather_all(depth, weights, splits, small, tokens, masked, live, tables):
    count = len(weights)
    chunks = []
    for index, weight in enumerate(weights):
        width = weight.shape[1] // splits[index]
        chunks += [(index, part * width, width) for part in range(splits[index])]
    shape = (len(chunks), 2 * (depth - 1), 10)
    frames, width = tokens.shape
    wide = weights[0].shape[1]
    heads = width // HEAD
    low, full = jnp.bfloat16, jnp.float32

    def array(shape, dtype):
        return jax.ShapeDtypeStruct(shape, dtype)

    outs = [array((weight.shape[0] * depth, weight.shape[1]), low) for weight in weights]
    outs.append(array((depth,) + small.shape, small.dtype))
    square = (frames, width)
    outs += [
        array(square, full),
        array(square, low),
        array((frames, wide), full),
        array((frames, wide), low),
        array(square, full),
        array(square, low),
        array(square, low),
        array(square, low),
        array(square, low),
        array((heads, 1, frames), full),
        array(square, low),
        array(square, full),
    ]
    any_spec = pl.BlockSpec(memory_space=pl.ANY)
    vmem_spec = pl.BlockSpec(memory_space=pltpu.VMEM)
    return pl.pallas_call(
        functools.partial(gather_kernel, depth, count, chunks, GATHER_LEAD),
        out_shape=outs,
        in_specs=[vmem_spec] * FORWARD_INPUTS + [any_spec] * (count + 1),
        out_specs=[any_spec] * count
        + [vmem_spec]
        + [any_spec] * 9
        + [vmem_spec]
        + [any_spec] * 2,
        scratch_shapes=[
            pltpu.VMEM(square, full),
            pltpu.VMEM(square, full),
            pltpu.VMEM(square, low),
            pltpu.VMEM((frames, wide), low),
            pltpu.VMEM((3,) + square, low),
            pltpu.VMEM(square, low),
            pltpu.VMEM((2, TILE, width), low),
            pltpu.VMEM((2, width, TILE), low),
            pltpu.VMEM((2, frames, TILE), full),
            pltpu.VMEM((small.shape[0], width), full),
            pltpu.SemaphoreType.DMA((10,)),
            pltpu.SemaphoreType.DMA((2,)),
            pltpu.SemaphoreType.DMA((2,)),
            pltpu.SemaphoreType.DMA((2,)),
            pltpu.SemaphoreType.DMA(shape),
            pltpu.SemaphoreType.DMA(shape),
            pltpu.SemaphoreType.DMA((count + 1, 2)),
            pltpu.SemaphoreType.DMA((2 * (depth - 1), 2)),
        ],
        compiler_params=pltpu.CompilerParams(
            collective_id=0, has_side_effects=True, vmem_limit_bytes=58 * 1024 * 1024
        ),
    )(tokens, masked, live, *tables, *weights, small)


def add_pair(left, right):
    return left + right


def join_moments(left, right):
    count = left[0:1] + right[0:1]
    mean = (left[0:1] * left[1:2] + right[0:1] * right[1:2]) / count
    gap = right[1:2] - left[1:2]
    spread = left[2:3] + right[2:3] + gap * gap * (left[0:1] * right[0:1] / count)
    return jnp.concatenate([count, mean, spread, left[3:]], axis=0)


def exchange_kernel(depth, groups, combine, value, result, work, inbox, line, send_sems, recv_sems):
    dp, z, core_bit, x_bit, y_bit = coordinates()
    peers = [dp + 1 - 2 * core_bit, dp + 2 - 4 * x_bit, dp + 4 - 8 * y_bit]
    group = dp // WAYS
    barrier = pltpu.get_barrier_semaphore()
    far = [lax.rem(group + step, groups) * WAYS + lax.rem(dp, WAYS) for step in range(1, groups)]
    for peer in peers + far:
        signal(barrier, (peer, z))
    for step in range(1, depth):
        signal(barrier, (dp, lax.rem(z + step, depth)))
    pl.semaphore_wait(barrier, len(peers) + len(far) + depth - 1)
    work[0] = value[...]
    for turn, peer in enumerate(peers):
        copy = pltpu.make_async_remote_copy(
            work.at[turn],
            inbox.at[turn],
            send_sems.at[turn],
            recv_sems.at[turn],
            device_id=(peer, z),
            device_id_type=MESH,
        )
        copy.start()
        copy.wait()
        work[turn + 1] = combine(work[turn], inbox[turn])

    def spread(source, slots, first, targets, own):
        copies = []
        for step, target in enumerate(targets):
            copy = pltpu.make_async_remote_copy(
                source,
                slots.at[own],
                send_sems.at[first + step],
                recv_sems.at[first + step],
                device_id=target,
                device_id_type=MESH,
            )
            copy.start()
            copies.append(copy)
        local = pltpu.make_async_copy(source, slots.at[own], send_sems.at[first + len(targets)])
        local.start()
        for copy in copies:
            copy.wait()
        local.wait()

    last = len(peers)
    if groups > 1:
        spread(work.at[last], inbox.at[pl.ds(last, groups)], last, [(peer, z) for peer in far], group)
        total = inbox[last]
        for step in range(1, groups):
            total = combine(total, inbox[last + step])
        work[last] = total
    first = last + groups
    spread(
        work.at[last],
        line,
        first,
        [(dp, lax.rem(z + step, depth)) for step in range(1, depth)],
        z,
    )
    total = line[0]
    for step in range(1, depth):
        total = combine(total, line[step])
    result[...] = total


def exchange(depth, groups, combine, value, collective):
    shape = value.shape
    sems = 3 + groups + depth
    return pl.pallas_call(
        functools.partial(exchange_kernel, depth, groups, combine),
        out_shape=jax.ShapeDtypeStruct(shape, value.dtype),
        in_specs=[pl.BlockSpec(memory_space=pltpu.VMEM)],
        out_specs=pl.BlockSpec(memory_space=pltpu.VMEM),
        scratch_shapes=[
            pltpu.VMEM((4,) + shape, value.dtype),
            pltpu.VMEM((3 + groups,) + shape, value.dtype),
            pltpu.VMEM((depth,) + shape, value.dtype),
            pltpu.SemaphoreType.DMA((sems,)),
            pltpu.SemaphoreType.DMA((sems,)),
        ],
        compiler_params=pltpu.CompilerParams(collective_id=collective, has_side_effects=True),
    )(value)


LANES = 128
HELD = 3
LINE_FIRST = ()
PLANE_LAGS = (2, 5, 8, 11, 14, 16)
LINE_LAGS = (5, 6, 7, 8, 9, 10)


def backward_units(inputs, made, results, scratch, small_first, pair_start):
    (
        grad_in,
        branch_in,
        queries_in,
        keys_in,
        values_in,
        attn_in_w,
        attn_out_w,
        ffn_in_w,
        ffn_out_w,
        inner_in,
        first_in,
        start_in,
        log_total,
        live,
        masked,
        cosine,
        sine,
        gains,
        small,
    ) = inputs
    joined_out, fresh_out, inner_out = made
    (input_grad,) = results
    (
        heads,
        joined,
        row_tiles,
        column_tiles,
        inner_tiles,
        grad,
        resid,
        total,
        gain_rows,
        sems,
        row_sems,
        column_sems,
        inner_sems,
        put_sems,
    ) = scratch
    frames, width = grad.shape
    ff_tiles = inner_in.shape[1] // TILE
    joined_tiles = joined_out.shape[1] // TILE
    row_plan = [(attn_out_w, index) for index in range(width // TILE)]
    row_plan += [(ffn_out_w, index) for index in range(ff_tiles)]
    column_plan = [(attn_in_w, index) for index in range(joined_tiles)]
    column_plan += [(ffn_in_w, index) for index in range(ff_tiles)]

    def row_copy(at):
        source, index = row_plan[at]
        return pltpu.make_async_copy(
            source.at[pl.ds(index * TILE, TILE)], row_tiles.at[at % 2], row_sems.at[at % 2]
        )

    def column_copy(at):
        source, index = column_plan[at]
        return pltpu.make_async_copy(
            source.at[:, column_tile(index)], column_tiles.at[at % 2], column_sems.at[at % 2]
        )

    def inner_copy(at):
        return pltpu.make_async_copy(
            inner_in.at[:, column_tile(at)], inner_tiles.at[at % 2], inner_sems.at[at % 2]
        )

    first_loads = [
        pltpu.make_async_copy(source, target, sems.at[index])
        for index, (source, target) in enumerate(
            (
                (branch_in, joined.at[:, pl.ds(0, width)]),
                (queries_in, heads.at[0]),
                (keys_in, heads.at[1]),
                (values_in, heads.at[2]),
                (grad_in, grad),
                (first_in, resid),
            )
        )
    ]

    def start_loads():
        for copy in first_loads[:1]:
            copy.start()
        for at in range(2):
            row_copy(at).start()
        for copy in first_loads[1:]:
            copy.start()
        for at in range(2):
            column_copy(at).start()
            inner_copy(at).start()

    def merged_grad():
        first_loads[0].wait()
        for at in range(width // TILE):
            row_copy(at).wait()

            def body(rows, at=at):
                heads[3, rows, column_tile(at)] = nt(
                    joined[rows, pl.ds(0, width)], row_tiles[at % 2]
                ).astype(jnp.bfloat16)

            row_blocks(frames, body)
            row_copy(at + 2).start()
        for copy in first_loads[1:4]:
            copy.wait()

    def turned(gradient):
        return gradient * cosine[...] + pltpu.roll(gradient, HEAD // 2, 1) * sine[...]

    def head_step(head):
        columns = pl.ds(pl.multiple_of(head * HEAD, HEAD), HEAD)
        query, key, value = heads[0, :, columns], heads[1, :, columns], heads[2, :, columns]
        upstream = heads[3, :, columns]
        scale = HEAD ** (-0.5)
        scores = jnp.where(live[...] > 0.0, nt(key, query) * scale, NEGATIVE)
        probs = jnp.exp(scores - log_total[head])
        value_grad = product(probs.astype(jnp.bfloat16), upstream)
        prob_grad = nt(value, upstream)
        row_term = jnp.sum(probs * prob_grad, axis=0, keepdims=True)
        score_grad = (probs * (prob_grad - row_term) * scale).astype(jnp.bfloat16)
        key_grad = turned(product(score_grad, query))
        query_grad = turned(
            lax.dot_general(
                score_grad, key, (((0,), (0,)), ((), ())), preferred_element_type=jnp.float32
            )
        )
        for part, value_of in enumerate((query_grad, key_grad, value_grad)):
            target = pl.ds(pl.multiple_of(part * width + head * HEAD, HEAD), HEAD)
            joined[:, target] = value_of.astype(jnp.bfloat16)

    def some_heads(low_head, high_head):
        def unit():
            pl.loop(low_head, high_head)(head_step)

        return unit

    joined_store = pltpu.make_async_copy(joined, joined_out, sems.at[6])
    fresh_store = pltpu.make_async_copy(heads.at[0], fresh_out, sems.at[7])
    start_load = pltpu.make_async_copy(start_in, resid, sems.at[5])
    grad_store = pltpu.make_async_copy(heads.at[1], input_grad, sems.at[8])

    def add_tile(at, source_of, first):
        column_copy(at).wait()

        def body(rows):
            product_part = nt(source_of(rows), column_tiles[at % 2])
            total[rows] = product_part if first else total[rows] + product_part

        row_blocks(frames, body)
        if at + 2 < len(column_plan):
            column_copy(at + 2).start()

    def project(low_tile, high_tile):
        def unit():
            if low_tile == 0:
                joined_store.start()
            for at in range(low_tile, high_tile):
                add_tile(at, lambda rows, at=at: joined[rows, column_tile(at)], at == 0)

        return unit

    def norm_step(row, rows, gain):
        value = resid[rows]
        centered = value - jnp.mean(value, axis=-1, keepdims=True)
        inverse = lax.rsqrt(jnp.mean(centered * centered, axis=-1, keepdims=True) + EPSILON)
        normed = centered * inverse
        upstream = total[rows]
        scaled = upstream * gain
        first_mean = jnp.mean(scaled, axis=-1, keepdims=True)
        second_mean = jnp.mean(scaled * normed, axis=-1, keepdims=True)
        gain_rows[row] = gain_rows[row] + jnp.sum(upstream * normed, axis=0, keepdims=True)
        grad[rows] = grad[rows] + inverse * (scaled - first_mean - normed * second_mean)

    def attention_done():
        joined_store.wait()
        pair_start(0)
        for copy in first_loads[4:]:
            copy.wait()
        gain_rows[...] = jnp.zeros_like(gain_rows)
        gain = gains[1:2]

        def body(rows):
            norm_step(1, rows, gain)
            heads[0, rows] = (0.5 * grad[rows]).astype(jnp.bfloat16)

        row_blocks(frames, body)
        start_load.start()
        fresh_store.start()

    def inner_put(at):
        return pltpu.make_async_copy(
            joined.at[:, column_tile(at % 2)], inner_out.at[:, column_tile(at)], put_sems.at[at % 2]
        )

    def feed_tiles(low_tile, high_tile):
        def unit():
            for at in range(low_tile, high_tile):
                if at == 0:
                    fresh_store.wait()
                    pair_start(1)
                row_at = width // TILE + at
                row_copy(row_at).wait()
                inner_copy(at).wait()
                if at >= 2:
                    inner_put(at - 2).wait()

                def body(rows, at=at, row_at=row_at):
                    active_grad = nt(heads[0, rows], row_tiles[row_at % 2])
                    inner = inner_tiles[at % 2, rows]
                    gate = jax.nn.sigmoid(inner)
                    joined[rows, column_tile(at % 2)] = (
                        active_grad * (gate * (1.0 + inner * (1.0 - gate)))
                    ).astype(jnp.bfloat16)

                row_blocks(frames, body)
                inner_put(at).start()
                if row_at + 2 < len(row_plan):
                    row_copy(row_at + 2).start()
                if at + 2 < ff_tiles:
                    inner_copy(at + 2).start()
                add_tile(
                    joined_tiles + at, lambda rows, at=at: joined[rows, column_tile(at % 2)], at == 0
                )
            if high_tile == ff_tiles:
                for at in range(ff_tiles - 2, ff_tiles):
                    inner_put(at).wait()
                pair_start(2)

        return unit

    def feed_done():
        start_load.wait()
        gain = gains[0:1]

        def body(rows):
            norm_step(0, rows, gain)
            hidden = masked[rows]
            final = grad[rows]
            gain_rows[2] = gain_rows[2] + jnp.sum(final * hidden, axis=0, keepdims=True)
            heads[1, rows] = (final * (1.0 - hidden)).astype(jnp.bfloat16)

        row_blocks(frames, body)
        grad_store.start()
        small_first[...] = small[...]
        small_first[0:1] = gain_rows[0]
        small_first[1:2] = gain_rows[1]
        small_first[5:6] = gain_rows[2]
        grad_store.wait()

    head_count = width // HEAD
    units = [merged_grad]
    for at in range(0, head_count, 2):
        units.append(some_heads(at, at + 2))
    for at in range(0, joined_tiles, 3):
        units.append(project(at, at + 3))
    units.append(attention_done)
    for at in range(0, ff_tiles, 2):
        units.append(feed_tiles(at, at + 2))
    units.append(feed_done)
    return start_loads, units


INPUTS = 19


def reduce_kernel(depth, groups, count, chunks, given, late, *refs):
    extra, refs = refs[:INPUTS], refs[INPUTS:]
    given_refs, refs = refs[: len(given)], refs[len(given) :]
    outs, small_out = refs[:count], refs[count]
    input_grad, made = refs[count + 1], refs[count + 2 : count + 2 + len(late)]
    at = count + 2 + len(late)
    left_peers, right_peers = refs[at : at + count], refs[at + count : at + 2 * count]
    at += 2 * count
    slots = dict(zip(given, given_refs))
    for name, ref in zip(late, made):
        slots[(name, 1)] = ref
    lefts = [slots[(index, 0)] for index in range(count)]
    rights = [slots[(index, 1)] for index in range(count)]
    unit_scratch, refs = refs[at : at + 14], refs[at + 14 :]
    at = 0
    (
        left_buf,
        right_buf,
        held,
        line_held,
        first_in,
        second_in,
        line_in,
        whole_in,
        half_in,
        quarter_in,
        far_in,
        final,
        small_work,
        small_in,
        small_line,
        pair_send,
        pair_recv,
        load_sems,
        send_sems,
        recv_sems,
        store_sems,
        small_send,
        small_recv,
    ) = refs[at:]
    dp, z, core_bit, x_bit, y_bit = coordinates()
    group = dp // WAYS
    peer_c, peer_x, peer_y = (
        dp + 1 - 2 * core_bit,
        dp + 2 - 4 * x_bit,
        dp + 4 - 8 * y_bit,
    )
    far = [lax.rem(group + step, groups) * WAYS + lax.rem(dp, WAYS) for step in range(1, groups)]
    barrier = pltpu.get_barrier_semaphore()
    for peer in [peer_c, peer_x, peer_y] + far:
        signal(barrier, (peer, z))
    for step in range(1, depth):
        signal(barrier, (dp, lax.rem(z + step, depth)))
    pl.semaphore_wait(barrier, 3 + len(far) + depth - 1)
    tokens = lefts[0].shape[0]
    block = left_buf.shape[2] // depth
    here = (dp, z)

    def remote(source, target, send_sem, recv_sem, device):
        return pltpu.make_async_remote_copy(
            source, target, send_sem, recv_sem, device_id=device, device_id_type=MESH
        )

    pair_copies = []
    for index in range(count):
        half = rights[index].shape[1] // 2
        columns = pl.ds(pl.multiple_of((1 - core_bit) * half, half), half)
        pair_copies.append(
            (
                remote(
                    lefts[index],
                    left_peers[index],
                    pair_send.at[index, 0],
                    pair_recv.at[index, 0],
                    (peer_c, z),
                ),
                remote(
                    rights[index].at[:, columns],
                    right_peers[index],
                    pair_send.at[index, 1],
                    pair_recv.at[index, 1],
                    (peer_c, z),
                ),
            )
        )

    def pair_start(index):
        for copy in pair_copies[index]:
            copy.start()

    pair_start(0)
    start_loads, units = backward_units(
        extra,
        made,
        (input_grad,),
        unit_scratch,
        small_work.at[0],
        lambda number: pair_start(late[number]),
    )
    start_loads()

    def loads(chunk):
        index, row, part, left_slot, right_slot, new_left, new_right = chunks[chunk]
        rows = lefts[index].shape[1] // depth
        half = rights[index].shape[1] // 2
        piece = half // 4
        copies = []
        if new_left:
            for side, source in enumerate((lefts[index], left_peers[index])):
                for owner in range(depth):
                    copies.append(
                        pltpu.make_async_copy(
                            source.at[:, pl.ds(owner * rows + row, block)],
                            left_buf.at[
                                left_slot, pl.ds(side * tokens, tokens), pl.ds(owner * block, block)
                            ],
                            load_sems.at[left_slot, side * depth + owner],
                        )
                    )
        if new_right:
            for quarter in range(4):
                start = quarter * piece + part * LANES
                own_start = pl.multiple_of(core_bit * half + start, LANES)
                target = pl.ds(quarter * LANES, LANES)
                copies.append(
                    pltpu.make_async_copy(
                        rights[index].at[:, pl.ds(own_start, LANES)],
                        right_buf.at[right_slot, pl.ds(0, tokens), target],
                        load_sems.at[2 + right_slot, quarter],
                    )
                )
                copies.append(
                    pltpu.make_async_copy(
                        right_peers[index].at[:, pl.ds(start, LANES)],
                        right_buf.at[right_slot, pl.ds(tokens, tokens), target],
                        load_sems.at[2 + right_slot, 4 + quarter],
                    )
                )
        return copies

    arrived = set()

    def load_start(chunk):
        index = chunks[chunk][0]
        if index not in arrived:
            arrived.add(index)
            for copy in pair_copies[index]:
                copy.wait_recv()
            if index + 1 < count and index + 1 not in late:
                pair_start(index + 1)
        for copy in loads(chunk):
            copy.start()

    def axes(chunk):
        if chunk % 2 == 0:
            return peer_x, peer_y, x_bit, y_bit
        return peer_y, peer_x, y_bit, x_bit

    def quarter_of(chunk, first_bit, second_bit):
        if chunk % 2 == 0:
            return 2 * first_bit + second_bit
        return 2 * second_bit + first_bit

    plane_at, line_at = {}, {}
    for chunk in range(len(chunks)):
        places = line_at if chunk in LINE_FIRST else plane_at
        places[chunk] = len(places)

    def first_copy(chunk, which, device):
        _, _, first_bit, _ = axes(chunk)
        quarter = quarter_of(chunk, 1 - first_bit, which)
        if chunk in line_at:
            source = whole_in.at[line_at[chunk], 0, quarter]
            target = half_in.at[line_at[chunk], which]
        else:
            source = held.at[chunk % HELD, quarter]
            target = first_in.at[plane_at[chunk], which]
        return remote(
            source,
            target,
            send_sems.at[chunk, which],
            recv_sems.at[chunk, which],
            device,
        )

    def second_copy(chunk, device):
        _, _, _, second_bit = axes(chunk)
        if chunk in line_at:
            source = half_in.at[line_at[chunk], 1 - second_bit]
            target = quarter_in.at[line_at[chunk]]
        else:
            source = first_in.at[plane_at[chunk], 1 - second_bit]
            target = second_in.at[plane_at[chunk]]
        return remote(
            source,
            target,
            send_sems.at[chunk, 2],
            recv_sems.at[chunk, 2],
            device,
        )

    def line_copy(chunk, step, device):
        owner = lax.rem(z + step, depth)
        if chunk in line_at:
            source = line_held.at[line_at[chunk], :, owner]
            target = whole_in.at[line_at[chunk], step - 1]
        else:
            source = second_in.at[plane_at[chunk], owner]
            target = line_in.at[plane_at[chunk], step - 1]
        return remote(
            source,
            target,
            send_sems.at[chunk, 2 + step],
            recv_sems.at[chunk, 2 + step],
            device,
        )

    def held_sent(chunk):
        if chunk not in line_at:
            for which in range(2):
                first_copy(chunk, which, here).wait_send()

    def line_start(chunk):
        for step in range(1, depth):
            line_copy(chunk, step, (dp, lax.rem(z + step, depth))).start()

    def multiply(chunk):
        index, row, part, left_slot, right_slot, new_left, new_right = chunks[chunk]
        for copy in loads(chunk):
            copy.wait()
        if chunk + 1 < len(chunks):
            load_start(chunk + 1)
        if chunk >= HELD:
            held_sent(chunk - HELD)

        def body(owner):
            columns = pl.ds(pl.multiple_of(owner * block, block), block)
            product = lax.dot_general(
                left_buf[left_slot, :, columns],
                right_buf[right_slot],
                (((0,), (0,)), ((), ())),
                preferred_element_type=jnp.float32,
            ).astype(jnp.bfloat16)
            for quarter in range(4):
                piece = product[:, quarter * LANES : (quarter + 1) * LANES]
                if chunk in line_at:
                    line_held[line_at[chunk], quarter, owner] = piece
                else:
                    held[chunk % HELD, quarter, owner] = piece

        pl.loop(0, depth)(body)
        if chunk in line_at:
            line_start(chunk)
            return
        first_peer, _, _, _ = axes(chunk)
        for which in range(2):
            first_copy(chunk, which, (first_peer, z)).start()

    def line_total(chunk):
        place = line_at[chunk]
        for step in range(1, depth):
            line_copy(chunk, step, here).wait_recv()
        for quarter in range(4):
            total = line_held[place, quarter, z].astype(jnp.float32)
            for step in range(1, depth):
                total = total + whole_in[place, step - 1, quarter].astype(jnp.float32)
            whole_in[place, 0, quarter] = total.astype(jnp.bfloat16)
        first_peer, _, _, _ = axes(chunk)
        for which in range(2):
            first_copy(chunk, which, (first_peer, z)).start()

    def line_first_sum(chunk):
        place = line_at[chunk]
        _, second_peer, first_bit, second_bit = axes(chunk)
        for which in range(2):
            first_copy(chunk, which, here).wait_recv()

        def add(which):
            half_in[place, which] = (
                half_in[place, which].astype(jnp.float32)
                + whole_in[place, 0, quarter_of(chunk, first_bit, which)].astype(jnp.float32)
            ).astype(jnp.bfloat16)

        add(1 - second_bit)
        second_copy(chunk, (second_peer, z)).start()
        add(second_bit)

    def add_first(chunk):
        if chunk in line_at:
            line_total(chunk)
            return
        place = plane_at[chunk]
        _, second_peer, first_bit, second_bit = axes(chunk)
        for which in range(2):
            first_copy(chunk, which, here).wait_recv()

        def add(which):
            first_in[place, which] = (
                first_in[place, which].astype(jnp.float32)
                + held[chunk % HELD, quarter_of(chunk, first_bit, which)].astype(jnp.float32)
            ).astype(jnp.bfloat16)

        add(1 - second_bit)
        second_copy(chunk, (second_peer, z)).start()
        add(second_bit)

    def add_second(chunk):
        if chunk in line_at:
            line_first_sum(chunk)
            return
        place = plane_at[chunk]
        _, _, _, second_bit = axes(chunk)
        second_copy(chunk, here).wait_recv()
        second_in[place] = (
            second_in[place].astype(jnp.float32) + first_in[place, second_bit].astype(jnp.float32)
        ).astype(jnp.bfloat16)
        line_start(chunk)

    base = 2 + depth

    def where(chunk, core, x_at, y_at, half=None):
        index, row, part = chunks[chunk][:3]
        width = outs[index].shape[1]
        start = core * (width // 2) + (2 * x_at + y_at) * (width // 8) + part * LANES
        size = block
        if half is not None:
            size = block // 2
            row = row + half * size
        return outs[index].at[pl.ds(row, size), pl.ds(pl.multiple_of(start, LANES), LANES)]

    def from_final(chunk, message, device):
        return remote(
            final.at[chunk],
            where(chunk, core_bit, x_bit, y_bit),
            send_sems.at[chunk, base + message],
            recv_sems.at[chunk, base + message],
            device,
        )

    def passed(chunk, message, core, x_at, y_at, device, half=None):
        place = where(chunk, core, x_at, y_at, half)
        return remote(
            place,
            place,
            send_sems.at[chunk, base + message],
            recv_sems.at[chunk, base + message],
            device,
        )

    def store(chunk):
        return pltpu.make_async_copy(
            final.at[chunk], where(chunk, core_bit, x_bit, y_bit), store_sems.at[chunk]
        )

    def far_copy(chunk, step, device):
        return remote(
            far_in.at[chunk, groups],
            far_in.at[chunk, group],
            send_sems.at[chunk, base + 9 + step],
            recv_sems.at[chunk, base + 9 + step],
            device,
        )

    def piece_total(chunk):
        if chunk in line_at:
            _, _, _, second_bit = axes(chunk)
            second_copy(chunk, here).wait_recv()
            place = line_at[chunk]
            return half_in[place, second_bit].astype(jnp.float32) + quarter_in[place].astype(
                jnp.float32
            )
        for step in range(1, depth):
            line_copy(chunk, step, here).wait_recv()
        total = second_in[plane_at[chunk], z].astype(jnp.float32)
        for step in range(1, depth):
            total = total + line_in[plane_at[chunk], step - 1].astype(jnp.float32)
        return total

    def finish(chunk):
        total = piece_total(chunk)
        if groups > 1:
            own = total.astype(jnp.bfloat16)
            far_in[chunk, groups] = own
            far_in[chunk, group] = own
            for step, peer in enumerate(far):
                far_copy(chunk, step, (peer, z)).start()
            for step in range(len(far)):
                far_copy(chunk, step, here).wait()
            total = far_in[chunk, 0].astype(jnp.float32)
            for step in range(1, groups):
                total = total + far_in[chunk, step].astype(jnp.float32)
        final[chunk] = total.astype(jnp.bfloat16)
        for message, peer in enumerate((peer_x, peer_y, peer_c)):
            from_final(chunk, message, (peer, z)).start()
        store(chunk).start()

    def plane_arrived(chunk):
        passed(chunk, 0, core_bit, 1 - x_bit, y_bit, here).wait_recv()
        passed(chunk, 3, core_bit, 1 - x_bit, y_bit, (peer_y, z), 0).start()
        passed(chunk, 5, core_bit, 1 - x_bit, y_bit, (peer_c, z)).start()
        passed(chunk, 1, core_bit, x_bit, 1 - y_bit, here).wait_recv()
        passed(chunk, 4, core_bit, x_bit, 1 - y_bit, (peer_x, z), 1).start()
        passed(chunk, 6, core_bit, x_bit, 1 - y_bit, (peer_c, z)).start()

    def corner_arrived(chunk):
        for half in range(2):
            passed(chunk, 3 + half, core_bit, 1 - x_bit, 1 - y_bit, here, half).wait_recv()
            passed(chunk, 7 + half, core_bit, 1 - x_bit, 1 - y_bit, (peer_c, z), half).start()

    def core_arrived(chunk):
        other = 1 - core_bit
        passed(chunk, 2, other, x_bit, y_bit, here).wait_recv()
        passed(chunk, 5, other, 1 - x_bit, y_bit, here).wait_recv()
        passed(chunk, 6, other, x_bit, 1 - y_bit, here).wait_recv()
        for half in range(2):
            passed(chunk, 7 + half, other, 1 - x_bit, 1 - y_bit, here, half).wait_recv()

    def small_copy(turn, device):
        return remote(
            small_work.at[turn],
            small_in.at[turn],
            small_send.at[turn],
            small_recv.at[turn],
            device,
        )

    def small_far_copy(step, device):
        return remote(
            small_work.at[3],
            small_in.at[3 + group],
            small_send.at[3 + step],
            small_recv.at[3 + step],
            device,
        )

    slice_width = small_out.shape[1]

    def small_line_copy(step, device):
        columns = pl.ds(
            pl.multiple_of(lax.rem(z + step, depth) * slice_width, slice_width), slice_width
        )
        return remote(
            small_work.at[4, :, columns],
            small_line.at[step - 1],
            small_send.at[2 + groups + step],
            small_recv.at[2 + groups + step],
            device,
        )

    small_peers = (peer_c, peer_x, peer_y)

    def small_turn(turn):
        if 1 <= turn <= 3:
            small_copy(turn - 1, here).wait_recv()
            small_work[turn] = small_work[turn - 1] + small_in[turn - 1]
        if turn < 3:
            small_copy(turn, (small_peers[turn], z)).start()
        if turn == 3:
            if groups > 1:
                small_in[3 + group] = small_work[3]
                for step, peer in enumerate(far):
                    small_far_copy(step, (peer, z)).start()
                for step in range(len(far)):
                    small_far_copy(step, here).wait()
                total = small_in[3]
                for step in range(1, groups):
                    total = total + small_in[3 + step]
                small_work[4] = total
            else:
                small_work[4] = small_work[3]
            for step in range(1, depth):
                small_line_copy(step, (dp, lax.rem(z + step, depth))).start()
        if turn == 4:
            columns = pl.ds(pl.multiple_of(z * slice_width, slice_width), slice_width)
            total = small_work[4, :, columns]
            for step in range(1, depth):
                small_line_copy(step, here).wait_recv()
                total = total + small_line[step - 1]
            small_out[...] = total

    total_chunks = len(chunks)
    load_start(0)
    stages = (add_first, add_second, finish, plane_arrived, corner_arrived, core_arrived)
    agenda = {}
    for chunk in range(total_chunks):
        for lag, action in zip(LINE_LAGS if chunk in line_at else PLANE_LAGS, stages):
            agenda.setdefault(chunk + lag, []).append((chunk, action))
    for turn in range(max(agenda) + 1):
        if turn < total_chunks:
            multiply(turn)
        if turn < len(units):
            units[turn]()
        if 0 <= turn - len(units) < 5:
            small_turn(turn - len(units))
        for chunk, action in sorted(agenda.get(turn, []), key=lambda item: -item[0]):
            action(chunk)
    for index in range(count):
        for copy in pair_copies[index]:
            copy.wait_send()
    for turn in range(3):
        small_copy(turn, here).wait_send()
    for step in range(1, depth):
        small_line_copy(step, here).wait_send()
    for chunk in range(total_chunks):
        if chunk >= total_chunks - HELD:
            held_sent(chunk)
        if chunk in line_at:
            for which in range(2):
                first_copy(chunk, which, here).wait_send()
        for step in range(1, depth):
            line_copy(chunk, step, here).wait_send()
        second_copy(chunk, here).wait_send()
        for message in range(3):
            from_final(chunk, message, here).wait_send()
        for message in (5, 6):
            passed(chunk, message, core_bit, x_bit, y_bit, here).wait_send()
        for message in (3, 4, 7, 8):
            passed(chunk, message, core_bit, x_bit, y_bit, here, 0).wait_send()
        store(chunk).wait()


def reduce_chunks(depth, pairs, block):
    chunks = []
    left_slot, right_slot = 1, 1
    last_left, last_right = None, None
    for index, (left, right) in enumerate(pairs):
        rows = left.shape[1] // depth
        for row in range(0, rows, block):
            for part in range(right.shape[1] // (WAYS * LANES)):
                new_left = last_left != (index, row)
                new_right = last_right != (index, part)
                if new_left:
                    left_slot = 1 - left_slot
                if new_right:
                    right_slot = 1 - right_slot
                last_left, last_right = (index, row), (index, part)
                chunks.append((index, row, part, left_slot, right_slot, new_left, new_right))
    return chunks


def reduce_all(depth, groups, pairs, extra, small, collective):
    count = len(pairs)
    tokens = pairs[0][0].shape[0]
    width = small.shape[1]
    block = width // depth
    shapes = [
        (left, right if not isinstance(right, int) else jax.ShapeDtypeStruct((tokens, right), left.dtype))
        for left, right in pairs
    ]
    chunks = reduce_chunks(depth, shapes, block)
    total = len(chunks)
    lines = len([chunk for chunk in range(total) if chunk in LINE_FIRST])
    low = jnp.bfloat16
    given, operands, late = [], [], []
    for index, (left, right) in enumerate(pairs):
        given.append((index, 0))
        operands.append(left)
        if isinstance(right, int):
            late.append(index)
        else:
            given.append((index, 1))
            operands.append(right)
    outs, made, left_peers, right_peers = [], [], [], []
    for index, (left, right) in enumerate(shapes):
        outs.append(jax.ShapeDtypeStruct((left.shape[1] // depth, right.shape[1]), low))
        left_peers.append(jax.ShapeDtypeStruct(left.shape, low))
        right_peers.append(jax.ShapeDtypeStruct((tokens, right.shape[1] // 2), low))
        if index in late:
            made.append(jax.ShapeDtypeStruct(right.shape, low))
    outs.append(jax.ShapeDtypeStruct((small.shape[0], block), jnp.float32))
    outs.append(jax.ShapeDtypeStruct((tokens, width), low))
    messages = 2 + depth + 9 + groups
    any_spec = pl.BlockSpec(memory_space=pl.ANY)
    vmem_spec = pl.BlockSpec(memory_space=pltpu.VMEM)
    results = pl.pallas_call(
        functools.partial(reduce_kernel, depth, groups, count, chunks, given, late),
        out_shape=outs + made + left_peers + right_peers,
        in_specs=[any_spec] * 12 + [vmem_spec] * 7 + [any_spec] * len(operands),
        out_specs=[any_spec] * count
        + [vmem_spec]
        + [any_spec] * (1 + len(made) + 2 * count),
        scratch_shapes=[
            pltpu.VMEM((4, tokens, width), low),
            pltpu.VMEM((tokens, 3 * width), low),
            pltpu.VMEM((2, TILE, width), low),
            pltpu.VMEM((2, width, TILE), low),
            pltpu.VMEM((2, tokens, TILE), jnp.float32),
            pltpu.VMEM((tokens, width), jnp.float32),
            pltpu.VMEM((tokens, width), jnp.float32),
            pltpu.VMEM((tokens, width), jnp.float32),
            pltpu.VMEM((3, 1, width), jnp.float32),
            pltpu.SemaphoreType.DMA((9,)),
            pltpu.SemaphoreType.DMA((2,)),
            pltpu.SemaphoreType.DMA((2,)),
            pltpu.SemaphoreType.DMA((2,)),
            pltpu.SemaphoreType.DMA((2,)),
            pltpu.VMEM((2, 2 * tokens, depth * block), low),
            pltpu.VMEM((2, 2 * tokens, 4 * LANES), low),
            pltpu.VMEM((HELD, 4, depth, block, LANES), low),
            pltpu.VMEM((max(lines, 1), 4, depth, block, LANES) if lines else (1, 1, 1, 16, LANES), low),
            pltpu.VMEM((total - lines, 2, depth, block, LANES), low),
            pltpu.VMEM((total - lines, depth, block, LANES), low),
            pltpu.VMEM((total - lines, depth - 1, block, LANES), low),
            pltpu.VMEM((max(lines, 1), depth - 1, 4, block, LANES), low),
            pltpu.VMEM((max(lines, 1), 2, block, LANES), low),
            pltpu.VMEM((max(lines, 1), block, LANES), low),
            pltpu.VMEM((total, groups + 1, block, LANES) if groups > 1 else (1, 1, 16, LANES), low),
            pltpu.VMEM((total, block, LANES), low),
            pltpu.VMEM((5,) + small.shape, jnp.float32),
            pltpu.VMEM((3 + groups,) + small.shape, jnp.float32),
            pltpu.VMEM((depth - 1, small.shape[0], block), jnp.float32),
            pltpu.SemaphoreType.DMA((count, 2)),
            pltpu.SemaphoreType.DMA((count, 2)),
            pltpu.SemaphoreType.DMA((4, max(2 * depth, 8))),
            pltpu.SemaphoreType.DMA((total, messages)),
            pltpu.SemaphoreType.DMA((total, messages)),
            pltpu.SemaphoreType.DMA((total,)),
            pltpu.SemaphoreType.DMA((3 + groups + depth,)),
            pltpu.SemaphoreType.DMA((3 + groups + depth,)),
        ],
        compiler_params=pltpu.CompilerParams(
            collective_id=collective, has_side_effects=True, vmem_limit_bytes=62 * 1024 * 1024
        ),
    )(*extra, small, *operands)
    return results[:count], results[count], results[count + 1]


def ffn_forward(inputs, layer_gain, weight_in, weight_out):
    out_norm, normed, inverse = layer_norm(inputs, layer_gain)
    hidden = out_norm.astype(jnp.bfloat16)
    inner = product(hidden, weight_in)
    active = jax.nn.silu(inner).astype(jnp.bfloat16)
    return (product(active, weight_out), (hidden, normed, inverse, inner, active))


def ffn_backward(upstream, stored, layer_gain, weight_in, weight_out):
    hidden, normed, inverse, inner, active = stored
    branch_grad = (0.5 * upstream).astype(jnp.bfloat16)
    active_grad = product_nt(branch_grad, weight_out)
    inner_grad = (active_grad * swish_slope(inner)).astype(jnp.bfloat16)
    norm_grad, gain_grad = norm_back(product_nt(inner_grad, weight_in), layer_gain, normed, inverse)
    return (upstream + norm_grad, [(hidden, inner_grad), (active, branch_grad)], gain_grad)


def conv_forward(inputs, layer_gain, weight_in, weight_out, small_low, live, units, share):
    row_count, model_width = inputs.shape
    frame_count = row_count // units
    out_norm, normed, inverse = layer_norm(inputs, layer_gain)
    hidden = out_norm.astype(jnp.bfloat16)
    proj = product(hidden, weight_in)
    linear_part = proj[:, :model_width]
    gate_part = jax.nn.sigmoid(proj[:, model_width:])
    glu = (linear_part * gate_part * live).reshape(units, frame_count, model_width)
    side = KER // 2
    padded = jnp.pad(glu, ((0, 0), (side, side), (0, 0)))
    kernel = small_low[1 : KER + 1].astype(jnp.float32)
    mixed = kernel[0] * padded[:, 0:frame_count]
    for offset in range(1, KER):
        mixed = mixed + kernel[offset] * padded[:, offset : offset + frame_count]
    mixed = mixed.reshape(row_count, model_width)
    local_count = jnp.sum(live)
    local_mean = jnp.sum(mixed * live, axis=0) / local_count
    local_spread = jnp.sum(jnp.square(mixed - local_mean) * live, axis=0)
    moments = jnp.stack([jnp.full((model_width,), local_count), local_mean, local_spread])
    moments = share(join_moments, jnp.pad(moments, ((0, 5), (0, 0))), 1)
    count, bmean = moments[0, 0], moments[1]
    bvar = moments[2] / count
    bn_inverse = lax.rsqrt(bvar + EPSILON)
    bn_normed = (mixed - bmean) * bn_inverse
    pre_act = small_low[KER + 1].astype(jnp.float32) * bn_normed + small_low[KER + 2].astype(
        jnp.float32
    )
    active = jax.nn.silu(pre_act).astype(jnp.bfloat16)
    stored = (
        hidden,
        normed,
        inverse,
        linear_part,
        gate_part,
        padded,
        bn_normed,
        bn_inverse,
        count,
        pre_act,
        active,
    )
    return (product(active, weight_out), stored)


def conv_backward(upstream, stored, layer_gain, weight_in, weight_out, small_low, live, units, share):
    (
        hidden,
        normed,
        inverse,
        linear_part,
        gate_part,
        padded,
        bn_normed,
        bn_inverse,
        count,
        pre_act,
        active,
    ) = stored
    row_count, model_width = upstream.shape
    frame_count = row_count // units
    kernel = small_low[1 : KER + 1].astype(jnp.float32)
    bn_scale = small_low[KER + 1].astype(jnp.float32)
    branch_grad = upstream.astype(jnp.bfloat16)
    pre_grad = product_nt(branch_grad, weight_out) * swish_slope(pre_act)
    sums = jnp.stack([jnp.sum(pre_grad, axis=0), jnp.sum(pre_grad * bn_normed, axis=0)])
    sums = share(add_pair, jnp.pad(sums, ((0, 6), (0, 0))), 2)
    shift_total, scale_total = sums[0], sums[1]
    mixed_grad = bn_inverse * (
        bn_scale * pre_grad
        - live * (bn_scale * shift_total) / count
        - live * bn_normed * (bn_scale * scale_total) / count
    )
    side = KER // 2
    grid_grad = mixed_grad.reshape(units, frame_count, model_width)
    grad_padded = jnp.pad(grid_grad, ((0, 0), (side, side), (0, 0)))
    last_tap = KER - 1
    glu_grad = kernel[0] * grad_padded[:, last_tap : last_tap + frame_count]
    for offset in range(1, KER):
        glu_grad = (
            glu_grad
            + kernel[offset] * grad_padded[:, last_tap - offset : last_tap - offset + frame_count]
        )
    kernel_grad = jnp.stack(
        [
            jnp.sum(padded[:, offset : offset + frame_count] * grid_grad, axis=(0, 1))
            for offset in range(KER)
        ]
    )
    glu_grad = glu_grad.reshape(row_count, model_width) * live
    proj_grad = jnp.concatenate(
        [glu_grad * gate_part, glu_grad * linear_part * gate_part * (1.0 - gate_part)], axis=1
    ).astype(jnp.bfloat16)
    norm_grad, gain_grad = norm_back(product_nt(proj_grad, weight_in), layer_gain, normed, inverse)
    return (
        upstream + norm_grad,
        [(hidden, proj_grad), (active, branch_grad)],
        gain_grad,
        kernel_grad,
        jnp.stack([scale_total, shift_total]),
    )


def local(
    depth_devices,
    groups,
    tokens,
    lengths,
    span_starts,
    mask_embed,
    norm_gains,
    ffn1_in,
    ffn1_out,
    attn_in,
    attn_out,
    conv_in,
    conv_out,
    depth,
    bn_affine,
    ffn2_in,
    ffn2_out,
    cotangent,
):
    units, frame_count, model_width = tokens.shape
    row_count = units * frame_count
    position = jnp.arange(frame_count, dtype=jnp.int32)
    valid = position[None, :] < lengths[:, None]
    inside = (position[None, None, :] >= span_starts[:, :, None]) & (
        position[None, None, :] < span_starts[:, :, None] + SPAN_LEN
    )
    masked = jnp.any(inside, axis=1) & valid
    live = valid.reshape(row_count, 1).astype(jnp.float32)
    masked_col = masked.reshape(row_count, 1)
    cosine, sine = rotation(frame_count)
    cosine, sine = cosine[:, 0], sine[:, 0]
    cosine_row = jnp.concatenate([cosine, cosine], axis=1)
    sine_row = jnp.concatenate([-sine, sine], axis=1)
    small = jnp.concatenate([norm_gains, mask_embed[None, :], depth, bn_affine], axis=0)
    small = jnp.pad(small, ((0, 16 - small.shape[0]), (0, 0)))
    gathered = gather_all(
        depth_devices,
        [ffn1_in, ffn1_out, attn_in, attn_out, conv_in, conv_out, ffn2_in, ffn2_out],
        (2, 2, 2, 1, 1, 1, 2, 2),
        small,
        tokens.reshape(row_count, model_width),
        masked_col.astype(jnp.float32),
        live,
        (cosine_row, sine_row),
    )
    (
        start,
        hidden_one,
        inner_one,
        active_one,
        first,
        hidden_two,
        queries,
        keys_rot,
        values_low,
        log_total,
        merged,
        second,
    ) = gathered[9:]
    small_all = gathered[8].transpose(1, 0, 2).reshape(16, model_width)
    third_small = jnp.concatenate([small_all[2:3], small_all[6:13]], axis=0)
    first_weights = (gathered[0], gathered[1])
    second_weights = (gathered[2], gathered[3])
    third_weights = (gathered[4], gathered[5], third_small)
    fourth_weights = (gathered[6], gathered[7], small_all[3:5])
    gain_three = third_weights[2][0].astype(jnp.float32)
    share = functools.partial(exchange, depth_devices, groups)
    branch, third_stored = conv_forward(
        second, gain_three, third_weights[0], third_weights[1], third_weights[2], live, units, share
    )
    third = second + branch
    gain_four = fourth_weights[2][0].astype(jnp.float32)
    gain_five = fourth_weights[2][1].astype(jnp.float32)
    branch, fourth_stored = ffn_forward(third, gain_four, fourth_weights[0], fourth_weights[1])
    fourth = third + 0.5 * branch
    out_norm, final_normed, final_inverse = layer_norm(fourth, gain_five)
    output = out_norm.astype(jnp.bfloat16).reshape(units, frame_count, model_width)
    upstream = cotangent.reshape(row_count, model_width).astype(jnp.float32)
    grad_four, gain_five_grad = norm_back(upstream, gain_five, final_normed, final_inverse)
    grad_three, fourth_pairs, gain_four_grad = ffn_backward(
        grad_four, fourth_stored, gain_four, fourth_weights[0], fourth_weights[1]
    )
    grad_two, third_pairs, gain_three_grad, kernel_grad, affine_full = conv_backward(
        grad_three,
        third_stored,
        gain_three,
        third_weights[0],
        third_weights[1],
        third_weights[2],
        live,
        units,
        share,
    )
    zero_row = jnp.zeros((1, model_width), jnp.float32)
    small_grads = jnp.concatenate(
        [
            zero_row,
            zero_row,
            gain_three_grad[None, :],
            gain_four_grad[None, :],
            gain_five_grad[None, :],
            zero_row,
            kernel_grad,
            jnp.zeros((5, model_width), jnp.float32),
        ],
        axis=0,
    )
    branch_grad = grad_two.astype(jnp.bfloat16)
    extra = [
        grad_two,
        branch_grad,
        queries,
        keys_rot,
        values_low,
        second_weights[0],
        second_weights[1],
        first_weights[0],
        first_weights[1],
        inner_one,
        first,
        start,
        log_total,
        live,
        masked_col.astype(jnp.float32),
        cosine_row,
        -sine_row,
        small_all[0:8].astype(jnp.float32),
    ]
    pairs = fourth_pairs + third_pairs
    pairs += [(merged, branch_grad), (hidden_two, attn_in.shape[1])]
    pairs += [(active_one, model_width), (hidden_one, ffn1_in.shape[1])]
    reduced, small_sum, input_grad = reduce_all(
        depth_devices, groups, pairs, extra, small_grads, 3
    )
    input_grad = input_grad.reshape(units, frame_count, model_width)
    ffn2_in_grad, ffn2_out_grad, conv_in_grad, conv_out_grad = (
        array.astype(jnp.float32) for array in reduced[:4]
    )
    attn_out_grad, attn_in_grad, ffn1_out_grad, ffn1_in_grad = (
        array.astype(jnp.float32) for array in reduced[4:]
    )
    column_width = norm_gains.shape[1]
    affine_grad = lax.dynamic_slice_in_dim(
        affine_full, lax.axis_index("fsdp") * column_width, column_width, 1
    )
    return (
        output,
        input_grad,
        small_sum[5],
        small_sum[0:5],
        ffn1_in_grad,
        ffn1_out_grad,
        attn_in_grad,
        attn_out_grad,
        conv_in_grad,
        conv_out_grad,
        small_sum[6 : 6 + KER],
        affine_grad,
        ffn2_in_grad,
        ffn2_out_grad,
    )


def solution(mesh):
    in_specs = (
        P(("dp", "fsdp"), None, None),
        P(("dp", "fsdp")),
        P(("dp", "fsdp"), None),
        P("fsdp"),
        P(None, "fsdp"),
        P("fsdp", None),
        P("fsdp", None),
        P("fsdp", None),
        P("fsdp", None),
        P("fsdp", None),
        P("fsdp", None),
        P(None, "fsdp"),
        P(None, "fsdp"),
        P("fsdp", None),
        P("fsdp", None),
        P(("dp", "fsdp"), None, None),
    )
    out_specs = (
        P(("dp", "fsdp"), None, None),
        P(("dp", "fsdp"), None, None),
        P("fsdp"),
        P(None, "fsdp"),
        P("fsdp", None),
        P("fsdp", None),
        P("fsdp", None),
        P("fsdp", None),
        P("fsdp", None),
        P("fsdp", None),
        P(None, "fsdp"),
        P(None, "fsdp"),
        P("fsdp", None),
        P("fsdp", None),
    )
    body = functools.partial(local, mesh.shape["fsdp"], mesh.shape["dp"] // WAYS)
    return jax.shard_map(body, mesh=mesh, in_specs=in_specs, out_specs=out_specs, check_vma=False)
```

```python
import functools

import jax
import jax.numpy as jnp
from jax import lax
from jax.experimental import pallas as pl
from jax.experimental.pallas import tpu as pltpu
from jax.sharding import PartitionSpec as P

HEAD = 128
KER = 5
SPAN_LEN = 10


EPSILON = 1e-05
NEGATIVE = -1000000000.0


def product(left_side, right_side):
    return jnp.dot(left_side, right_side, preferred_element_type=jnp.float32)


def product_nt(left_side, right_side):
    return lax.dot_general(
        left_side, right_side, (((1,), (1,)), ((), ())), preferred_element_type=jnp.float32
    )


def layer_norm(inputs, layer_gain):
    average = jnp.mean(inputs, axis=-1, keepdims=True)
    centered = inputs - average
    inverse = lax.rsqrt(jnp.mean(centered * centered, axis=-1, keepdims=True) + EPSILON)
    normed = centered * inverse
    return (normed * layer_gain, normed, inverse)


def norm_back(upstream, layer_gain, normed, inverse):
    scaled = upstream * layer_gain
    first_mean = jnp.mean(scaled, axis=-1, keepdims=True)
    second_mean = jnp.mean(scaled * normed, axis=-1, keepdims=True)
    return (
        inverse * (scaled - first_mean - normed * second_mean),
        jnp.sum(upstream * normed, axis=0),
    )


def swish_slope(inputs):
    sigmoid_part = jax.nn.sigmoid(inputs)
    return sigmoid_part * (1.0 + inputs * (1.0 - sigmoid_part))


def rotation(frame_count):
    half_size = HEAD // 2
    position = jnp.arange(frame_count, dtype=jnp.float32)
    frequency = 10000.0 ** (-jnp.arange(half_size, dtype=jnp.float32) / half_size)
    angles = position[:, None] * frequency[None, :]
    return (jnp.cos(angles)[:, None, :], jnp.sin(angles)[:, None, :])


MESH = pl.DeviceIdType.MESH
WAYS = 8


def coordinates():
    dp = lax.axis_index("dp")
    z = lax.axis_index("fsdp")
    core_bit = lax.rem(dp, 2)
    x_bit = lax.rem(dp // 2, 2)
    y_bit = lax.rem(dp // 4, 2)
    return dp, z, core_bit, x_bit, y_bit


def signal(sem, device):
    pl.semaphore_signal(sem, inc=1, device_id=device, device_id_type=MESH)


def greet(depth, dp, z, flat_peers):
    barrier = pltpu.get_barrier_semaphore()
    signal(barrier, (dp, lax.rem(z + 1, depth)))
    signal(barrier, (dp, lax.rem(z + depth - 1, depth)))
    for peer in flat_peers:
        signal(barrier, (peer, z))
    pl.semaphore_wait(barrier, 2 + len(flat_peers))


TILE = 512
ROWS = 256
ALONG_LINE = (5,)
GATHER_LAGS = (2, 4, 6)
GATHER_LEAD = 3
PER_TURN = 3


def column_tile(index):
    return pl.ds(index * TILE, TILE)


def row_blocks(rows, body):
    def step(block):
        body(pl.ds(pl.multiple_of(block * ROWS, ROWS), ROWS))

    pl.loop(0, rows // ROWS)(step)


def nt(left_side, right_side):
    return lax.dot_general(
        left_side, right_side, (((1,), (1,)), ((), ())), preferred_element_type=jnp.float32
    )


def forward_units(inputs, weights, results, scratch, small_full):
    tokens, masked, live, cosine, sine = inputs
    ffn_in_w, ffn_out_w, attn_in_w, attn_out_w = weights
    (
        start_out,
        hidden_one_out,
        inner_out,
        active_out,
        first_out,
        hidden_two_out,
        queries_out,
        keys_out,
        values_out,
        log_out,
        merged_out,
        second_out,
    ) = results
    (
        resid,
        total,
        hidden,
        active,
        heads,
        merged,
        row_tiles,
        column_tiles,
        inner_tiles,
        gains,
        sems,
        row_sems,
        column_sems,
        inner_sems,
    ) = scratch
    frames, width = resid.shape
    ff_tiles = active.shape[1] // TILE
    head_tiles = width // TILE

    def row_copy(source):
        return lambda at: pltpu.make_async_copy(
            source.at[pl.ds(at * TILE, TILE)], row_tiles.at[at % 2], row_sems.at[at % 2]
        )

    def column_copy(source):
        return lambda at: pltpu.make_async_copy(
            source.at[:, column_tile(at)], column_tiles.at[at % 2], column_sems.at[at % 2]
        )

    def stream(copy_of, low_tile, high_tile, count, body):
        if low_tile == 0:
            for at in range(min(2, count)):
                copy_of(at).start()
        for at in range(low_tile, high_tile):
            copy_of(at).wait()
            body(at)
            if at + 2 < count:
                copy_of(at + 2).start()

    def put(source, target, index):
        return pltpu.make_async_copy(source, target, sems.at[index])

    start_put = put(resid, start_out, 0)
    hidden_one_put = put(hidden, hidden_one_out, 1)
    active_put = put(active, active_out, 2)
    first_put = put(resid, first_out, 3)
    hidden_two_put = put(hidden, hidden_two_out, 4)
    head_puts = [
        put(heads.at[part], target, 5 + part)
        for part, target in enumerate((queries_out, keys_out, values_out))
    ]
    merged_put = put(merged, merged_out, 8)
    second_put = put(total, second_out, 9)

    def normed(value, gain):
        centered = value - jnp.mean(value, axis=-1, keepdims=True)
        inverse = lax.rsqrt(jnp.mean(centered * centered, axis=-1, keepdims=True) + EPSILON)
        return (centered * inverse * gain).astype(jnp.bfloat16)

    def prepare():
        depth, _, piece = small_full.shape
        for owner in range(depth):
            gains[:, owner * piece : (owner + 1) * piece] = small_full[owner].astype(jnp.float32)
        gain, embed = gains[0:1], gains[5:6]

        def body(rows):
            value = jnp.where(masked[rows] > 0.0, embed, tokens[rows].astype(jnp.float32))
            resid[rows] = value
            hidden[rows] = normed(value, gain)

        row_blocks(frames, body)
        start_put.start()
        hidden_one_put.start()

    def inner_put(at):
        return pltpu.make_async_copy(
            inner_tiles.at[at % 2], inner_out.at[:, column_tile(at)], inner_sems.at[at % 2]
        )

    def widen(low_tile, high_tile):
        def unit():
            def body(at):
                if at >= 2:
                    inner_put(at - 2).wait()

                def step(rows):
                    inner = product(hidden[rows], column_tiles[at % 2])
                    inner_tiles[at % 2, rows] = inner
                    active[rows, column_tile(at)] = (inner * jax.nn.sigmoid(inner)).astype(
                        jnp.bfloat16
                    )

                row_blocks(frames, step)
                inner_put(at).start()

            stream(column_copy(ffn_in_w), low_tile, high_tile, ff_tiles, body)
            if high_tile == ff_tiles:
                active_put.start()
                for at in range(ff_tiles - 2, ff_tiles):
                    inner_put(at).wait()

        return unit

    def narrow(low_tile, high_tile):
        def unit():
            def body(at):
                def step(rows):
                    part = product(active[rows, column_tile(at)], row_tiles[at % 2])
                    total[rows] = part if at == 0 else total[rows] + part

                row_blocks(frames, step)

            stream(row_copy(ffn_out_w), low_tile, high_tile, ff_tiles, body)

        return unit

    def first_done():
        start_put.wait()
        hidden_one_put.wait()
        active_put.wait()
        gain = gains[1:2]

        def body(rows):
            value = resid[rows] + 0.5 * total[rows]
            resid[rows] = value
            hidden[rows] = normed(value, gain)

        row_blocks(frames, body)
        first_put.start()
        hidden_two_put.start()

    def split_heads(low_tile, high_tile):
        def unit():
            def body(at):
                part = at // head_tiles

                def step(rows):
                    value = product(hidden[rows], column_tiles[at % 2])
                    for head in range(TILE // HEAD):
                        piece = value[:, head * HEAD : (head + 1) * HEAD]
                        if part < 2:
                            piece = piece * cosine[rows] + pltpu.roll(piece, HEAD // 2, 1) * sine[rows]
                        first = (at % head_tiles) * TILE + head * HEAD
                        heads[part, rows, pl.ds(first, HEAD)] = piece.astype(jnp.bfloat16)

                row_blocks(frames, step)

            stream(column_copy(attn_in_w), low_tile, high_tile, 3 * head_tiles, body)
            if high_tile == 3 * head_tiles:
                for copy in head_puts:
                    copy.start()

        return unit

    def head_step(head):
        columns = pl.ds(pl.multiple_of(head * HEAD, HEAD), HEAD)
        query, key, value = heads[0, :, columns], heads[1, :, columns], heads[2, :, columns]
        scores = jnp.where(live[...] > 0.0, nt(key, query) * HEAD ** (-0.5), NEGATIVE)
        top_score = jnp.max(scores, axis=0, keepdims=True)
        raised = jnp.exp(scores - top_score)
        amount = jnp.sum(raised, axis=0, keepdims=True)
        log_out[head] = top_score + jnp.log(amount)
        probs = (raised * (1.0 / amount)).astype(jnp.bfloat16)
        merged[:, columns] = lax.dot_general(
            probs, value, (((0,), (0,)), ((), ())), preferred_element_type=jnp.float32
        ).astype(jnp.bfloat16)

    def some_heads(low_head, high_head):
        def unit():
            pl.loop(low_head, high_head)(head_step)

        return unit

    def attention_done():
        merged_put.start()

        def body(at):
            def step(rows):
                part = product(merged[rows, column_tile(at)], row_tiles[at % 2])
                total[rows] = (resid[rows] if at == 0 else total[rows]) + part

            row_blocks(frames, step)

        stream(row_copy(attn_out_w), 0, head_tiles, head_tiles, body)
        second_put.start()

    def finish():
        for copy in [first_put, hidden_two_put, merged_put, second_put] + head_puts:
            copy.wait()

    units = [(None, prepare)]
    for at in range(0, ff_tiles, 2):
        units.append((0, widen(at, at + 2)))
    for at in range(0, ff_tiles, 4):
        units.append((1, narrow(at, at + 4)))
    units.append((1, first_done))
    for at in range(0, 3 * head_tiles, 3):
        units.append((2, split_heads(at, at + 3)))
    for at in range(0, width // HEAD, 2):
        units.append((2, some_heads(at, at + 2)))
    units.append((3, attention_done))
    return units, finish


FORWARD_INPUTS = 5
FORWARD_RESULTS = 12
FORWARD_SCRATCH = 14


def gather_kernel(depth, count, chunks, lead, *refs):
    extra, refs = refs[:FORWARD_INPUTS], refs[FORWARD_INPUTS:]
    shards, small = refs[:count], refs[count]
    fulls, small_full = refs[count + 1 : 2 * count + 1], refs[2 * count + 1]
    refs = refs[2 * count + 2 :]
    results, refs = refs[:FORWARD_RESULTS], refs[FORWARD_RESULTS:]
    unit_scratch, refs = refs[:FORWARD_SCRATCH], refs[FORWARD_SCRATCH:]
    send_sems, recv_sems, own_sems, small_sems = refs
    dp, z, core_bit, x_bit, y_bit = coordinates()
    mine = lax.rem(dp, WAYS)
    step_c, step_x, step_y = 1 - 2 * core_bit, 2 - 4 * x_bit, 4 - 8 * y_bit
    peer_c, peer_x, peer_y = dp + step_c, dp + step_x, dp + step_y
    greet(depth, dp, z, (peer_c, peer_x, peer_y))

    def remote(source, target, send_sem, recv_sem, device):
        return pltpu.make_async_remote_copy(
            source, target, send_sem, recv_sem, device_id=device, device_id_type=MESH
        )

    def slot(chunk, owner, piece, half):
        index, first, width = chunks[chunk]
        rows = shards[index].shape[0]
        part = rows // WAYS
        if index in ALONG_LINE:
            part = rows // 2
        if half is not None:
            width = width // 2
            first = first + half * width
        start = pl.multiple_of(owner * rows + piece * part, part)
        return fulls[index].at[pl.ds(start, part), pl.ds(first, width)]

    def place(chunk, index, message, owner, piece, device, half=None):
        where = slot(chunk, owner, piece, half)
        return remote(
            where,
            where,
            send_sems.at[chunk, index, message],
            recv_sems.at[chunk, index, message],
            device,
        )

    def each(action):
        for hop in range(depth - 1):

            @pl.when(z - 1 - hop >= 0)
            def _():
                action(2 * hop, z - 1 - hop, hop, 1)

            @pl.when(z + 1 + hop < depth)
            def _():
                action(2 * hop + 1, z + 1 + hop, hop, -1)

    here = (dp, z)
    core_dev, x_dev, y_dev = (peer_c, z), (peer_x, z), (peer_y, z)
    piece_x, piece_y, piece_xy = mine + step_x, mine + step_y, mine + step_x + step_y
    other = mine + step_c
    other_x, other_y, other_xy = other + step_x, other + step_y, other + step_x + step_y

    small_local = pltpu.make_async_copy(small, small_full.at[z], own_sems.at[count, 0])
    small_local.start()

    def small_out(index, source, owner, device):
        return remote(
            source, small_full.at[owner], small_sems.at[index, 0], small_sems.at[index, 1], device
        )

    @pl.when(z + 1 < depth)
    def _():
        small_out(0, small, z, (dp, z + 1)).start()

    @pl.when(z > 0)
    def _():
        small_out(1, small, z, (dp, z - 1)).start()

    def line_start(chunk):
        index, first, width = chunks[chunk]
        whole_line = index in ALONG_LINE
        part = shards[index].shape[0] // (2 if whole_line else WAYS)
        piece = core_bit if whole_line else mine
        source = shards[index].at[
            pl.ds(pl.multiple_of(piece * part, part), part), pl.ds(first, width)
        ]
        target = slot(chunk, z, piece, None)

        @pl.when(z + 1 < depth)
        def _():
            remote(
                source, target, send_sems.at[chunk, 0, 0], recv_sems.at[chunk, 0, 0], (dp, z + 1)
            ).start()

        @pl.when(z > 0)
        def _():
            remote(
                source, target, send_sems.at[chunk, 1, 0], recv_sems.at[chunk, 1, 0], (dp, z - 1)
            ).start()

    def along_line(chunk):
        return chunks[chunk][0] in ALONG_LINE

    def line_arrived(chunk):
        piece = core_bit if along_line(chunk) else mine

        def action(index, owner, hop, way):
            place(chunk, index, 0, owner, piece, here).wait_recv()
            if hop < depth - 2:
                following = z + way

                @pl.when((following >= 0) & (following < depth))
                def _():
                    place(chunk, index + 2, 0, owner, piece, (dp, following)).start()

            if along_line(chunk):
                place(chunk, index, 5, owner, piece, core_dev).start()
                return
            place(chunk, index, 1, owner, mine, x_dev).start()
            place(chunk, index, 2, owner, mine, y_dev).start()
            place(chunk, index, 5, owner, mine, core_dev).start()

        each(action)

    def plane_arrived(chunk):
        def action(index, owner, hop, way):
            place(chunk, index, 1, owner, piece_x, here).wait_recv()
            place(chunk, index, 3, owner, piece_x, y_dev, 0).start()
            place(chunk, index, 6, owner, piece_x, core_dev).start()
            place(chunk, index, 2, owner, piece_y, here).wait_recv()
            place(chunk, index, 4, owner, piece_y, x_dev, 1).start()
            place(chunk, index, 7, owner, piece_y, core_dev).start()

        each(action)

    def corner_arrived(chunk):
        def action(index, owner, hop, way):
            for half in range(2):
                place(chunk, index, 3 + half, owner, piece_xy, here, half).wait_recv()
                place(chunk, index, 8 + half, owner, piece_xy, core_dev, half).start()

        each(action)

    def core_arrived(chunk):
        def action(index, owner, hop, way):
            if along_line(chunk):
                place(chunk, index, 5, owner, 1 - core_bit, here).wait_recv()
                return
            place(chunk, index, 5, owner, other, here).wait_recv()
            place(chunk, index, 6, owner, other_x, here).wait_recv()
            place(chunk, index, 7, owner, other_y, here).wait_recv()
            for half in range(2):
                place(chunk, index, 8 + half, owner, other_xy, here, half).wait_recv()

        each(action)

    def small_action(index, owner, hop, way):
        small_out(index, small, owner, here).wait_recv()
        if hop < depth - 2:
            following = z + way

            @pl.when((following >= 0) & (following < depth))
            def _():
                small_out(index + 2, small_full.at[owner], owner, (dp, following)).start()

    total = len(chunks)
    for chunk in range(min(lead, total)):
        line_start(chunk)
    own_copies = []
    for index in range(count):
        rows = shards[index].shape[0]
        target = fulls[index].at[pl.ds(pl.multiple_of(z * rows, rows), rows)]
        copy = remote(
            shards[index], target, own_sems.at[index, 0], own_sems.at[index, 1], core_dev
        )
        copy.start()
        own_copies.append(copy)
    last_chunk = {index: chunk for chunk, (index, _, _) in enumerate(chunks)}
    seen = set()
    units, finish = forward_units(extra, fulls[:4], results, unit_scratch, small_full)
    plane_lag, corner_lag, core_lag = GATHER_LAGS
    for turn in range(total + core_lag):
        if turn + lead < total:
            line_start(turn + lead)
        if turn < total:
            line_arrived(turn)
        if turn == 0:
            each(small_action)
            small_local.wait()
        if 0 <= turn - plane_lag < total and not along_line(turn - plane_lag):
            plane_arrived(turn - plane_lag)
        if 0 <= turn - corner_lag < total and not along_line(turn - corner_lag):
            corner_arrived(turn - corner_lag)
        if 0 <= turn - core_lag < total:
            core_arrived(turn - core_lag)
        for _ in range(PER_TURN):
            if units and (units[0][0] is None or last_chunk[units[0][0]] <= turn - core_lag):
                needed, unit = units.pop(0)
                if needed is not None and needed not in seen:
                    seen.add(needed)
                    own_copies[needed].wait_recv()
                unit()
    assert not units
    finish()
    for index, copy in enumerate(own_copies):
        if index not in seen:
            copy.wait_recv()
        copy.wait_send()

    @pl.when(z + 1 < depth)
    def _():
        small_out(0, small, z, here).wait_send()

    @pl.when(z > 0)
    def _():
        small_out(1, small, z, here).wait_send()

    def small_drain(index, owner, hop, way):
        if hop < depth - 2:
            following = z + way

            @pl.when((following >= 0) & (following < depth))
            def _():
                small_out(index + 2, small, owner, here).wait_send()

    each(small_drain)
    for chunk in range(total):
        piece = core_bit if along_line(chunk) else mine

        @pl.when(z + 1 < depth)
        def _():
            place(chunk, 0, 0, z, piece, here).wait_send()

        @pl.when(z > 0)
        def _():
            place(chunk, 1, 0, z, piece, here).wait_send()

        def drain(index, owner, hop, way):
            if hop < depth - 2:
                following = z + way

                @pl.when((following >= 0) & (following < depth))
                def _():
                    place(chunk, index + 2, 0, owner, piece, here).wait_send()

            if along_line(chunk):
                place(chunk, index, 5, owner, piece, here).wait_send()
                return
            for message in (1, 2, 5, 6, 7):
                place(chunk, index, message, owner, mine, here).wait_send()
            for message in (3, 4, 8, 9):
                place(chunk, index, message, owner, mine, here, 0).wait_send()

        each(drain)


def gather_all(depth, weights, splits, small, tokens, masked, live, tables):
    count = len(weights)
    chunks = []
    for index, weight in enumerate(weights):
        width = weight.shape[1] // splits[index]
        chunks += [(index, part * width, width) for part in range(splits[index])]
    shape = (len(chunks), 2 * (depth - 1), 10)
    frames, width = tokens.shape
    wide = weights[0].shape[1]
    heads = width // HEAD
    low, full = jnp.bfloat16, jnp.float32

    def array(shape, dtype):
        return jax.ShapeDtypeStruct(shape, dtype)

    outs = [array((weight.shape[0] * depth, weight.shape[1]), low) for weight in weights]
    outs.append(array((depth,) + small.shape, small.dtype))
    square = (frames, width)
    outs += [
        array(square, full),
        array(square, low),
        array((frames, wide), full),
        array((frames, wide), low),
        array(square, full),
        array(square, low),
        array(square, low),
        array(square, low),
        array(square, low),
        array((heads, 1, frames), full),
        array(square, low),
        array(square, full),
    ]
    any_spec = pl.BlockSpec(memory_space=pl.ANY)
    vmem_spec = pl.BlockSpec(memory_space=pltpu.VMEM)
    return pl.pallas_call(
        functools.partial(gather_kernel, depth, count, chunks, GATHER_LEAD),
        out_shape=outs,
        in_specs=[vmem_spec] * FORWARD_INPUTS + [any_spec] * (count + 1),
        out_specs=[any_spec] * count
        + [vmem_spec]
        + [any_spec] * 9
        + [vmem_spec]
        + [any_spec] * 2,
        scratch_shapes=[
            pltpu.VMEM(square, full),
            pltpu.VMEM(square, full),
            pltpu.VMEM(square, low),
            pltpu.VMEM((frames, wide), low),
            pltpu.VMEM((3,) + square, low),
            pltpu.VMEM(square, low),
            pltpu.VMEM((2, TILE, width), low),
            pltpu.VMEM((2, width, TILE), low),
            pltpu.VMEM((2, frames, TILE), full),
            pltpu.VMEM((small.shape[0], width), full),
            pltpu.SemaphoreType.DMA((10,)),
            pltpu.SemaphoreType.DMA((2,)),
            pltpu.SemaphoreType.DMA((2,)),
            pltpu.SemaphoreType.DMA((2,)),
            pltpu.SemaphoreType.DMA(shape),
            pltpu.SemaphoreType.DMA(shape),
            pltpu.SemaphoreType.DMA((count + 1, 2)),
            pltpu.SemaphoreType.DMA((2 * (depth - 1), 2)),
        ],
        compiler_params=pltpu.CompilerParams(
            collective_id=0, has_side_effects=True, vmem_limit_bytes=58 * 1024 * 1024
        ),
    )(tokens, masked, live, *tables, *weights, small)


def add_pair(left, right):
    return left + right


def join_moments(left, right):
    count = left[0:1] + right[0:1]
    mean = (left[0:1] * left[1:2] + right[0:1] * right[1:2]) / count
    gap = right[1:2] - left[1:2]
    spread = left[2:3] + right[2:3] + gap * gap * (left[0:1] * right[0:1] / count)
    return jnp.concatenate([count, mean, spread, left[3:]], axis=0)


def exchange_kernel(depth, groups, combine, value, result, work, inbox, line, send_sems, recv_sems):
    dp, z, core_bit, x_bit, y_bit = coordinates()
    peers = [dp + 1 - 2 * core_bit, dp + 2 - 4 * x_bit, dp + 4 - 8 * y_bit]
    group = dp // WAYS
    barrier = pltpu.get_barrier_semaphore()
    far = [lax.rem(group + step, groups) * WAYS + lax.rem(dp, WAYS) for step in range(1, groups)]
    for peer in peers + far:
        signal(barrier, (peer, z))
    for step in range(1, depth):
        signal(barrier, (dp, lax.rem(z + step, depth)))
    pl.semaphore_wait(barrier, len(peers) + len(far) + depth - 1)
    work[0] = value[...]
    for turn, peer in enumerate(peers):
        copy = pltpu.make_async_remote_copy(
            work.at[turn],
            inbox.at[turn],
            send_sems.at[turn],
            recv_sems.at[turn],
            device_id=(peer, z),
            device_id_type=MESH,
        )
        copy.start()
        copy.wait()
        work[turn + 1] = combine(work[turn], inbox[turn])

    def spread(source, slots, first, targets, own):
        copies = []
        for step, target in enumerate(targets):
            copy = pltpu.make_async_remote_copy(
                source,
                slots.at[own],
                send_sems.at[first + step],
                recv_sems.at[first + step],
                device_id=target,
                device_id_type=MESH,
            )
            copy.start()
            copies.append(copy)
        local = pltpu.make_async_copy(source, slots.at[own], send_sems.at[first + len(targets)])
        local.start()
        for copy in copies:
            copy.wait()
        local.wait()

    last = len(peers)
    if groups > 1:
        spread(work.at[last], inbox.at[pl.ds(last, groups)], last, [(peer, z) for peer in far], group)
        total = inbox[last]
        for step in range(1, groups):
            total = combine(total, inbox[last + step])
        work[last] = total
    first = last + groups
    spread(
        work.at[last],
        line,
        first,
        [(dp, lax.rem(z + step, depth)) for step in range(1, depth)],
        z,
    )
    total = line[0]
    for step in range(1, depth):
        total = combine(total, line[step])
    result[...] = total


def exchange(depth, groups, combine, value, collective):
    shape = value.shape
    sems = 3 + groups + depth
    return pl.pallas_call(
        functools.partial(exchange_kernel, depth, groups, combine),
        out_shape=jax.ShapeDtypeStruct(shape, value.dtype),
        in_specs=[pl.BlockSpec(memory_space=pltpu.VMEM)],
        out_specs=pl.BlockSpec(memory_space=pltpu.VMEM),
        scratch_shapes=[
            pltpu.VMEM((4,) + shape, value.dtype),
            pltpu.VMEM((3 + groups,) + shape, value.dtype),
            pltpu.VMEM((depth,) + shape, value.dtype),
            pltpu.SemaphoreType.DMA((sems,)),
            pltpu.SemaphoreType.DMA((sems,)),
        ],
        compiler_params=pltpu.CompilerParams(collective_id=collective, has_side_effects=True),
    )(value)


LANES = 128
HELD = 3
LINE_FIRST = (3, 8, 13, 17)
PLANE_LAGS = (2, 5, 9, 12, 15, 17)
LINE_LAGS = (5, 8, 10, 13, 16, 18)


def backward_units(inputs, made, results, scratch, small_first, pair_start):
    (
        grad_in,
        branch_in,
        queries_in,
        keys_in,
        values_in,
        attn_in_w,
        attn_out_w,
        ffn_in_w,
        ffn_out_w,
        inner_in,
        first_in,
        start_in,
        log_total,
        live,
        masked,
        cosine,
        sine,
        gains,
        small,
    ) = inputs
    joined_out, fresh_out, inner_out = made
    (input_grad,) = results
    (
        heads,
        joined,
        row_tiles,
        column_tiles,
        inner_tiles,
        grad,
        resid,
        total,
        gain_rows,
        sems,
        row_sems,
        column_sems,
        inner_sems,
        put_sems,
    ) = scratch
    frames, width = grad.shape
    ff_tiles = inner_in.shape[1] // TILE
    joined_tiles = joined_out.shape[1] // TILE
    row_plan = [(attn_out_w, index) for index in range(width // TILE)]
    row_plan += [(ffn_out_w, index) for index in range(ff_tiles)]
    column_plan = [(attn_in_w, index) for index in range(joined_tiles)]
    column_plan += [(ffn_in_w, index) for index in range(ff_tiles)]

    def row_copy(at):
        source, index = row_plan[at]
        return pltpu.make_async_copy(
            source.at[pl.ds(index * TILE, TILE)], row_tiles.at[at % 2], row_sems.at[at % 2]
        )

    def column_copy(at):
        source, index = column_plan[at]
        return pltpu.make_async_copy(
            source.at[:, column_tile(index)], column_tiles.at[at % 2], column_sems.at[at % 2]
        )

    def inner_copy(at):
        return pltpu.make_async_copy(
            inner_in.at[:, column_tile(at)], inner_tiles.at[at % 2], inner_sems.at[at % 2]
        )

    first_loads = [
        pltpu.make_async_copy(source, target, sems.at[index])
        for index, (source, target) in enumerate(
            (
                (branch_in, joined.at[:, pl.ds(0, width)]),
                (queries_in, heads.at[0]),
                (keys_in, heads.at[1]),
                (values_in, heads.at[2]),
                (grad_in, grad),
                (first_in, resid),
            )
        )
    ]

    def start_loads():
        for copy in first_loads[:1]:
            copy.start()
        for at in range(2):
            row_copy(at).start()
        for copy in first_loads[1:]:
            copy.start()
        for at in range(2):
            column_copy(at).start()
            inner_copy(at).start()

    def merged_grad():
        first_loads[0].wait()
        for at in range(width // TILE):
            row_copy(at).wait()

            def body(rows, at=at):
                heads[3, rows, column_tile(at)] = nt(
                    joined[rows, pl.ds(0, width)], row_tiles[at % 2]
                ).astype(jnp.bfloat16)

            row_blocks(frames, body)
            row_copy(at + 2).start()
        for copy in first_loads[1:4]:
            copy.wait()

    def turned(gradient):
        return gradient * cosine[...] + pltpu.roll(gradient, HEAD // 2, 1) * sine[...]

    def head_step(head):
        columns = pl.ds(pl.multiple_of(head * HEAD, HEAD), HEAD)
        query, key, value = heads[0, :, columns], heads[1, :, columns], heads[2, :, columns]
        upstream = heads[3, :, columns]
        scale = HEAD ** (-0.5)
        scores = jnp.where(live[...] > 0.0, nt(key, query) * scale, NEGATIVE)
        probs = jnp.exp(scores - log_total[head])
        value_grad = product(probs.astype(jnp.bfloat16), upstream)
        prob_grad = nt(value, upstream)
        row_term = jnp.sum(probs * prob_grad, axis=0, keepdims=True)
        score_grad = (probs * (prob_grad - row_term) * scale).astype(jnp.bfloat16)
        key_grad = turned(product(score_grad, query))
        query_grad = turned(
            lax.dot_general(
                score_grad, key, (((0,), (0,)), ((), ())), preferred_element_type=jnp.float32
            )
        )
        for part, value_of in enumerate((query_grad, key_grad, value_grad)):
            target = pl.ds(pl.multiple_of(part * width + head * HEAD, HEAD), HEAD)
            joined[:, target] = value_of.astype(jnp.bfloat16)

    def some_heads(low_head, high_head):
        def unit():
            pl.loop(low_head, high_head)(head_step)

        return unit

    joined_store = pltpu.make_async_copy(joined, joined_out, sems.at[6])
    fresh_store = pltpu.make_async_copy(heads.at[0], fresh_out, sems.at[7])
    start_load = pltpu.make_async_copy(start_in, resid, sems.at[5])
    grad_store = pltpu.make_async_copy(heads.at[1], input_grad, sems.at[8])

    def add_tile(at, source_of, first):
        column_copy(at).wait()

        def body(rows):
            product_part = nt(source_of(rows), column_tiles[at % 2])
            total[rows] = product_part if first else total[rows] + product_part

        row_blocks(frames, body)
        if at + 2 < len(column_plan):
            column_copy(at + 2).start()

    def project(low_tile, high_tile):
        def unit():
            if low_tile == 0:
                joined_store.start()
            for at in range(low_tile, high_tile):
                add_tile(at, lambda rows, at=at: joined[rows, column_tile(at)], at == 0)

        return unit

    def norm_step(row, rows, gain):
        value = resid[rows]
        centered = value - jnp.mean(value, axis=-1, keepdims=True)
        inverse = lax.rsqrt(jnp.mean(centered * centered, axis=-1, keepdims=True) + EPSILON)
        normed = centered * inverse
        upstream = total[rows]
        scaled = upstream * gain
        first_mean = jnp.mean(scaled, axis=-1, keepdims=True)
        second_mean = jnp.mean(scaled * normed, axis=-1, keepdims=True)
        gain_rows[row] = gain_rows[row] + jnp.sum(upstream * normed, axis=0, keepdims=True)
        grad[rows] = grad[rows] + inverse * (scaled - first_mean - normed * second_mean)

    def attention_done():
        joined_store.wait()
        pair_start(0)
        for copy in first_loads[4:]:
            copy.wait()
        gain_rows[...] = jnp.zeros_like(gain_rows)
        gain = gains[1:2]

        def body(rows):
            norm_step(1, rows, gain)
            heads[0, rows] = (0.5 * grad[rows]).astype(jnp.bfloat16)

        row_blocks(frames, body)
        start_load.start()
        fresh_store.start()

    def inner_put(at):
        return pltpu.make_async_copy(
            joined.at[:, column_tile(at % 2)], inner_out.at[:, column_tile(at)], put_sems.at[at % 2]
        )

    def feed_tiles(low_tile, high_tile):
        def unit():
            for at in range(low_tile, high_tile):
                if at == 0:
                    fresh_store.wait()
                    pair_start(1)
                row_at = width // TILE + at
                row_copy(row_at).wait()
                inner_copy(at).wait()
                if at >= 2:
                    inner_put(at - 2).wait()

                def body(rows, at=at, row_at=row_at):
                    active_grad = nt(heads[0, rows], row_tiles[row_at % 2])
                    inner = inner_tiles[at % 2, rows]
                    gate = jax.nn.sigmoid(inner)
                    joined[rows, column_tile(at % 2)] = (
                        active_grad * (gate * (1.0 + inner * (1.0 - gate)))
                    ).astype(jnp.bfloat16)

                row_blocks(frames, body)
                inner_put(at).start()
                if row_at + 2 < len(row_plan):
                    row_copy(row_at + 2).start()
                if at + 2 < ff_tiles:
                    inner_copy(at + 2).start()
                add_tile(
                    joined_tiles + at, lambda rows, at=at: joined[rows, column_tile(at % 2)], at == 0
                )
            if high_tile == ff_tiles:
                for at in range(ff_tiles - 2, ff_tiles):
                    inner_put(at).wait()
                pair_start(2)

        return unit

    def feed_done():
        start_load.wait()
        gain = gains[0:1]

        def body(rows):
            norm_step(0, rows, gain)
            hidden = masked[rows]
            final = grad[rows]
            gain_rows[2] = gain_rows[2] + jnp.sum(final * hidden, axis=0, keepdims=True)
            heads[1, rows] = (final * (1.0 - hidden)).astype(jnp.bfloat16)

        row_blocks(frames, body)
        grad_store.start()
        small_first[...] = small[...]
        small_first[0:1] = gain_rows[0]
        small_first[1:2] = gain_rows[1]
        small_first[5:6] = gain_rows[2]
        grad_store.wait()

    head_count = width // HEAD
    units = [merged_grad]
    for at in range(0, head_count, 2):
        units.append(some_heads(at, at + 2))
    for at in range(0, joined_tiles, 3):
        units.append(project(at, at + 3))
    units.append(attention_done)
    for at in range(0, ff_tiles, 2):
        units.append(feed_tiles(at, at + 2))
    units.append(feed_done)
    return start_loads, units


INPUTS = 19


def line_chunks(groups):
    return LINE_FIRST if groups == 1 else LINE_FIRST[:1]


def reduce_kernel(depth, groups, count, chunks, given, late, *refs):
    extra, refs = refs[:INPUTS], refs[INPUTS:]
    given_refs, refs = refs[: len(given)], refs[len(given) :]
    outs, small_out = refs[:count], refs[count]
    input_grad, made = refs[count + 1], refs[count + 2 : count + 2 + len(late)]
    at = count + 2 + len(late)
    left_peers, right_peers = refs[at : at + count], refs[at + count : at + 2 * count]
    at += 2 * count
    slots = dict(zip(given, given_refs))
    for name, ref in zip(late, made):
        slots[(name, 1)] = ref
    lefts = [slots[(index, 0)] for index in range(count)]
    rights = [slots[(index, 1)] for index in range(count)]
    unit_scratch, refs = refs[at : at + 14], refs[at + 14 :]
    at = 0
    (
        left_buf,
        right_buf,
        held,
        line_held,
        first_in,
        second_in,
        line_in,
        whole_in,
        half_in,
        quarter_in,
        far_in,
        final,
        small_work,
        small_in,
        small_line,
        pair_send,
        pair_recv,
        load_sems,
        send_sems,
        recv_sems,
        store_sems,
        small_send,
        small_recv,
    ) = refs[at:]
    dp, z, core_bit, x_bit, y_bit = coordinates()
    group = dp // WAYS
    peer_c, peer_x, peer_y = (
        dp + 1 - 2 * core_bit,
        dp + 2 - 4 * x_bit,
        dp + 4 - 8 * y_bit,
    )
    far = [lax.rem(group + step, groups) * WAYS + lax.rem(dp, WAYS) for step in range(1, groups)]
    barrier = pltpu.get_barrier_semaphore()
    for peer in [peer_c, peer_x, peer_y] + far:
        signal(barrier, (peer, z))
    for step in range(1, depth):
        signal(barrier, (dp, lax.rem(z + step, depth)))
    pl.semaphore_wait(barrier, 3 + len(far) + depth - 1)
    tokens = lefts[0].shape[0]
    block = left_buf.shape[2] // depth
    here = (dp, z)

    def remote(source, target, send_sem, recv_sem, device):
        return pltpu.make_async_remote_copy(
            source, target, send_sem, recv_sem, device_id=device, device_id_type=MESH
        )

    pair_copies = []
    for index in range(count):
        half = rights[index].shape[1] // 2
        columns = pl.ds(pl.multiple_of((1 - core_bit) * half, half), half)
        pair_copies.append(
            (
                remote(
                    lefts[index],
                    left_peers[index],
                    pair_send.at[index, 0],
                    pair_recv.at[index, 0],
                    (peer_c, z),
                ),
                remote(
                    rights[index].at[:, columns],
                    right_peers[index],
                    pair_send.at[index, 1],
                    pair_recv.at[index, 1],
                    (peer_c, z),
                ),
            )
        )

    def pair_start(index):
        for copy in pair_copies[index]:
            copy.start()

    pair_start(0)
    start_loads, units = backward_units(
        extra,
        made,
        (input_grad,),
        unit_scratch,
        small_work.at[0],
        lambda number: pair_start(late[number]),
    )
    start_loads()

    def loads(chunk):
        index, row, part, left_slot, right_slot, new_left, new_right = chunks[chunk]
        rows = lefts[index].shape[1] // depth
        half = rights[index].shape[1] // 2
        piece = half // 4
        copies = []
        if new_left:
            for side, source in enumerate((lefts[index], left_peers[index])):
                for owner in range(depth):
                    copies.append(
                        pltpu.make_async_copy(
                            source.at[:, pl.ds(owner * rows + row, block)],
                            left_buf.at[
                                left_slot, pl.ds(side * tokens, tokens), pl.ds(owner * block, block)
                            ],
                            load_sems.at[left_slot, side * depth + owner],
                        )
                    )
        if new_right:
            for quarter in range(4):
                start = quarter * piece + part * LANES
                own_start = pl.multiple_of(core_bit * half + start, LANES)
                target = pl.ds(quarter * LANES, LANES)
                copies.append(
                    pltpu.make_async_copy(
                        rights[index].at[:, pl.ds(own_start, LANES)],
                        right_buf.at[right_slot, pl.ds(0, tokens), target],
                        load_sems.at[2 + right_slot, quarter],
                    )
                )
                copies.append(
                    pltpu.make_async_copy(
                        right_peers[index].at[:, pl.ds(start, LANES)],
                        right_buf.at[right_slot, pl.ds(tokens, tokens), target],
                        load_sems.at[2 + right_slot, 4 + quarter],
                    )
                )
        return copies

    arrived = set()

    def load_start(chunk):
        index = chunks[chunk][0]
        if index not in arrived:
            arrived.add(index)
            for copy in pair_copies[index]:
                copy.wait_recv()
            if index + 1 < count and index + 1 not in late:
                pair_start(index + 1)
        for copy in loads(chunk):
            copy.start()

    def axes(chunk):
        if chunk % 2 == 0:
            return peer_x, peer_y, x_bit, y_bit
        return peer_y, peer_x, y_bit, x_bit

    def quarter_of(chunk, first_bit, second_bit):
        if chunk % 2 == 0:
            return 2 * first_bit + second_bit
        return 2 * second_bit + first_bit

    plane_at, line_at = {}, {}
    for chunk in range(len(chunks)):
        places = line_at if chunk in line_chunks(groups) else plane_at
        places[chunk] = len(places)

    def first_copy(chunk, which, device):
        _, _, first_bit, _ = axes(chunk)
        quarter = quarter_of(chunk, 1 - first_bit, which)
        if chunk in line_at:
            source = whole_in.at[line_at[chunk], 0, quarter]
            target = half_in.at[line_at[chunk], which]
        else:
            source = held.at[chunk % HELD, quarter]
            target = first_in.at[plane_at[chunk], which]
        return remote(
            source,
            target,
            send_sems.at[chunk, which],
            recv_sems.at[chunk, which],
            device,
        )

    def second_copy(chunk, device):
        _, _, _, second_bit = axes(chunk)
        if chunk in line_at:
            source = half_in.at[line_at[chunk], 1 - second_bit]
            target = quarter_in.at[line_at[chunk]]
        else:
            source = first_in.at[plane_at[chunk], 1 - second_bit]
            target = second_in.at[plane_at[chunk]]
        return remote(
            source,
            target,
            send_sems.at[chunk, 2],
            recv_sems.at[chunk, 2],
            device,
        )

    def line_copy(chunk, step, device):
        owner = lax.rem(z + step, depth)
        if chunk in line_at:
            source = line_held.at[line_at[chunk], :, owner]
            target = whole_in.at[line_at[chunk], step - 1]
        else:
            source = second_in.at[plane_at[chunk], owner]
            target = line_in.at[plane_at[chunk], step - 1]
        return remote(
            source,
            target,
            send_sems.at[chunk, 2 + step],
            recv_sems.at[chunk, 2 + step],
            device,
        )

    def held_sent(chunk):
        if chunk not in line_at:
            for which in range(2):
                first_copy(chunk, which, here).wait_send()

    def line_start(chunk):
        for step in range(1, depth):
            line_copy(chunk, step, (dp, lax.rem(z + step, depth))).start()

    def multiply(chunk):
        index, row, part, left_slot, right_slot, new_left, new_right = chunks[chunk]
        for copy in loads(chunk):
            copy.wait()
        if chunk + 1 < len(chunks):
            load_start(chunk + 1)
        if chunk >= HELD:
            held_sent(chunk - HELD)

        def body(owner):
            columns = pl.ds(pl.multiple_of(owner * block, block), block)
            product = lax.dot_general(
                left_buf[left_slot, :, columns],
                right_buf[right_slot],
                (((0,), (0,)), ((), ())),
                preferred_element_type=jnp.float32,
            ).astype(jnp.bfloat16)
            for quarter in range(4):
                piece = product[:, quarter * LANES : (quarter + 1) * LANES]
                if chunk in line_at:
                    line_held[line_at[chunk], quarter, owner] = piece
                else:
                    held[chunk % HELD, quarter, owner] = piece

        pl.loop(0, depth)(body)
        if chunk in line_at:
            line_start(chunk)
            return
        first_peer, _, _, _ = axes(chunk)
        for which in range(2):
            first_copy(chunk, which, (first_peer, z)).start()

    def line_total(chunk):
        place = line_at[chunk]
        for step in range(1, depth):
            line_copy(chunk, step, here).wait_recv()
        for quarter in range(4):
            total = line_held[place, quarter, z].astype(jnp.float32)
            for step in range(1, depth):
                total = total + whole_in[place, step - 1, quarter].astype(jnp.float32)
            whole_in[place, 0, quarter] = total.astype(jnp.bfloat16)
        first_peer, _, _, _ = axes(chunk)
        for which in range(2):
            first_copy(chunk, which, (first_peer, z)).start()

    def line_first_sum(chunk):
        place = line_at[chunk]
        _, second_peer, first_bit, second_bit = axes(chunk)
        for which in range(2):
            first_copy(chunk, which, here).wait_recv()

        def add(which):
            half_in[place, which] = (
                half_in[place, which].astype(jnp.float32)
                + whole_in[place, 0, quarter_of(chunk, first_bit, which)].astype(jnp.float32)
            ).astype(jnp.bfloat16)

        add(1 - second_bit)
        second_copy(chunk, (second_peer, z)).start()
        add(second_bit)

    def add_first(chunk):
        if chunk in line_at:
            line_total(chunk)
            return
        place = plane_at[chunk]
        _, second_peer, first_bit, second_bit = axes(chunk)
        for which in range(2):
            first_copy(chunk, which, here).wait_recv()

        def add(which):
            first_in[place, which] = (
                first_in[place, which].astype(jnp.float32)
                + held[chunk % HELD, quarter_of(chunk, first_bit, which)].astype(jnp.float32)
            ).astype(jnp.bfloat16)

        add(1 - second_bit)
        second_copy(chunk, (second_peer, z)).start()
        add(second_bit)

    def add_second(chunk):
        if chunk in line_at:
            line_first_sum(chunk)
            return
        place = plane_at[chunk]
        _, _, _, second_bit = axes(chunk)
        second_copy(chunk, here).wait_recv()
        second_in[place] = (
            second_in[place].astype(jnp.float32) + first_in[place, second_bit].astype(jnp.float32)
        ).astype(jnp.bfloat16)
        line_start(chunk)

    base = 2 + depth

    def where(chunk, core, x_at, y_at, half=None):
        index, row, part = chunks[chunk][:3]
        width = outs[index].shape[1]
        start = core * (width // 2) + (2 * x_at + y_at) * (width // 8) + part * LANES
        size = block
        if half is not None:
            size = block // 2
            row = row + half * size
        return outs[index].at[pl.ds(row, size), pl.ds(pl.multiple_of(start, LANES), LANES)]

    def from_final(chunk, message, device):
        return remote(
            final.at[chunk],
            where(chunk, core_bit, x_bit, y_bit),
            send_sems.at[chunk, base + message],
            recv_sems.at[chunk, base + message],
            device,
        )

    def passed(chunk, message, core, x_at, y_at, device, half=None):
        place = where(chunk, core, x_at, y_at, half)
        return remote(
            place,
            place,
            send_sems.at[chunk, base + message],
            recv_sems.at[chunk, base + message],
            device,
        )

    def store(chunk):
        return pltpu.make_async_copy(
            final.at[chunk], where(chunk, core_bit, x_bit, y_bit), store_sems.at[chunk]
        )

    def far_copy(chunk, step, device):
        return remote(
            far_in.at[chunk, groups],
            far_in.at[chunk, group],
            send_sems.at[chunk, base + 9 + step],
            recv_sems.at[chunk, base + 9 + step],
            device,
        )

    def piece_total(chunk):
        if chunk in line_at:
            _, _, _, second_bit = axes(chunk)
            second_copy(chunk, here).wait_recv()
            place = line_at[chunk]
            return half_in[place, second_bit].astype(jnp.float32) + quarter_in[place].astype(
                jnp.float32
            )
        for step in range(1, depth):
            line_copy(chunk, step, here).wait_recv()
        total = second_in[plane_at[chunk], z].astype(jnp.float32)
        for step in range(1, depth):
            total = total + line_in[plane_at[chunk], step - 1].astype(jnp.float32)
        return total

    def finish(chunk):
        total = piece_total(chunk)
        if groups > 1:
            own = total.astype(jnp.bfloat16)
            far_in[chunk, groups] = own
            far_in[chunk, group] = own
            for step, peer in enumerate(far):
                far_copy(chunk, step, (peer, z)).start()
            for step in range(len(far)):
                far_copy(chunk, step, here).wait()
            total = far_in[chunk, 0].astype(jnp.float32)
            for step in range(1, groups):
                total = total + far_in[chunk, step].astype(jnp.float32)
        final[chunk] = total.astype(jnp.bfloat16)
        for message, peer in enumerate((peer_x, peer_y, peer_c)):
            from_final(chunk, message, (peer, z)).start()
        store(chunk).start()

    def plane_arrived(chunk):
        passed(chunk, 0, core_bit, 1 - x_bit, y_bit, here).wait_recv()
        passed(chunk, 3, core_bit, 1 - x_bit, y_bit, (peer_y, z), 0).start()
        passed(chunk, 5, core_bit, 1 - x_bit, y_bit, (peer_c, z)).start()
        passed(chunk, 1, core_bit, x_bit, 1 - y_bit, here).wait_recv()
        passed(chunk, 4, core_bit, x_bit, 1 - y_bit, (peer_x, z), 1).start()
        passed(chunk, 6, core_bit, x_bit, 1 - y_bit, (peer_c, z)).start()

    def corner_arrived(chunk):
        for half in range(2):
            passed(chunk, 3 + half, core_bit, 1 - x_bit, 1 - y_bit, here, half).wait_recv()
            passed(chunk, 7 + half, core_bit, 1 - x_bit, 1 - y_bit, (peer_c, z), half).start()

    def core_arrived(chunk):
        other = 1 - core_bit
        passed(chunk, 2, other, x_bit, y_bit, here).wait_recv()
        passed(chunk, 5, other, 1 - x_bit, y_bit, here).wait_recv()
        passed(chunk, 6, other, x_bit, 1 - y_bit, here).wait_recv()
        for half in range(2):
            passed(chunk, 7 + half, other, 1 - x_bit, 1 - y_bit, here, half).wait_recv()

    def small_copy(turn, device):
        return remote(
            small_work.at[turn],
            small_in.at[turn],
            small_send.at[turn],
            small_recv.at[turn],
            device,
        )

    def small_far_copy(step, device):
        return remote(
            small_work.at[3],
            small_in.at[3 + group],
            small_send.at[3 + step],
            small_recv.at[3 + step],
            device,
        )

    slice_width = small_out.shape[1]

    def small_line_copy(step, device):
        columns = pl.ds(
            pl.multiple_of(lax.rem(z + step, depth) * slice_width, slice_width), slice_width
        )
        return remote(
            small_work.at[4, :, columns],
            small_line.at[step - 1],
            small_send.at[2 + groups + step],
            small_recv.at[2 + groups + step],
            device,
        )

    small_peers = (peer_c, peer_x, peer_y)

    def small_turn(turn):
        if 1 <= turn <= 3:
            small_copy(turn - 1, here).wait_recv()
            small_work[turn] = small_work[turn - 1] + small_in[turn - 1]
        if turn < 3:
            small_copy(turn, (small_peers[turn], z)).start()
        if turn == 3:
            if groups > 1:
                small_in[3 + group] = small_work[3]
                for step, peer in enumerate(far):
                    small_far_copy(step, (peer, z)).start()
                for step in range(len(far)):
                    small_far_copy(step, here).wait()
                total = small_in[3]
                for step in range(1, groups):
                    total = total + small_in[3 + step]
                small_work[4] = total
            else:
                small_work[4] = small_work[3]
            for step in range(1, depth):
                small_line_copy(step, (dp, lax.rem(z + step, depth))).start()
        if turn == 4:
            columns = pl.ds(pl.multiple_of(z * slice_width, slice_width), slice_width)
            total = small_work[4, :, columns]
            for step in range(1, depth):
                small_line_copy(step, here).wait_recv()
                total = total + small_line[step - 1]
            small_out[...] = total

    total_chunks = len(chunks)
    load_start(0)
    stages = (add_first, add_second, finish, plane_arrived, corner_arrived, core_arrived)
    agenda = {}
    for chunk in range(total_chunks):
        for lag, action in zip(LINE_LAGS if chunk in line_at else PLANE_LAGS, stages):
            agenda.setdefault(chunk + lag, []).append((chunk, action))
    for turn in range(max(agenda) + 1):
        if turn < total_chunks:
            multiply(turn)
        if turn < len(units):
            units[turn]()
        if 0 <= turn - len(units) < 5:
            small_turn(turn - len(units))
        for chunk, action in sorted(agenda.get(turn, []), key=lambda item: -item[0]):
            action(chunk)
    for index in range(count):
        for copy in pair_copies[index]:
            copy.wait_send()
    for turn in range(3):
        small_copy(turn, here).wait_send()
    for step in range(1, depth):
        small_line_copy(step, here).wait_send()
    for chunk in range(total_chunks):
        if chunk >= total_chunks - HELD:
            held_sent(chunk)
        if chunk in line_at:
            for which in range(2):
                first_copy(chunk, which, here).wait_send()
        for step in range(1, depth):
            line_copy(chunk, step, here).wait_send()
        second_copy(chunk, here).wait_send()
        for message in range(3):
            from_final(chunk, message, here).wait_send()
        for message in (5, 6):
            passed(chunk, message, core_bit, x_bit, y_bit, here).wait_send()
        for message in (3, 4, 7, 8):
            passed(chunk, message, core_bit, x_bit, y_bit, here, 0).wait_send()
        store(chunk).wait()


def reduce_chunks(depth, pairs, block):
    chunks = []
    left_slot, right_slot = 1, 1
    last_left, last_right = None, None
    for index, (left, right) in enumerate(pairs):
        rows = left.shape[1] // depth
        for row in range(0, rows, block):
            for part in range(right.shape[1] // (WAYS * LANES)):
                new_left = last_left != (index, row)
                new_right = last_right != (index, part)
                if new_left:
                    left_slot = 1 - left_slot
                if new_right:
                    right_slot = 1 - right_slot
                last_left, last_right = (index, row), (index, part)
                chunks.append((index, row, part, left_slot, right_slot, new_left, new_right))
    return chunks


def reduce_all(depth, groups, pairs, extra, small, collective):
    count = len(pairs)
    tokens = pairs[0][0].shape[0]
    width = small.shape[1]
    block = width // depth
    shapes = [
        (left, right if not isinstance(right, int) else jax.ShapeDtypeStruct((tokens, right), left.dtype))
        for left, right in pairs
    ]
    chunks = reduce_chunks(depth, shapes, block)
    total = len(chunks)
    lines = len([chunk for chunk in range(total) if chunk in line_chunks(groups)])
    low = jnp.bfloat16
    given, operands, late = [], [], []
    for index, (left, right) in enumerate(pairs):
        given.append((index, 0))
        operands.append(left)
        if isinstance(right, int):
            late.append(index)
        else:
            given.append((index, 1))
            operands.append(right)
    outs, made, left_peers, right_peers = [], [], [], []
    for index, (left, right) in enumerate(shapes):
        outs.append(jax.ShapeDtypeStruct((left.shape[1] // depth, right.shape[1]), low))
        left_peers.append(jax.ShapeDtypeStruct(left.shape, low))
        right_peers.append(jax.ShapeDtypeStruct((tokens, right.shape[1] // 2), low))
        if index in late:
            made.append(jax.ShapeDtypeStruct(right.shape, low))
    outs.append(jax.ShapeDtypeStruct((small.shape[0], block), jnp.float32))
    outs.append(jax.ShapeDtypeStruct((tokens, width), low))
    messages = 2 + depth + 9 + groups
    any_spec = pl.BlockSpec(memory_space=pl.ANY)
    vmem_spec = pl.BlockSpec(memory_space=pltpu.VMEM)
    results = pl.pallas_call(
        functools.partial(reduce_kernel, depth, groups, count, chunks, given, late),
        out_shape=outs + made + left_peers + right_peers,
        in_specs=[any_spec] * 12 + [vmem_spec] * 7 + [any_spec] * len(operands),
        out_specs=[any_spec] * count
        + [vmem_spec]
        + [any_spec] * (1 + len(made) + 2 * count),
        scratch_shapes=[
            pltpu.VMEM((4, tokens, width), low),
            pltpu.VMEM((tokens, 3 * width), low),
            pltpu.VMEM((2, TILE, width), low),
            pltpu.VMEM((2, width, TILE), low),
            pltpu.VMEM((2, tokens, TILE), jnp.float32),
            pltpu.VMEM((tokens, width), jnp.float32),
            pltpu.VMEM((tokens, width), jnp.float32),
            pltpu.VMEM((tokens, width), jnp.float32),
            pltpu.VMEM((3, 1, width), jnp.float32),
            pltpu.SemaphoreType.DMA((9,)),
            pltpu.SemaphoreType.DMA((2,)),
            pltpu.SemaphoreType.DMA((2,)),
            pltpu.SemaphoreType.DMA((2,)),
            pltpu.SemaphoreType.DMA((2,)),
            pltpu.VMEM((2, 2 * tokens, depth * block), low),
            pltpu.VMEM((2, 2 * tokens, 4 * LANES), low),
            pltpu.VMEM((HELD, 4, depth, block, LANES), low),
            pltpu.VMEM((max(lines, 1), 4, depth, block, LANES) if lines else (1, 1, 1, 16, LANES), low),
            pltpu.VMEM((total - lines, 2, depth, block, LANES), low),
            pltpu.VMEM((total - lines, depth, block, LANES), low),
            pltpu.VMEM((total - lines, depth - 1, block, LANES), low),
            pltpu.VMEM((max(lines, 1), depth - 1, 4, block, LANES), low),
            pltpu.VMEM((max(lines, 1), 2, block, LANES), low),
            pltpu.VMEM((max(lines, 1), block, LANES), low),
            pltpu.VMEM((total, groups + 1, block, LANES) if groups > 1 else (1, 1, 16, LANES), low),
            pltpu.VMEM((total, block, LANES), low),
            pltpu.VMEM((5,) + small.shape, jnp.float32),
            pltpu.VMEM((3 + groups,) + small.shape, jnp.float32),
            pltpu.VMEM((depth - 1, small.shape[0], block), jnp.float32),
            pltpu.SemaphoreType.DMA((count, 2)),
            pltpu.SemaphoreType.DMA((count, 2)),
            pltpu.SemaphoreType.DMA((4, max(2 * depth, 8))),
            pltpu.SemaphoreType.DMA((total, messages)),
            pltpu.SemaphoreType.DMA((total, messages)),
            pltpu.SemaphoreType.DMA((total,)),
            pltpu.SemaphoreType.DMA((3 + groups + depth,)),
            pltpu.SemaphoreType.DMA((3 + groups + depth,)),
        ],
        compiler_params=pltpu.CompilerParams(
            collective_id=collective, has_side_effects=True, vmem_limit_bytes=62 * 1024 * 1024
        ),
    )(*extra, small, *operands)
    return results[:count], results[count], results[count + 1]


def ffn_forward(inputs, layer_gain, weight_in, weight_out):
    out_norm, normed, inverse = layer_norm(inputs, layer_gain)
    hidden = out_norm.astype(jnp.bfloat16)
    inner = product(hidden, weight_in)
    active = jax.nn.silu(inner).astype(jnp.bfloat16)
    return (product(active, weight_out), (hidden, normed, inverse, inner, active))


def ffn_backward(upstream, stored, layer_gain, weight_in, weight_out):
    hidden, normed, inverse, inner, active = stored
    branch_grad = (0.5 * upstream).astype(jnp.bfloat16)
    active_grad = product_nt(branch_grad, weight_out)
    inner_grad = (active_grad * swish_slope(inner)).astype(jnp.bfloat16)
    norm_grad, gain_grad = norm_back(product_nt(inner_grad, weight_in), layer_gain, normed, inverse)
    return (upstream + norm_grad, [(hidden, inner_grad), (active, branch_grad)], gain_grad)


def conv_forward(inputs, layer_gain, weight_in, weight_out, small_low, live, units, share):
    row_count, model_width = inputs.shape
    frame_count = row_count // units
    out_norm, normed, inverse = layer_norm(inputs, layer_gain)
    hidden = out_norm.astype(jnp.bfloat16)
    proj = product(hidden, weight_in)
    linear_part = proj[:, :model_width]
    gate_part = jax.nn.sigmoid(proj[:, model_width:])
    glu = (linear_part * gate_part * live).reshape(units, frame_count, model_width)
    side = KER // 2
    padded = jnp.pad(glu, ((0, 0), (side, side), (0, 0)))
    kernel = small_low[1 : KER + 1].astype(jnp.float32)
    mixed = kernel[0] * padded[:, 0:frame_count]
    for offset in range(1, KER):
        mixed = mixed + kernel[offset] * padded[:, offset : offset + frame_count]
    mixed = mixed.reshape(row_count, model_width)
    local_count = jnp.sum(live)
    local_mean = jnp.sum(mixed * live, axis=0) / local_count
    local_spread = jnp.sum(jnp.square(mixed - local_mean) * live, axis=0)
    moments = jnp.stack([jnp.full((model_width,), local_count), local_mean, local_spread])
    moments = share(join_moments, jnp.pad(moments, ((0, 5), (0, 0))), 1)
    count, bmean = moments[0, 0], moments[1]
    bvar = moments[2] / count
    bn_inverse = lax.rsqrt(bvar + EPSILON)
    bn_normed = (mixed - bmean) * bn_inverse
    pre_act = small_low[KER + 1].astype(jnp.float32) * bn_normed + small_low[KER + 2].astype(
        jnp.float32
    )
    active = jax.nn.silu(pre_act).astype(jnp.bfloat16)
    stored = (
        hidden,
        normed,
        inverse,
        linear_part,
        gate_part,
        padded,
        bn_normed,
        bn_inverse,
        count,
        pre_act,
        active,
    )
    return (product(active, weight_out), stored)


def conv_backward(upstream, stored, layer_gain, weight_in, weight_out, small_low, live, units, share):
    (
        hidden,
        normed,
        inverse,
        linear_part,
        gate_part,
        padded,
        bn_normed,
        bn_inverse,
        count,
        pre_act,
        active,
    ) = stored
    row_count, model_width = upstream.shape
    frame_count = row_count // units
    kernel = small_low[1 : KER + 1].astype(jnp.float32)
    bn_scale = small_low[KER + 1].astype(jnp.float32)
    branch_grad = upstream.astype(jnp.bfloat16)
    pre_grad = product_nt(branch_grad, weight_out) * swish_slope(pre_act)
    sums = jnp.stack([jnp.sum(pre_grad, axis=0), jnp.sum(pre_grad * bn_normed, axis=0)])
    sums = share(add_pair, jnp.pad(sums, ((0, 6), (0, 0))), 2)
    shift_total, scale_total = sums[0], sums[1]
    mixed_grad = bn_inverse * (
        bn_scale * pre_grad
        - live * (bn_scale * shift_total) / count
        - live * bn_normed * (bn_scale * scale_total) / count
    )
    side = KER // 2
    grid_grad = mixed_grad.reshape(units, frame_count, model_width)
    grad_padded = jnp.pad(grid_grad, ((0, 0), (side, side), (0, 0)))
    last_tap = KER - 1
    glu_grad = kernel[0] * grad_padded[:, last_tap : last_tap + frame_count]
    for offset in range(1, KER):
        glu_grad = (
            glu_grad
            + kernel[offset] * grad_padded[:, last_tap - offset : last_tap - offset + frame_count]
        )
    kernel_grad = jnp.stack(
        [
            jnp.sum(padded[:, offset : offset + frame_count] * grid_grad, axis=(0, 1))
            for offset in range(KER)
        ]
    )
    glu_grad = glu_grad.reshape(row_count, model_width) * live
    proj_grad = jnp.concatenate(
        [glu_grad * gate_part, glu_grad * linear_part * gate_part * (1.0 - gate_part)], axis=1
    ).astype(jnp.bfloat16)
    norm_grad, gain_grad = norm_back(product_nt(proj_grad, weight_in), layer_gain, normed, inverse)
    return (
        upstream + norm_grad,
        [(hidden, proj_grad), (active, branch_grad)],
        gain_grad,
        kernel_grad,
        jnp.stack([scale_total, shift_total]),
    )


def local(
    depth_devices,
    groups,
    tokens,
    lengths,
    span_starts,
    mask_embed,
    norm_gains,
    ffn1_in,
    ffn1_out,
    attn_in,
    attn_out,
    conv_in,
    conv_out,
    depth,
    bn_affine,
    ffn2_in,
    ffn2_out,
    cotangent,
):
    units, frame_count, model_width = tokens.shape
    row_count = units * frame_count
    position = jnp.arange(frame_count, dtype=jnp.int32)
    valid = position[None, :] < lengths[:, None]
    inside = (position[None, None, :] >= span_starts[:, :, None]) & (
        position[None, None, :] < span_starts[:, :, None] + SPAN_LEN
    )
    masked = jnp.any(inside, axis=1) & valid
    live = valid.reshape(row_count, 1).astype(jnp.float32)
    masked_col = masked.reshape(row_count, 1)
    cosine, sine = rotation(frame_count)
    cosine, sine = cosine[:, 0], sine[:, 0]
    cosine_row = jnp.concatenate([cosine, cosine], axis=1)
    sine_row = jnp.concatenate([-sine, sine], axis=1)
    small = jnp.concatenate([norm_gains, mask_embed[None, :], depth, bn_affine], axis=0)
    small = jnp.pad(small, ((0, 16 - small.shape[0]), (0, 0)))
    gathered = gather_all(
        depth_devices,
        [ffn1_in, ffn1_out, attn_in, attn_out, conv_in, conv_out, ffn2_in, ffn2_out],
        (2, 2, 2, 1, 1, 1, 2, 2),
        small,
        tokens.reshape(row_count, model_width),
        masked_col.astype(jnp.float32),
        live,
        (cosine_row, sine_row),
    )
    (
        start,
        hidden_one,
        inner_one,
        active_one,
        first,
        hidden_two,
        queries,
        keys_rot,
        values_low,
        log_total,
        merged,
        second,
    ) = gathered[9:]
    small_all = gathered[8].transpose(1, 0, 2).reshape(16, model_width)
    third_small = jnp.concatenate([small_all[2:3], small_all[6:13]], axis=0)
    first_weights = (gathered[0], gathered[1])
    second_weights = (gathered[2], gathered[3])
    third_weights = (gathered[4], gathered[5], third_small)
    fourth_weights = (gathered[6], gathered[7], small_all[3:5])
    gain_three = third_weights[2][0].astype(jnp.float32)
    share = functools.partial(exchange, depth_devices, groups)
    branch, third_stored = conv_forward(
        second, gain_three, third_weights[0], third_weights[1], third_weights[2], live, units, share
    )
    third = second + branch
    gain_four = fourth_weights[2][0].astype(jnp.float32)
    gain_five = fourth_weights[2][1].astype(jnp.float32)
    branch, fourth_stored = ffn_forward(third, gain_four, fourth_weights[0], fourth_weights[1])
    fourth = third + 0.5 * branch
    out_norm, final_normed, final_inverse = layer_norm(fourth, gain_five)
    output = out_norm.astype(jnp.bfloat16).reshape(units, frame_count, model_width)
    upstream = cotangent.reshape(row_count, model_width).astype(jnp.float32)
    grad_four, gain_five_grad = norm_back(upstream, gain_five, final_normed, final_inverse)
    grad_three, fourth_pairs, gain_four_grad = ffn_backward(
        grad_four, fourth_stored, gain_four, fourth_weights[0], fourth_weights[1]
    )
    grad_two, third_pairs, gain_three_grad, kernel_grad, affine_full = conv_backward(
        grad_three,
        third_stored,
        gain_three,
        third_weights[0],
        third_weights[1],
        third_weights[2],
        live,
        units,
        share,
    )
    zero_row = jnp.zeros((1, model_width), jnp.float32)
    small_grads = jnp.concatenate(
        [
            zero_row,
            zero_row,
            gain_three_grad[None, :],
            gain_four_grad[None, :],
            gain_five_grad[None, :],
            zero_row,
            kernel_grad,
            jnp.zeros((5, model_width), jnp.float32),
        ],
        axis=0,
    )
    branch_grad = grad_two.astype(jnp.bfloat16)
    extra = [
        grad_two,
        branch_grad,
        queries,
        keys_rot,
        values_low,
        second_weights[0],
        second_weights[1],
        first_weights[0],
        first_weights[1],
        inner_one,
        first,
        start,
        log_total,
        live,
        masked_col.astype(jnp.float32),
        cosine_row,
        -sine_row,
        small_all[0:8].astype(jnp.float32),
    ]
    pairs = fourth_pairs + third_pairs
    pairs += [(merged, branch_grad), (hidden_two, attn_in.shape[1])]
    pairs += [(active_one, model_width), (hidden_one, ffn1_in.shape[1])]
    reduced, small_sum, input_grad = reduce_all(
        depth_devices, groups, pairs, extra, small_grads, 3
    )
    input_grad = input_grad.reshape(units, frame_count, model_width)
    ffn2_in_grad, ffn2_out_grad, conv_in_grad, conv_out_grad = (
        array.astype(jnp.float32) for array in reduced[:4]
    )
    attn_out_grad, attn_in_grad, ffn1_out_grad, ffn1_in_grad = (
        array.astype(jnp.float32) for array in reduced[4:]
    )
    column_width = norm_gains.shape[1]
    affine_grad = lax.dynamic_slice_in_dim(
        affine_full, lax.axis_index("fsdp") * column_width, column_width, 1
    )
    return (
        output,
        input_grad,
        small_sum[5],
        small_sum[0:5],
        ffn1_in_grad,
        ffn1_out_grad,
        attn_in_grad,
        attn_out_grad,
        conv_in_grad,
        conv_out_grad,
        small_sum[6 : 6 + KER],
        affine_grad,
        ffn2_in_grad,
        ffn2_out_grad,
    )


def solution(mesh):
    in_specs = (
        P(("dp", "fsdp"), None, None),
        P(("dp", "fsdp")),
        P(("dp", "fsdp"), None),
        P("fsdp"),
        P(None, "fsdp"),
        P("fsdp", None),
        P("fsdp", None),
        P("fsdp", None),
        P("fsdp", None),
        P("fsdp", None),
        P("fsdp", None),
        P(None, "fsdp"),
        P(None, "fsdp"),
        P("fsdp", None),
        P("fsdp", None),
        P(("dp", "fsdp"), None, None),
    )
    out_specs = (
        P(("dp", "fsdp"), None, None),
        P(("dp", "fsdp"), None, None),
        P("fsdp"),
        P(None, "fsdp"),
        P("fsdp", None),
        P("fsdp", None),
        P("fsdp", None),
        P("fsdp", None),
        P("fsdp", None),
        P("fsdp", None),
        P(None, "fsdp"),
        P(None, "fsdp"),
        P("fsdp", None),
        P("fsdp", None),
    )
    body = functools.partial(local, mesh.shape["fsdp"], mesh.shape["dp"] // WAYS)
    return jax.shard_map(body, mesh=mesh, in_specs=in_specs, out_specs=out_specs, check_vma=False)
```
